32 devices in a mesh: freq: 4 (over z), px: 4 (over y, x), py: 2 (over core).
Axes of the slice: x: 2, y: 2, z: 4, core: 2. Of those that a mesh axis runs over, the one named last changes fastest.
Arguments:
- observed: float32 [4, 32, 2, 128], P('freq', ('px', 'py')), may hold values from -6 to 6
- noise_scale: float32 [4, 32], P('freq', ('px', 'py')), may hold values from 0.5 to 2
- forward_kernel: bfloat16 [4, 32, 128, 2, 32], P('freq', 'px', 'py'), may hold values from -0.125 to 0.125
- model_field: float32 [32, 128, 128], P('px', 'py'), may hold values from -6 to 6
- classes: int32 [32, 128], P('px', 'py'), may hold values from 0 to 15
- kappa_table: float32 [16], replicated, may hold values from 0.1 to 0.6
- coupling_table: float32 [4, 16], replicated, may hold values from 0.15 to 0.35
Outputs:
- weighted_residual: float32 [4, 32, 2, 128], P('freq', ('px', 'py'))
- gradient: float32 [32, 128, 128], P('px', 'py')
The draws below stay inside these ranges and needn't reach their ends.
All inputs are finite; a program needn't handle non-finite values.
Results may differ from the reference program's by a relative error of at most 0.003.
Values may be sent and summed in bfloat16 or wider, within the bound.
No kernel may reach another device: no remote copies, remote signals or barrier semaphores. Data moves between devices by JAX's collectives and lax.ppermute only.
A program may use at most 64 MiB of HBM per device.

```python
import math
import jax
import jax.numpy as jnp
from jax import lax

R = 128
CLASSES = 16
SWEEPS = 4
NF = 4
SENS = 32
NX = 32
NY = 128


def set_ends(entries, key, smallest, largest):
    index_at = [jax.random.randint(jax.random.fold_in(key, axis), (), 0, length) for axis, length in enumerate(entries.shape)]
    main_axis = entries.shape.index(max(entries.shape))
    beside = index_at[:main_axis] + [(index_at[main_axis] + 1) % entries.shape[main_axis]] + index_at[main_axis + 1:]
    return entries.at[tuple(index_at)].set(smallest).at[tuple(beside)].set(largest)


def raised(array, own_key, source, target, blocks, factor):
    def block_of(axis_at):
        return (jnp.arange(array.shape[axis_at]) // (array.shape[axis_at] // blocks)).reshape((-1,) + (1,) * (array.ndim - 1 - axis_at))

    one_side = jax.random.permutation(own_key, blocks)[block_of(target)]
    far = (block_of(target) + blocks // 2) % blocks
    return jnp.where((block_of(source) == one_side) | (block_of(source) == far), factor * array, array)


def block_levels(stream_key, extent, cuts, low, top_value):
    level = 1.0
    for axis_at, shards_of in cuts:
        heights = jax.random.uniform(jax.random.fold_in(jax.random.fold_in(stream_key, 6), axis_at), (shards_of,), jnp.float32, low / len(cuts), top_value / len(cuts))
        level = level * jnp.repeat(jnp.exp(heights), extent[axis_at] // shards_of).reshape((-1,) + (1,) * (len(extent) - 1 - axis_at))
    return level


def bell_draw(rng, shape, deviation, reach, split=(), kind=jnp.bfloat16):
    array = deviation * jax.random.normal(rng, shape, jnp.float32)
    if split:
        array = array * block_levels(rng, shape, split, -0.22, 0.18)
    return jnp.clip(array, -reach, reach).astype(kind)


def heavy_noise(rng, dims, scale, limit, shards, heavy, kind=jnp.bfloat16):
    drawn = scale * jax.random.normal(rng, dims, jnp.float32)
    if shards:
        drawn = drawn * block_levels(rng, dims, shards, -0.22, 0.18)
    return jnp.clip(raised(drawn, jax.random.fold_in(rng, 3), *heavy), -limit, limit).astype(kind)


def setup_inputs(seed: int = 0) -> dict:
    arg_keys = jax.random.split(jax.random.key(seed), 8)
    observed = bell_draw(arg_keys[0], (NF, SENS, 2, R), 1.0, 6.0, ((0, 4), (1, 8)), jnp.float32)
    noise_scale = jnp.clip(jnp.exp(math.log(2.0) - 1.3862944 * jax.random.uniform(arg_keys[1], (NF, SENS), jnp.float32) ** block_levels(arg_keys[1], (NF, SENS), ((0, 4), (1, 8)), -0.2, 0.2)), 0.5, 2.0)
    forward_kernel = heavy_noise(arg_keys[2], (NF, NX, NY, 2, SENS), (NX * NY) ** -0.5, 0.125, ((0, 4), (1, 4), (2, 2)), (1, 4, 4, 2.0))
    model_field = bell_draw(arg_keys[3], (NX, NY, R), 1.0, 6.0, ((0, 4), (1, 2)), jnp.float32)
    classes = set_ends(jax.random.randint(arg_keys[4], (NX, NY), 0, CLASSES), jax.random.fold_in(arg_keys[4], 1), 0, CLASSES - 1).astype(jnp.int32)
    kappa_table = jnp.clip(jnp.exp(jax.random.uniform(arg_keys[5], (CLASSES,), jnp.float32, math.log(0.1), math.log(0.6))), 0.1, 0.6)
    coupling_table = jnp.clip(jax.random.uniform(arg_keys[6], (4, CLASSES), jnp.float32, 0.15, 0.35), 0.15, 0.35)
    return dict(observed=observed, noise_scale=noise_scale, forward_kernel=forward_kernel, model_field=model_field, classes=classes, kappa_table=kappa_table, coupling_table=coupling_table)


FREEDOM = 4.0
PRIOR_WEIGHT = 0.04


def student_weights(misfit, noise):
    inverse = 1.0 / (noise * noise)
    spread = (misfit[:, 0] * misfit[:, 0] + misfit[:, 1] * misfit[:, 1]) * inverse[:, None]
    factor = (FREEDOM + 2.0) / (FREEDOM + spread) * inverse[:, None]
    return misfit * factor[:, None, :]


def coefficients(classes, kappa_table, coupling_table):
    levels = jnp.arange(kappa_table.shape[0], dtype=jnp.int32)
    onehot = (classes[..., None] == levels).astype(jnp.float32)
    diagonal = kappa_table + jnp.sum(coupling_table, axis=0)
    class_table = jnp.concatenate([diagonal[None, :], coupling_table], axis=0)
    return jnp.einsum("xyk,ck->xyc", onehot, class_table, precision=lax.Precision.HIGHEST)


def operate(padded, coefficient):
    center = padded[1:-1, 1:-1]
    beside = coefficient[..., 1:2] * padded[:-2, 1:-1] + coefficient[..., 2:3] * padded[2:, 1:-1]
    beside = beside + coefficient[..., 3:4] * padded[1:-1, :-2] + coefficient[..., 4:5] * padded[1:-1, 2:]
    return coefficient[..., 0:1] * center - beside


def reference(observed, noise_scale, forward_kernel, model_field, classes, kappa_table, coupling_table):
    model_low = lax.optimization_barrier(model_field.astype(jnp.bfloat16)).astype(jnp.float32).reshape(NX * NY, R)
    data_grad = jnp.zeros((NX * NY, R), jnp.float32)
    outputs = []
    for frequency in range(NF):
        kernel_flat = forward_kernel[frequency].reshape(NX * NY, 2, SENS).astype(jnp.float32)
        predicted = jnp.einsum("pcs,pr->scr", kernel_flat, model_low, precision=lax.Precision.HIGHEST)
        weighted = student_weights(predicted - observed[frequency], noise_scale[frequency])
        outputs.append(weighted)
        weighted_low = lax.optimization_barrier(weighted.astype(jnp.bfloat16)).astype(jnp.float32)
        data_grad = data_grad + jnp.einsum("pcs,scr->pr", kernel_flat, weighted_low, precision=lax.Precision.HIGHEST)
    coefficient = coefficients(classes, kappa_table, coupling_table)
    state_field = model_field
    for sweep_index in range(SWEEPS):
        padded = jnp.pad(state_field, ((1, 1), (1, 1), (0, 0)))
        state_field = operate(padded, coefficient)
    return jnp.stack(outputs), data_grad.reshape(NX, NY, R) + PRIOR_WEIGHT * state_field
```

```python
import jax
import jax.numpy as jnp
from jax import lax
from jax.sharding import PartitionSpec as P

SWEEPS = 4
FREEDOM = 4.0
PRIOR_WEIGHT = 0.04
GATHER_LIMIT = 4 << 20


def rim(shard, axis, dim, width):
    peers, length = lax.axis_size(axis), shard.shape[dim]
    last = lax.slice_in_dim(shard, length - width, length, axis=dim)
    first = lax.slice_in_dim(shard, 0, width, axis=dim)
    even = lax.axis_index(axis) % 2 == 0

    def swap(start, own):
        pairs = [(i, i + 1) for i in range(start, peers - 1, 2)]
        if not pairs:
            return jnp.zeros_like(own)
        return lax.ppermute(own, axis, pairs + [(j, i) for i, j in pairs])

    one = swap(0, jnp.where(even, last, first))
    two = swap(1, jnp.where(even, first, last))
    before = jnp.where(even, two, one)
    after = jnp.where(even, one, two)
    return jnp.concatenate([before, shard, after], axis=dim)


def coefficients(classes, kappa_table, coupling_table):
    levels = jnp.arange(kappa_table.shape[0], dtype=jnp.int32)
    onehot = (classes[..., None] == levels).astype(jnp.float32)
    diagonal = kappa_table + jnp.sum(coupling_table, axis=0)
    class_table = jnp.concatenate([diagonal[None, :], coupling_table], axis=0)
    return jnp.einsum("xyk,ck->xyc", onehot, class_table, precision=lax.Precision.HIGHEST)


def operate(padded, coefficient):
    center = padded[1:-1, 1:-1]
    beside = coefficient[..., 1:2] * padded[:-2, 1:-1] + coefficient[..., 2:3] * padded[2:, 1:-1]
    beside = (
        beside
        + coefficient[..., 3:4] * padded[1:-1, :-2]
        + coefficient[..., 4:5] * padded[1:-1, 2:]
    )
    return coefficient[..., 0:1] * center - beside


def local(observed, noise_scale, forward_kernel, model_field, classes, kappa_table, coupling_table):
    space = ("px", "py")
    peers = lax.axis_size("px") * lax.axis_size("py")
    rows, cols, real = model_field.shape
    comps, sensors = forward_kernel.shape[3:]
    own = observed.shape[1]
    place = lax.axis_index(space)
    kernel_own = forward_kernel[0].transpose(0, 2, 3, 1)
    kernel_all = lax.all_gather(kernel_own, "freq", axis=0)
    model_low = model_field.astype(jnp.bfloat16)
    partial = jnp.einsum("xcsy,xyr->csr", kernel_own, model_low, preferred_element_type=jnp.float32)
    minus = lax.dynamic_update_slice(
        jnp.zeros_like(partial), observed[0].transpose(1, 0, 2), (0, place * own, 0)
    )
    partial = (partial - minus).reshape(comps * sensors, real)
    noise_row = lax.dynamic_update_slice(
        jnp.zeros((sensors,), jnp.float32), noise_scale[0], (place * own,)
    )
    noise_rows = jnp.broadcast_to(noise_row[:, None], (sensors, real))
    payload = jnp.concatenate([partial, noise_rows], axis=0)
    if peers * payload.size * 4 <= GATHER_LIMIT:
        total = jnp.sum(lax.all_gather(payload, space, axis=0), axis=0)
    else:
        total = lax.psum(payload, space)
    misfit = total[: comps * sensors].reshape(comps, sensors, real)
    noise = total[comps * sensors :]
    inverse = 1.0 / (noise * noise)
    spread = (misfit[0] * misfit[0] + misfit[1] * misfit[1]) * inverse
    factor = (FREEDOM + 2.0) / (FREEDOM + spread) * inverse
    weighted = misfit * factor
    weighted_low = lax.all_gather(weighted.astype(jnp.bfloat16), "freq", axis=0)
    weighted_own = lax.dynamic_slice_in_dim(weighted, place * own, own, axis=1).transpose(1, 0, 2)
    data_grad = jnp.einsum(
        "fxcsy,fcsr->xyr", kernel_all, weighted_low, preferred_element_type=jnp.float32
    )
    grid = lax.all_gather(classes, "py", axis=1, tiled=True)
    grid = lax.all_gather(grid, "px", axis=0, tiled=True)
    grid = jnp.pad(grid, SWEEPS, constant_values=-1)
    wide = lax.dynamic_slice(
        grid,
        (lax.axis_index("px") * rows, lax.axis_index("py") * cols),
        (rows + 2 * SWEEPS, cols + 2 * SWEEPS),
    )
    coefficient = coefficients(wide, kappa_table, coupling_table)
    state = rim(rim(model_field, "px", 0, SWEEPS), "py", 1, SWEEPS)
    for step in range(SWEEPS):
        lo = step + 1
        state = operate(
            state, coefficient[lo : coefficient.shape[0] - lo, lo : coefficient.shape[1] - lo]
        )
    return weighted_own[None], data_grad + PRIOR_WEIGHT * state


def solution(mesh):
    in_specs = (
        P("freq", ("px", "py"), None, None),
        P("freq", ("px", "py")),
        P("freq", "px", "py", None, None),
        P("px", "py", None),
        P("px", "py"),
        P(),
        P(),
    )
    out_specs = (P("freq", ("px", "py"), None, None), P("px", "py", None))
    return jax.shard_map(local, mesh=mesh, in_specs=in_specs, out_specs=out_specs, check_vma=False)
```

```python
import jax
import jax.numpy as jnp
from jax import lax
from jax.sharding import PartitionSpec as P

SWEEPS = 4
FREEDOM = 4.0
PRIOR_WEIGHT = 0.04
LANES = 128


def swap(own, axis, partner):
    return lax.ppermute(own, axis, [(i, partner(i)) for i in range(lax.axis_size(axis))])


def bits(axis):
    size = lax.axis_size(axis)
    assert size & (size - 1) == 0
    return [1 << k for k in range(size.bit_length() - 1)]


def summed(own, axes):
    for axis in axes:
        for bit in bits(axis):
            own = own + swap(own, axis, lambda i: i ^ bit)
    return own


def gathered(own, axis):
    blocks = own[None]
    for bit in bits(axis):
        blocks = jnp.concatenate([blocks, swap(blocks, axis, lambda i: i ^ bit)], axis=0)
    return blocks


def rims(shard, axis, width):
    peers, length = lax.axis_size(axis), shard.shape[0]
    me = lax.axis_index(axis)
    even = me % 2 == 0
    last, first = shard[length - width :], shard[:width]
    one = swap(jnp.where(even, last, first), axis, lambda i: i ^ 1)
    if peers > 2:
        two = swap(
            jnp.where(even, first, last), axis, lambda i: (((i + 1) ^ 1) - 1) % peers
        )
        before = jnp.where(even, two, one)
        after = jnp.where(even, one, two)
    else:
        before, after = one, one
    before = jnp.where(me == 0, 0.0, before)
    after = jnp.where(me == peers - 1, 0.0, after)
    return before, after


def coefficients(classes, kappa_table, coupling_table):
    levels = jnp.arange(kappa_table.shape[0], dtype=jnp.float32)
    onehot = (classes[..., None] == levels).astype(jnp.float32)
    diagonal = kappa_table + jnp.sum(coupling_table, axis=0)
    class_table = jnp.concatenate([diagonal[None, :], coupling_table], axis=0)
    return jnp.einsum("xyk,ck->xyc", onehot, class_table, precision=lax.Precision.HIGHEST)


def operate(padded, coefficient):
    center = padded[1:-1, 1:-1]
    beside = coefficient[..., 1:2] * padded[:-2, 1:-1] + coefficient[..., 2:3] * padded[2:, 1:-1]
    beside = (
        beside
        + coefficient[..., 3:4] * padded[1:-1, :-2]
        + coefficient[..., 4:5] * padded[1:-1, 2:]
    )
    return coefficient[..., 0:1] * center - beside


def local(observed, noise_scale, forward_kernel, model_field, classes, kappa_table, coupling_table):
    space = ("py", "px")
    rows, cols, real = model_field.shape
    comps, sensors = forward_kernel.shape[3:]
    own = observed.shape[1]
    place = lax.axis_index(("px", "py"))
    kernel_own = forward_kernel[0].transpose(0, 2, 3, 1)
    model_low = model_field.astype(jnp.bfloat16)
    partial = jnp.einsum("xcsy,xyr->csr", kernel_own, model_low, preferred_element_type=jnp.float32)
    minus = lax.dynamic_update_slice(
        jnp.zeros_like(partial), observed[0].transpose(1, 0, 2), (0, place * own, 0)
    )
    partial = (partial - minus).reshape(comps * sensors, real)
    noise_rows = -(-sensors // real)
    noise_row = lax.dynamic_update_slice(
        jnp.zeros((noise_rows * real,), jnp.float32), noise_scale[0], (place * own,)
    ).reshape(noise_rows, real)
    total = summed(jnp.concatenate([partial, noise_row], axis=0), space)
    misfit = total[: comps * sensors].reshape(comps, sensors, real)
    noise = total[comps * sensors :].reshape(-1)[:sensors, None]
    inverse = 1.0 / (noise * noise)
    spread = (misfit[0] * misfit[0] + misfit[1] * misfit[1]) * inverse
    factor = (FREEDOM + 2.0) / (FREEDOM + spread) * inverse
    weighted = misfit * factor
    weighted_low = gathered(weighted.astype(jnp.bfloat16), "freq")
    weighted_own = lax.dynamic_slice_in_dim(weighted, place * own, own, axis=1).transpose(1, 0, 2)
    kernel_all = gathered(kernel_own, "freq")
    data_grad = jnp.einsum(
        "fxcsy,fcsr->xyr", kernel_all, weighted_low, preferred_element_type=jnp.float32
    )
    marks = (classes + 1).astype(jnp.float32)
    field_t = model_field.transpose(1, 0, 2)
    before, after = rims(
        jnp.concatenate(
            [field_t, jnp.pad(marks.T, ((0, 0), (0, real - rows)))[:, None, :]], axis=1
        ),
        "py",
        SWEEPS,
    )
    state = jnp.concatenate([before[:, :rows], field_t, after[:, :rows]], axis=0).transpose(1, 0, 2)
    marks = jnp.concatenate([before[:, rows, :rows], marks.T, after[:, rows, :rows]], axis=0).T
    wide = cols + 2 * SWEEPS
    mark_rows = -(-wide // real)
    before, after = rims(
        jnp.concatenate(
            [
                state,
                jnp.pad(marks, ((0, 0), (0, mark_rows * real - wide))).reshape(rows, mark_rows, real),
            ],
            axis=1,
        ),
        "px",
        SWEEPS,
    )
    state = jnp.concatenate([before[:, :wide], state, after[:, :wide]], axis=0)
    marks = jnp.concatenate(
        [
            before[:, wide:].reshape(SWEEPS, -1)[:, :wide],
            marks,
            after[:, wide:].reshape(SWEEPS, -1)[:, :wide],
        ],
        axis=0,
    )
    coefficient = coefficients(marks - 1.0, kappa_table, coupling_table)
    for step in range(SWEEPS):
        lo = step + 1
        state = operate(
            state, coefficient[lo : coefficient.shape[0] - lo, lo : coefficient.shape[1] - lo]
        )
    return weighted_own[None], data_grad + PRIOR_WEIGHT * state


def solution(mesh):
    in_specs = (
        P("freq", ("px", "py"), None, None),
        P("freq", ("px", "py")),
        P("freq", "px", "py", None, None),
        P("px", "py", None),
        P("px", "py"),
        P(),
        P(),
    )
    out_specs = (P("freq", ("px", "py"), None, None), P("px", "py", None))
    return jax.shard_map(local, mesh=mesh, in_specs=in_specs, out_specs=out_specs, check_vma=False)
```

```python
import jax
import jax.numpy as jnp
from jax import lax
from jax.experimental import pallas as pl
from jax.experimental.pallas import tpu as pltpu
from jax.sharding import PartitionSpec as P

SWEEPS = 4
FREEDOM = 4.0
PRIOR_WEIGHT = 0.04
LANES = 128
TILE = 8
VMEM_BYTES = 40 << 20
ALL_VMEM_BYTES = 63 << 20


def swap(own, axis, partner):
    return lax.ppermute(own, axis, [(i, partner(i)) for i in range(lax.axis_size(axis))])


def bits(axis):
    size = lax.axis_size(axis)
    assert size & (size - 1) == 0
    return [1 << k for k in range(size.bit_length() - 1)]


def near(i):
    return i ^ 1


def far(axis):
    return lambda i: (((i + 1) ^ 1) - 1) % lax.axis_size(axis)


def both_sides(one, two, axis):
    peers, me = lax.axis_size(axis), lax.axis_index(axis)
    even = me % 2 == 0
    zero = jnp.zeros_like(one)
    before, after = jnp.where(even, two, one), jnp.where(even, one, two)
    return jnp.where(me == 0, zero, before), jnp.where(me == peers - 1, zero, after)


def call(body, *out_shapes, fetch=False):
    def run(*operands):
        count = len(operands)

        def fetched(*refs):
            outs, held, sems = (
                refs[count : count + len(out_shapes)],
                refs[count + len(out_shapes) : -1],
                refs[-1],
            )
            copies = [
                pltpu.make_async_copy(src, dst, sems.at[k])
                for k, (src, dst) in enumerate(zip(refs[:count], held))
            ]
            for copy in copies:
                copy.start()
            for copy in copies:
                copy.wait()
            body(*held, *outs)

        return pl.pallas_call(
            fetched if fetch else body,
            out_shape=[jax.ShapeDtypeStruct(shape, dtype) for shape, dtype in out_shapes],
            in_specs=[pl.BlockSpec(memory_space=pltpu.HBM if fetch else pltpu.VMEM)] * count,
            out_specs=[pl.BlockSpec(memory_space=pltpu.VMEM)] * len(out_shapes),
            scratch_shapes=[pltpu.VMEM(x.shape, x.dtype) for x in operands] * fetch
            + [pltpu.SemaphoreType.DMA((count,))] * fetch,
            compiler_params=pltpu.CompilerParams(vmem_limit_bytes=ALL_VMEM_BYTES if fetch else VMEM_BYTES),
        )(*operands)

    return run


def prepare(noise_ref, observed_ref, kernel_ref, field_ref, classes_ref, pay_ref, packed_ref, *far_ref):
    beside, points, width = packed_ref.shape
    rows, cols, real = field_ref.shape
    own, comps = observed_ref.shape[:2]
    sensors = points // comps
    place = lax.axis_index("px") * lax.axis_size("py") + lax.axis_index("py")
    even = lax.axis_index("py") % 2 == 0
    total = jnp.zeros((points, real), jnp.float32)
    for x in range(beside):
        picks = range(x, rows, beside)
        packed = jnp.concatenate([kernel_ref[k] for k in picks], axis=1)
        packed_ref[x] = packed
        field = jnp.concatenate([field_ref[k].astype(jnp.bfloat16) for k in picks], axis=0)
        total = total + jnp.dot(packed, field, preferred_element_type=jnp.float32)
    spot = lax.broadcasted_iota(jnp.int32, (points, real), 0)
    for c in range(comps):
        for k in range(own):
            row = c * sensors + place * own + k
            total = total - jnp.where(spot == row, observed_ref[k, c : c + 1, :], 0.0)
    pay_ref[:points] = total
    spot = lax.broadcasted_iota(jnp.int32, (TILE, real), 0) * real + lax.broadcasted_iota(
        jnp.int32, (TILE, real), 1
    )
    noise = jnp.zeros((TILE, real), jnp.float32)
    for k in range(own):
        noise = noise + jnp.where(spot == place * own + k, noise_ref[0:1, k : k + 1], 0.0)
    pay_ref[points : points + TILE] = noise
    marks = (classes_ref[...] + 1).astype(jnp.float32)
    edges = [
        (field_ref[:, cols - SWEEPS :, :], marks[:, cols - SWEEPS :]),
        (field_ref[:, :SWEEPS, :], marks[:, :SWEEPS]),
    ]

    def put(ref, start, chosen):
        for x in range(rows):
            ref[start + x * SWEEPS : start + (x + 1) * SWEEPS] = jnp.where(
                chosen, edges[0][0][x], edges[1][0][x]
            )
        start = start + rows * SWEEPS
        ref[start : start + rows] = jnp.zeros((rows, real), jnp.float32)
        ref[start : start + rows, :SWEEPS] = jnp.where(chosen, edges[0][1], edges[1][1])

    put(pay_ref, points + TILE, even)
    for ref in far_ref:
        put(ref, 0, jnp.logical_not(even))


def add_first(mine_ref, got_ref, out_ref):
    size = out_ref.shape[0]
    out_ref[...] = mine_ref[:size] + got_ref[:size]


def add_and_join(mine_ref, got_ref, one_ref, two_ref, out_ref, joined_ref):
    out_ref[...] = mine_ref[...] + got_ref[...]
    half = one_ref.shape[0]
    joined_ref[:half] = one_ref[...]
    joined_ref[half:] = two_ref[...]


def weigh(mine_ref, got_ref, held_ref, low_ref, weighted_ref, passed_ref):
    comps, sensors, real = weighted_ref.shape
    points = comps * sensors
    total = mine_ref[...] + got_ref[...]
    chunk = min(sensors, real)
    eye = lax.broadcasted_iota(jnp.int32, (chunk, real), 0) == lax.broadcasted_iota(
        jnp.int32, (chunk, real), 1
    )
    for k in range(sensors // chunk):
        row = total[points + k : points + k + 1]
        noise = jnp.sum(jnp.where(eye, row, 0.0), axis=1, keepdims=True)
        inverse = 1.0 / (noise * noise)
        misfit = [total[c * sensors + k * chunk : c * sensors + (k + 1) * chunk] for c in range(comps)]
        spread = sum(part * part for part in misfit) * inverse
        factor = (FREEDOM + 2.0) / (FREEDOM + spread) * inverse
        for c in range(comps):
            weighted = misfit[c] * factor
            weighted_ref[c, k * chunk : (k + 1) * chunk] = weighted
            low_ref[c * sensors + k * chunk : c * sensors + (k + 1) * chunk] = weighted.astype(
                jnp.bfloat16
            )
    passed_ref[...] = held_ref[...]


def coefficients(classes, kappa_table, coupling_table):
    levels = jnp.arange(kappa_table.shape[0], dtype=jnp.float32)
    onehot = (classes[..., None] == levels).astype(jnp.float32)
    diagonal = kappa_table + jnp.sum(coupling_table, axis=0)
    class_table = jnp.concatenate([diagonal[None, :], coupling_table], axis=0)
    return jnp.einsum("xyk,ck->xyc", onehot, class_table, precision=lax.Precision.HIGHEST)


def operate(padded, coefficient):
    center = padded[1:-1, 1:-1]
    beside = coefficient[..., 1:2] * padded[:-2, 1:-1] + coefficient[..., 2:3] * padded[2:, 1:-1]
    beside = (
        beside
        + coefficient[..., 3:4] * padded[1:-1, :-2]
        + coefficient[..., 4:5] * padded[1:-1, 2:]
    )
    return coefficient[..., 0:1] * center - beside


def local(observed, noise_scale, forward_kernel, model_field, classes, kappa_table, coupling_table):
    rows, cols, real = model_field.shape
    comps, sensors = forward_kernel.shape[3:]
    own = observed.shape[1]
    points = comps * sensors
    place = lax.axis_index(("px", "py"))
    kernel_own = forward_kernel[0].transpose(0, 2, 3, 1).reshape(rows, points, cols)
    beside = rows // max(1, min(rows, LANES // cols))
    side = rows // beside
    assert sensors <= TILE * real
    rim_rows = rows * (SWEEPS + 1)
    wide_py, wide_px = lax.axis_size("py") > 2, lax.axis_size("px") > 2
    payload, kernel_own, *far_rim = call(
        prepare,
        ((points + TILE + rim_rows, real), jnp.float32),
        ((beside, points, side * cols), jnp.bfloat16),
        *[((rim_rows, real), jnp.float32)] * wide_py,
        fetch=True,
    )(noise_scale, observed[0], kernel_own, model_field, classes)
    got = swap(payload, "py", near)
    kernel_next = swap(kernel_own, "freq", near)
    (total,) = call(add_first, ((points + TILE, real), jnp.float32))(payload, got)
    for bit in bits("py")[1:]:
        total = total + swap(total, "py", lambda i: i ^ bit)

    one = got[points + TILE :]
    two = swap(far_rim[0], "py", far("py")) if wide_py else one
    before, after = both_sides(one, two, "py")
    marks = (classes + 1).astype(jnp.float32)

    def fields(rim):
        return rim[: rows * SWEEPS].reshape(rows, SWEEPS, real)

    wide_field = jnp.concatenate([fields(before), model_field, fields(after)], axis=1)
    marks = jnp.concatenate(
        [before[rows * SWEEPS :, :SWEEPS], marks, after[rows * SWEEPS :, :SWEEPS]], axis=1
    )
    wide = cols + 2 * SWEEPS
    even = lax.axis_index("px") % 2 == 0
    mark_rows = -(-wide // real)

    def sent(chosen):
        return jnp.concatenate(
            [
                jnp.where(chosen, wide_field[rows - SWEEPS :], wide_field[:SWEEPS]),
                jnp.pad(
                    jnp.where(chosen, marks[rows - SWEEPS :], marks[:SWEEPS]),
                    ((0, 0), (0, mark_rows * real - wide)),
                ).reshape(SWEEPS, mark_rows, real),
            ],
            axis=1,
        ).astype(jnp.bfloat16)

    one = swap(sent(even), "px", near)
    held = sent(jnp.logical_not(even))

    steps = bits("px")
    for bit in steps[:-1]:
        got = swap(total, "px", lambda i: i ^ bit)
        if bit == steps[-2]:
            total, kernel_pair = call(
                add_and_join,
                ((points + TILE, real), jnp.float32),
                ((2 * beside, points, side * cols), jnp.bfloat16),
            )(total, got, kernel_own, kernel_next)
        else:
            total = total + got
    kernel_far = swap(kernel_pair, "freq", lambda i: i ^ 2)
    got = swap(total, "px", lambda i: i ^ steps[-1])
    weighted_low, weighted, held = call(
        weigh,
        ((points, real), jnp.bfloat16),
        ((comps, sensors, real), jnp.float32),
        (held.shape, held.dtype),
    )(total, got, held)
    low_next = swap(weighted_low, "freq", near)
    low_pair = jnp.concatenate([weighted_low[None], low_next[None]], axis=0)
    low_far = swap(low_pair, "freq", lambda i: i ^ 2)
    weighted_own = lax.dynamic_slice_in_dim(weighted, place * own, own, axis=1).transpose(1, 0, 2)

    two = swap(held, "px", far("px")) if wide_px else one
    before, after = both_sides(one, two, "px")
    state = jnp.concatenate(
        [
            before[:, :wide].astype(jnp.float32),
            wide_field,
            after[:, :wide].astype(jnp.float32),
        ],
        axis=0,
    )
    marks = jnp.concatenate(
        [
            before[:, wide:].reshape(SWEEPS, -1)[:, :wide].astype(jnp.float32),
            marks,
            after[:, wide:].reshape(SWEEPS, -1)[:, :wide].astype(jnp.float32),
        ],
        axis=0,
    )
    coefficient = coefficients(marks - 1.0, kappa_table, coupling_table)
    for step in range(SWEEPS):
        lo = step + 1
        state = operate(
            state, coefficient[lo : coefficient.shape[0] - lo, lo : coefficient.shape[1] - lo]
        )

    data_grad = jnp.einsum(
        "fxqy,fqr->xyr",
        jnp.concatenate([kernel_pair, kernel_far]).reshape(4, beside, points, side * cols),
        jnp.concatenate([low_pair, low_far]),
        preferred_element_type=jnp.float32,
    )
    data_grad = jnp.concatenate(
        [data_grad[:, k * cols : (k + 1) * cols] for k in range(side)], axis=0
    )
    return weighted_own[None], data_grad + PRIOR_WEIGHT * state


def solution(mesh):
    in_specs = (
        P("freq", ("px", "py"), None, None),
        P("freq", ("px", "py")),
        P("freq", "px", "py", None, None),
        P("px", "py", None),
        P("px", "py"),
        P(),
        P(),
    )
    out_specs = (P("freq", ("px", "py"), None, None), P("px", "py", None))
    return jax.shard_map(local, mesh=mesh, in_specs=in_specs, out_specs=out_specs, check_vma=False)
```

```python
import jax
import jax.numpy as jnp
from jax import lax
from jax.experimental import pallas as pl
from jax.experimental.pallas import tpu as pltpu
from jax.sharding import PartitionSpec as P

SWEEPS = 4
FREEDOM = 4.0
PRIOR_WEIGHT = 0.04
LANES = 128
TILE = 8
VMEM_BYTES = 40 << 20
ALL_VMEM_BYTES = 63 << 20


def swap(own, axis, partner):
    return lax.ppermute(own, axis, [(i, partner(i)) for i in range(lax.axis_size(axis))])


def bits(axis):
    size = lax.axis_size(axis)
    assert size & (size - 1) == 0
    return [1 << k for k in range(size.bit_length() - 1)]


def near(i):
    return i ^ 1


def far(axis):
    return lambda i: (((i + 1) ^ 1) - 1) % lax.axis_size(axis)


def both_sides(one, two, axis):
    peers, me = lax.axis_size(axis), lax.axis_index(axis)
    even = me % 2 == 0
    zero = jnp.zeros_like(one)
    before, after = jnp.where(even, two, one), jnp.where(even, one, two)
    return jnp.where(me == 0, zero, before), jnp.where(me == peers - 1, zero, after)


def call(body, *out_shapes, fetch=False):
    def run(*operands):
        count = len(operands)

        def fetched(*refs):
            outs, held, sems = (
                refs[count : count + len(out_shapes)],
                refs[count + len(out_shapes) : -1],
                refs[-1],
            )
            copies = [
                pltpu.make_async_copy(src, dst, sems.at[k])
                for k, (src, dst) in enumerate(zip(refs[:count], held))
            ]
            for copy in copies:
                copy.start()
            for copy in copies:
                copy.wait()
            body(*held, *outs)

        return pl.pallas_call(
            fetched if fetch else body,
            out_shape=[jax.ShapeDtypeStruct(shape, dtype) for shape, dtype in out_shapes],
            in_specs=[pl.BlockSpec(memory_space=pltpu.HBM if fetch else pltpu.VMEM)] * count,
            out_specs=[pl.BlockSpec(memory_space=pltpu.VMEM)] * len(out_shapes),
            scratch_shapes=[pltpu.VMEM(x.shape, x.dtype) for x in operands] * fetch
            + [pltpu.SemaphoreType.DMA((count,))] * fetch,
            compiler_params=pltpu.CompilerParams(vmem_limit_bytes=ALL_VMEM_BYTES if fetch else VMEM_BYTES),
        )(*operands)

    return run


def prepare(kernel_ref, field_ref, classes_ref, pay_ref, packed_ref, rim_ref, *far_ref):
    beside, points, width = packed_ref.shape
    rows, cols, real = field_ref.shape
    owners, block = pay_ref.shape[:2]
    comps = 2
    own = block // comps
    even = lax.axis_index("py") % 2 == 0
    total = jnp.zeros((points, real), jnp.float32)
    for x in range(beside):
        picks = range(x, rows, beside)
        packed = jnp.concatenate([kernel_ref[k] for k in picks], axis=1)
        packed_ref[x] = packed
        field = jnp.concatenate([field_ref[k].astype(jnp.bfloat16) for k in picks], axis=0)
        total = total + jnp.dot(packed, field, preferred_element_type=jnp.float32)
    for p in range(owners):
        for c in range(comps):
            start = (c * owners + p) * own
            pay_ref[p, c * own : (c + 1) * own] = total[start : start + own]
    marks = (classes_ref[...] + 1).astype(jnp.float32)
    edges = [
        (field_ref[:, cols - SWEEPS :, :], marks[:, cols - SWEEPS :]),
        (field_ref[:, :SWEEPS, :], marks[:, :SWEEPS]),
    ]

    def put(ref, start, chosen):
        for x in range(rows):
            ref[start + x * SWEEPS : start + (x + 1) * SWEEPS] = jnp.where(
                chosen, edges[0][0][x], edges[1][0][x]
            )
        start = start + rows * SWEEPS
        ref[start : start + rows] = jnp.zeros((rows, real), jnp.float32)
        ref[start : start + rows, :SWEEPS] = jnp.where(chosen, edges[0][1], edges[1][1])

    put(rim_ref, 0, even)
    for ref in far_ref:
        put(ref, 0, jnp.logical_not(even))


def weigh(got_ref, observed_ref, noise_ref, low_ref, weighted_ref):
    own, comps, real = weighted_ref.shape
    total = got_ref[0]
    for p in range(1, got_ref.shape[0]):
        total = total + got_ref[p]
    misfit = [total[c * own : (c + 1) * own] - observed_ref[:, c, :] for c in range(comps)]
    noise = noise_ref[...]
    inverse = 1.0 / (noise * noise)
    spread = sum(part * part for part in misfit) * inverse
    factor = (FREEDOM + 2.0) / (FREEDOM + spread) * inverse
    weighted = [part * factor for part in misfit]
    for c in range(comps):
        weighted_ref[:, c, :] = weighted[c]
    low_ref[...] = jnp.concatenate(weighted, axis=0).astype(jnp.bfloat16)


def coefficients(classes, kappa_table, coupling_table):
    levels = jnp.arange(kappa_table.shape[0], dtype=jnp.float32)
    onehot = (classes[..., None] == levels).astype(jnp.float32)
    diagonal = kappa_table + jnp.sum(coupling_table, axis=0)
    class_table = jnp.concatenate([diagonal[None, :], coupling_table], axis=0)
    return jnp.einsum("xyk,ck->xyc", onehot, class_table, precision=lax.Precision.HIGHEST)


def operate(padded, coefficient):
    center = padded[1:-1, 1:-1]
    beside = coefficient[..., 1:2] * padded[:-2, 1:-1] + coefficient[..., 2:3] * padded[2:, 1:-1]
    beside = (
        beside
        + coefficient[..., 3:4] * padded[1:-1, :-2]
        + coefficient[..., 4:5] * padded[1:-1, 2:]
    )
    return coefficient[..., 0:1] * center - beside


def local(observed, noise_scale, forward_kernel, model_field, classes, kappa_table, coupling_table):
    rows, cols, real = model_field.shape
    comps, sensors = forward_kernel.shape[3:]
    own = observed.shape[1]
    points = comps * sensors
    kernel_own = forward_kernel[0].transpose(0, 2, 3, 1).reshape(rows, points, cols)
    beside = rows // max(1, min(rows, LANES // cols))
    side = rows // beside
    rim_rows = rows * (SWEEPS + 1)
    space = ("px", "py")
    everyone = ("freq", "px", "py")
    owners = lax.axis_size(space)
    peers = lax.axis_size(everyone)
    wide_py, wide_px = lax.axis_size("py") > 2, lax.axis_size("px") > 2
    payload, kernel_own, *rim = call(
        prepare,
        ((owners, comps * own, real), jnp.float32),
        ((beside, points, side * cols), jnp.bfloat16),
        *[((rim_rows, real), jnp.float32)] * (1 + wide_py),
        fetch=True,
    )(kernel_own, model_field, classes)
    got = lax.all_to_all(payload, space, split_axis=0, concat_axis=0, tiled=True)
    kernel_next = swap(kernel_own, "freq", near)
    kernel_pair = jnp.concatenate([kernel_own, kernel_next])
    kernel_far = swap(kernel_pair, "freq", lambda i: i ^ 2)
    weighted_low, weighted_own = call(
        weigh,
        ((comps * own, real), jnp.bfloat16),
        ((own, comps, real), jnp.float32),
    )(got, observed[0], noise_scale.reshape(own, 1))
    low_all = lax.all_to_all(
        jnp.broadcast_to(weighted_low[None], (peers, comps * own, real)),
        everyone,
        split_axis=0,
        concat_axis=0,
        tiled=True,
    )
    low_all = low_all.reshape(-1, owners, comps, own, real).transpose(0, 2, 1, 3, 4).reshape(-1, points, real)
    me = lax.axis_index("freq")
    low_all = jnp.stack(
        [lax.dynamic_index_in_dim(low_all, me ^ k, 0, keepdims=False) for k in range(4)]
    )

    one = swap(rim[0], "py", near)
    two = swap(rim[1], "py", far("py")) if wide_py else one
    before, after = both_sides(one, two, "py")
    marks = (classes + 1).astype(jnp.float32)

    def fields(rim):
        return rim[: rows * SWEEPS].reshape(rows, SWEEPS, real)

    wide_field = jnp.concatenate([fields(before), model_field, fields(after)], axis=1)
    marks = jnp.concatenate(
        [before[rows * SWEEPS :, :SWEEPS], marks, after[rows * SWEEPS :, :SWEEPS]], axis=1
    )
    wide = cols + 2 * SWEEPS
    even = lax.axis_index("px") % 2 == 0
    mark_rows = -(-wide // real)

    def sent(chosen):
        return jnp.concatenate(
            [
                jnp.where(chosen, wide_field[rows - SWEEPS :], wide_field[:SWEEPS]),
                jnp.pad(
                    jnp.where(chosen, marks[rows - SWEEPS :], marks[:SWEEPS]),
                    ((0, 0), (0, mark_rows * real - wide)),
                ).reshape(SWEEPS, mark_rows, real),
            ],
            axis=1,
        ).astype(jnp.bfloat16)

    one = swap(sent(even), "px", near)
    held = sent(jnp.logical_not(even))
    two = swap(held, "px", far("px")) if wide_px else one
    before, after = both_sides(one, two, "px")
    state = jnp.concatenate(
        [
            before[:, :wide].astype(jnp.float32),
            wide_field,
            after[:, :wide].astype(jnp.float32),
        ],
        axis=0,
    )
    marks = jnp.concatenate(
        [
            before[:, wide:].reshape(SWEEPS, -1)[:, :wide].astype(jnp.float32),
            marks,
            after[:, wide:].reshape(SWEEPS, -1)[:, :wide].astype(jnp.float32),
        ],
        axis=0,
    )
    coefficient = coefficients(marks - 1.0, kappa_table, coupling_table)
    for step in range(SWEEPS):
        lo = step + 1
        state = operate(
            state, coefficient[lo : coefficient.shape[0] - lo, lo : coefficient.shape[1] - lo]
        )

    data_grad = jnp.einsum(
        "fxqy,fqr->xyr",
        jnp.concatenate([kernel_pair, kernel_far]).reshape(4, beside, points, side * cols),
        low_all,
        preferred_element_type=jnp.float32,
    )
    data_grad = jnp.concatenate(
        [data_grad[:, k * cols : (k + 1) * cols] for k in range(side)], axis=0
    )
    return weighted_own[None], data_grad + PRIOR_WEIGHT * state


def solution(mesh):
    in_specs = (
        P("freq", ("px", "py"), None, None),
        P("freq", ("px", "py")),
        P("freq", "px", "py", None, None),
        P("px", "py", None),
        P("px", "py"),
        P(),
        P(),
    )
    out_specs = (P("freq", ("px", "py"), None, None), P("px", "py", None))
    return jax.shard_map(local, mesh=mesh, in_specs=in_specs, out_specs=out_specs, check_vma=False)
```

```python
import jax
import jax.numpy as jnp
from jax import lax
from jax.experimental import pallas as pl
from jax.experimental.pallas import tpu as pltpu
from jax.sharding import PartitionSpec as P

SWEEPS = 4
FREEDOM = 4.0
PRIOR_WEIGHT = 0.04
LANES = 128
TILE = 8
VMEM_BYTES = 40 << 20


def swap(own, axis, partner):
    return lax.ppermute(own, axis, [(i, partner(i)) for i in range(lax.axis_size(axis))])


def bits(axis):
    size = lax.axis_size(axis)
    assert size & (size - 1) == 0
    return [1 << k for k in range(size.bit_length() - 1)]


def near(i):
    return i ^ 1


def far(axis):
    return lambda i: (((i + 1) ^ 1) - 1) % lax.axis_size(axis)


def both_sides(one, two, axis):
    peers, me = lax.axis_size(axis), lax.axis_index(axis)
    even = me % 2 == 0
    zero = jnp.zeros_like(one)
    before, after = jnp.where(even, two, one), jnp.where(even, one, two)
    return jnp.where(me == 0, zero, before), jnp.where(me == peers - 1, zero, after)


def call(body, *out_shapes, fetch=False):
    def run(*operands):
        count = len(operands)
        if fetch:
            operands = [pltpu.with_memory_space_constraint(x, pltpu.HBM) for x in operands]

        def fetched(*refs):
            outs, held, sems = (
                refs[count : count + len(out_shapes)],
                refs[count + len(out_shapes) : -1],
                refs[-1],
            )
            copies = [
                pltpu.make_async_copy(src, dst, sems.at[k])
                for k, (src, dst) in enumerate(zip(refs[:count], held))
            ]
            for copy in copies:
                copy.start()
            for copy in copies:
                copy.wait()
            body(*held, *outs)

        return pl.pallas_call(
            fetched if fetch else body,
            out_shape=[jax.ShapeDtypeStruct(shape, dtype) for shape, dtype in out_shapes],
            in_specs=[pl.BlockSpec(memory_space=pltpu.HBM if fetch else pltpu.VMEM)] * count,
            out_specs=[pl.BlockSpec(memory_space=pltpu.VMEM)] * len(out_shapes),
            scratch_shapes=[pltpu.VMEM(x.shape, x.dtype) for x in operands] * fetch
            + [pltpu.SemaphoreType.DMA((count,))] * fetch,
            compiler_params=pltpu.CompilerParams(vmem_limit_bytes=VMEM_BYTES),
        )(*operands)

    return run


def prepare(
    noise_ref,
    observed_ref,
    kernel_ref,
    field_ref,
    classes_ref,
    kappa_ref,
    coupling_ref,
    pay_ref,
    packed_ref,
    held_ref,
    marks_ref,
    table_ref,
    *far_ref,
):
    beside, points, width = packed_ref.shape
    rows, cols, real = field_ref.shape
    own, comps = observed_ref.shape[:2]
    sensors = points // comps
    place = lax.axis_index("px") * lax.axis_size("py") + lax.axis_index("py")
    even = lax.axis_index("py") % 2 == 0
    total = jnp.zeros((points, real), jnp.float32)
    for x in range(beside):
        picks = range(x, rows, beside)
        packed = jnp.concatenate([kernel_ref[k] for k in picks], axis=1)
        packed_ref[x] = packed
        field = jnp.concatenate([field_ref[k].astype(jnp.bfloat16) for k in picks], axis=0)
        total = total + jnp.dot(packed, field, preferred_element_type=jnp.float32)
    spot = lax.broadcasted_iota(jnp.int32, (points, real), 0)
    for c in range(comps):
        for k in range(own):
            row = c * sensors + place * own + k
            total = total - jnp.where(spot == row, observed_ref[k, c : c + 1, :], 0.0)
    pay_ref[:points] = total
    spot = lax.broadcasted_iota(jnp.int32, (TILE, real), 0) * real + lax.broadcasted_iota(
        jnp.int32, (TILE, real), 1
    )
    noise = jnp.zeros((TILE, real), jnp.float32)
    for k in range(own):
        noise = noise + jnp.where(spot == place * own + k, noise_ref[0:1, k : k + 1], 0.0)
    pay_ref[points : points + TILE] = noise
    held_ref[...] = field_ref[...]
    coupling = coupling_ref[...]
    table_ref[0:1] = kappa_ref[...] + jnp.sum(coupling, axis=0, keepdims=True)
    table_ref[1:] = coupling
    marks = (classes_ref[...] + 1).astype(jnp.float32)
    marks_ref[...] = marks
    edges = [
        (field_ref[:, cols - SWEEPS :, :], marks[:, cols - SWEEPS :]),
        (field_ref[:, :SWEEPS, :], marks[:, :SWEEPS]),
    ]

    def put(ref, start, chosen):
        for x in range(rows):
            ref[start + x * SWEEPS : start + (x + 1) * SWEEPS] = jnp.where(
                chosen, edges[0][0][x], edges[1][0][x]
            )
        start = start + rows * SWEEPS
        ref[start : start + rows] = jnp.zeros((rows, real), jnp.float32)
        ref[start : start + rows, :SWEEPS] = jnp.where(chosen, edges[0][1], edges[1][1])

    put(pay_ref, points + TILE, even)
    for ref in far_ref:
        put(ref, 0, jnp.logical_not(even))


def add_first(mine_ref, got_ref, out_ref):
    size = out_ref.shape[0]
    out_ref[...] = mine_ref[:size] + got_ref[:size]


def add_and_join(mine_ref, got_ref, one_ref, two_ref, out_ref, joined_ref):
    out_ref[...] = mine_ref[...] + got_ref[...]
    half = one_ref.shape[0]
    joined_ref[:half] = one_ref[...]
    joined_ref[half:] = two_ref[...]


def weigh(mine_ref, got_ref, low_ref, weighted_ref):
    comps, sensors, real = weighted_ref.shape
    points = comps * sensors
    total = mine_ref[...] + got_ref[...]
    chunk = min(sensors, real)
    eye = lax.broadcasted_iota(jnp.int32, (chunk, real), 0) == lax.broadcasted_iota(
        jnp.int32, (chunk, real), 1
    )
    for k in range(sensors // chunk):
        row = total[points + k : points + k + 1]
        noise = jnp.sum(jnp.where(eye, row, 0.0), axis=1, keepdims=True)
        inverse = 1.0 / (noise * noise)
        misfit = [total[c * sensors + k * chunk : c * sensors + (k + 1) * chunk] for c in range(comps)]
        spread = sum(part * part for part in misfit) * inverse
        factor = (FREEDOM + 2.0) / (FREEDOM + spread) * inverse
        for c in range(comps):
            weighted = misfit[c] * factor
            weighted_ref[c, k * chunk : (k + 1) * chunk] = weighted
            low_ref[c * sensors + k * chunk : c * sensors + (k + 1) * chunk] = weighted.astype(
                jnp.bfloat16
            )


def coefficients(classes, table):
    levels = jnp.arange(table.shape[1], dtype=jnp.float32)
    onehot = (classes[..., None] == levels).astype(jnp.float32)
    return jnp.einsum("xyk,ck->xyc", onehot, table, precision=lax.Precision.HIGHEST)


def operate(padded, coefficient):
    center = padded[1:-1, 1:-1]
    beside = coefficient[..., 1:2] * padded[:-2, 1:-1] + coefficient[..., 2:3] * padded[2:, 1:-1]
    beside = (
        beside
        + coefficient[..., 3:4] * padded[1:-1, :-2]
        + coefficient[..., 4:5] * padded[1:-1, 2:]
    )
    return coefficient[..., 0:1] * center - beside


def local(observed, noise_scale, forward_kernel, model_field, classes, kappa_table, coupling_table):
    rows, cols, real = model_field.shape
    comps, sensors = forward_kernel.shape[3:]
    own = observed.shape[1]
    points = comps * sensors
    place = lax.axis_index(("px", "py"))
    kernel_own = forward_kernel[0].transpose(0, 2, 3, 1).reshape(rows, points, cols)
    beside = rows // max(1, min(rows, LANES // cols))
    side = rows // beside
    assert sensors <= TILE * real
    rim_rows = rows * (SWEEPS + 1)
    wide_py, wide_px = lax.axis_size("py") > 2, lax.axis_size("px") > 2
    payload, kernel_own, model_field, marks, table, *far_rim = call(
        prepare,
        ((points + TILE + rim_rows, real), jnp.float32),
        ((beside, points, side * cols), jnp.bfloat16),
        (model_field.shape, jnp.float32),
        (classes.shape, jnp.float32),
        ((1 + coupling_table.shape[0], coupling_table.shape[1]), jnp.float32),
        *[((rim_rows, real), jnp.float32)] * wide_py,
        fetch=True,
    )(
        noise_scale,
        observed[0],
        kernel_own,
        model_field,
        classes,
        kappa_table[None],
        coupling_table,
    )
    got = swap(payload, "py", near)
    kernel_next = swap(kernel_own, "freq", near)
    (total,) = call(add_first, ((points + TILE, real), jnp.float32))(payload, got)
    for bit in bits("py")[1:]:
        total = total + swap(total, "py", lambda i: i ^ bit)

    one = got[points + TILE :]
    two = swap(far_rim[0], "py", far("py")) if wide_py else one
    before, after = both_sides(one, two, "py")

    def fields(rim):
        return rim[: rows * SWEEPS].reshape(rows, SWEEPS, real)

    wide_field = jnp.concatenate([fields(before), model_field, fields(after)], axis=1)
    marks = jnp.concatenate(
        [before[rows * SWEEPS :, :SWEEPS], marks, after[rows * SWEEPS :, :SWEEPS]], axis=1
    )
    wide = cols + 2 * SWEEPS
    even = lax.axis_index("px") % 2 == 0
    mark_rows = -(-wide // real)

    def sent(chosen):
        return jnp.concatenate(
            [
                jnp.where(chosen, wide_field[rows - SWEEPS :], wide_field[:SWEEPS]),
                jnp.pad(
                    jnp.where(chosen, marks[rows - SWEEPS :], marks[:SWEEPS]),
                    ((0, 0), (0, mark_rows * real - wide)),
                ).reshape(SWEEPS, mark_rows, real),
            ],
            axis=1,
        ).astype(jnp.bfloat16)

    one = swap(sent(even), "px", near)
    two = swap(sent(jnp.logical_not(even)), "px", far("px")) if wide_px else one

    steps = bits("px")
    for bit in steps[:-1]:
        got = swap(total, "px", lambda i: i ^ bit)
        if bit == steps[-2]:
            total, kernel_pair = call(
                add_and_join,
                ((points + TILE, real), jnp.float32),
                ((2 * beside, points, side * cols), jnp.bfloat16),
            )(total, got, kernel_own, kernel_next)
        else:
            total = total + got
    kernel_far = swap(kernel_pair, "freq", lambda i: i ^ 2)
    got = swap(total, "px", lambda i: i ^ steps[-1])
    weighted_low, weighted = call(
        weigh,
        ((points, real), jnp.bfloat16),
        ((comps, sensors, real), jnp.float32),
    )(total, got)
    freqs = lax.axis_size("freq")
    low_all = lax.all_to_all(
        jnp.broadcast_to(weighted_low[None], (freqs, points, real)),
        "freq",
        split_axis=0,
        concat_axis=0,
        tiled=True,
    )
    me = lax.axis_index("freq")
    low_all = jnp.stack(
        [lax.dynamic_index_in_dim(low_all, me ^ k, 0, keepdims=False) for k in range(freqs)]
    )
    weighted_own = lax.dynamic_slice_in_dim(weighted, place * own, own, axis=1).transpose(1, 0, 2)

    before, after = both_sides(one, two, "px")
    state = jnp.concatenate(
        [
            before[:, :wide].astype(jnp.float32),
            wide_field,
            after[:, :wide].astype(jnp.float32),
        ],
        axis=0,
    )
    marks = jnp.concatenate(
        [
            before[:, wide:].reshape(SWEEPS, -1)[:, :wide].astype(jnp.float32),
            marks,
            after[:, wide:].reshape(SWEEPS, -1)[:, :wide].astype(jnp.float32),
        ],
        axis=0,
    )
    coefficient = coefficients(marks - 1.0, table)
    for step in range(SWEEPS):
        lo = step + 1
        state = operate(
            state, coefficient[lo : coefficient.shape[0] - lo, lo : coefficient.shape[1] - lo]
        )

    data_grad = jnp.einsum(
        "fxqy,fqr->xyr",
        jnp.concatenate([kernel_pair, kernel_far]).reshape(4, beside, points, side * cols),
        low_all,
        preferred_element_type=jnp.float32,
    )
    data_grad = jnp.concatenate(
        [data_grad[:, k * cols : (k + 1) * cols] for k in range(side)], axis=0
    )
    return weighted_own[None], data_grad + PRIOR_WEIGHT * state


def solution(mesh):
    in_specs = (
        P("freq", ("px", "py"), None, None),
        P("freq", ("px", "py")),
        P("freq", "px", "py", None, None),
        P("px", "py", None),
        P("px", "py"),
        P(),
        P(),
    )
    out_specs = (P("freq", ("px", "py"), None, None), P("px", "py", None))
    return jax.shard_map(local, mesh=mesh, in_specs=in_specs, out_specs=out_specs, check_vma=False)
```

```python
import jax
import jax.numpy as jnp
from jax import lax
from jax.experimental import pallas as pl
from jax.experimental.pallas import tpu as pltpu
from jax.sharding import PartitionSpec as P

SWEEPS = 4
FREEDOM = 4.0
PRIOR_WEIGHT = 0.04
LANES = 128
TILE = 8
VMEM_BYTES = 40 << 20
PRIOR_FLOPS = 1 << 30


def swap(own, axis, partner):
    return lax.ppermute(own, axis, [(i, partner(i)) for i in range(lax.axis_size(axis))])


def bits(axis):
    size = lax.axis_size(axis)
    assert size & (size - 1) == 0
    return [1 << k for k in range(size.bit_length() - 1)]


def near(i):
    return i ^ 1


def far(axis):
    return lambda i: (((i + 1) ^ 1) - 1) % lax.axis_size(axis)


def call(body, *out_shapes, fetch=False, scratch=(), stored=(), flops=0):
    def run(*operands):
        count = len(operands)
        if fetch:
            operands = [pltpu.with_memory_space_constraint(x, pltpu.HBM) for x in operands]

        def fetched(*refs):
            outs, held, sems = (
                refs[count : count + len(out_shapes)],
                refs[count + len(out_shapes) : -1],
                refs[-1],
            )
            copies = [
                pltpu.make_async_copy(src, dst, sems.at[k])
                for k, (src, dst) in enumerate(zip(refs[:count], held))
            ]
            for copy in copies:
                copy.start()
            for copy in copies:
                copy.wait()
            body(*held, *outs)

        return pl.pallas_call(
            fetched if fetch else body,
            out_shape=[jax.ShapeDtypeStruct(shape, dtype) for shape, dtype in out_shapes],
            in_specs=[pl.BlockSpec(memory_space=pltpu.HBM if fetch else pltpu.VMEM)] * count,
            out_specs=[
                pl.BlockSpec(memory_space=pltpu.HBM if k in stored else pltpu.VMEM)
                for k in range(len(out_shapes))
            ],
            scratch_shapes=list(scratch)
            + [pltpu.VMEM(x.shape, x.dtype) for x in operands] * fetch
            + [pltpu.SemaphoreType.DMA((count,))] * fetch,
            compiler_params=pltpu.CompilerParams(vmem_limit_bytes=VMEM_BYTES),
            cost_estimate=pl.CostEstimate(flops=flops, bytes_accessed=0, transcendentals=0),
        )(*operands)

    return run


def prepare(
    noise_ref,
    observed_ref,
    kernel_ref,
    field_ref,
    classes_ref,
    kappa_ref,
    coupling_ref,
    pay_ref,
    packed_ref,
    held_ref,
    marks_ref,
    table_ref,
    *far_ref,
):
    beside, points, width = packed_ref.shape
    rows, cols, real = field_ref.shape
    own, comps = observed_ref.shape[:2]
    sensors = points // comps
    place = lax.axis_index("px") * lax.axis_size("py") + lax.axis_index("py")
    even = lax.axis_index("py") % 2 == 0
    total = jnp.zeros((points, real), jnp.float32)
    for x in range(beside):
        picks = range(x, rows, beside)
        packed = jnp.concatenate([kernel_ref[k] for k in picks], axis=1)
        packed_ref[x] = packed
        field = jnp.concatenate([field_ref[k].astype(jnp.bfloat16) for k in picks], axis=0)
        total = total + jnp.dot(packed, field, preferred_element_type=jnp.float32)
    spot = lax.broadcasted_iota(jnp.int32, (points, real), 0)
    for c in range(comps):
        for k in range(own):
            row = c * sensors + place * own + k
            total = total - jnp.where(spot == row, observed_ref[k, c : c + 1, :], 0.0)
    pay_ref[:points] = total
    spot = lax.broadcasted_iota(jnp.int32, (TILE, real), 0) * real + lax.broadcasted_iota(
        jnp.int32, (TILE, real), 1
    )
    noise = jnp.zeros((TILE, real), jnp.float32)
    for k in range(own):
        noise = noise + jnp.where(spot == place * own + k, noise_ref[0:1, k : k + 1], 0.0)
    pay_ref[points : points + TILE] = noise
    held_ref[...] = field_ref[...]
    coupling = coupling_ref[...]
    table_ref[0:1] = kappa_ref[...] + jnp.sum(coupling, axis=0, keepdims=True)
    table_ref[1:] = coupling
    marks = (classes_ref[...] + 1).astype(jnp.float32)
    marks_ref[...] = jnp.zeros_like(marks_ref)
    marks_ref[:, :cols] = marks
    edges = [
        (field_ref[:, cols - SWEEPS :, :], marks[:, cols - SWEEPS :]),
        (field_ref[:, :SWEEPS, :], marks[:, :SWEEPS]),
    ]

    def put(ref, start, chosen):
        for x in range(rows):
            ref[start + x * SWEEPS : start + (x + 1) * SWEEPS] = jnp.where(
                chosen, edges[0][0][x], edges[1][0][x]
            )
        start = start + rows * SWEEPS
        ref[start : start + rows] = jnp.zeros((rows, real), jnp.float32)
        ref[start : start + rows, :SWEEPS] = jnp.where(chosen, edges[0][1], edges[1][1])

    put(pay_ref, points + TILE, even)
    for ref in far_ref:
        put(ref, 0, jnp.logical_not(even))


def sides_of(one, two, axis):
    me = lax.axis_index(axis)
    even = me % 2 == 0
    before = jnp.where(me == 0, 0.0, jnp.where(even, two, one))
    after = jnp.where(me == lax.axis_size(axis) - 1, 0.0, jnp.where(even, one, two))
    return before, after


def add_and_edge(
    mine_ref, got_ref, field_ref, marks_ref, *refs
):
    *far_ref, out_ref, side_ref, wide_ref, near_ref, far_rows_ref = refs
    size = out_ref.shape[0]
    rows, cols, real = field_ref.shape
    out_ref[...] = mine_ref[:size] + got_ref[:size]
    one = got_ref[size:]
    before, after = sides_of(one, far_ref[0][...] if far_ref else one, "py")
    fields = rows * SWEEPS
    wide_ref[...] = (
        marks_ref[...]
        + pltpu.roll(after[fields:], cols, 1)
        + pltpu.roll(before[fields:], cols + SWEEPS, 1)
    )
    for x in range(rows):
        pick = slice(x * SWEEPS, (x + 1) * SWEEPS)
        side_ref[x] = jnp.concatenate([after[pick], before[pick]], axis=0)
    even = lax.axis_index("px") % 2 == 0
    top = lax.broadcasted_iota(jnp.int32, (TILE, real), 0) == 0
    step = near_ref.shape[0] // SWEEPS
    for ref, chosen in ((near_ref, even), (far_rows_ref, jnp.logical_not(even))):
        for k in range(SWEEPS):
            last = rows - SWEEPS + k
            marks = jnp.where(chosen, wide_ref[last : last + 1], wide_ref[k : k + 1])
            ref[k * step : (k + 1) * step] = jnp.concatenate(
                [
                    jnp.where(chosen, field_ref[last], field_ref[k]),
                    jnp.where(chosen, side_ref[last], side_ref[k]),
                    jnp.where(top, marks, 0.0),
                ],
                axis=0,
            ).astype(jnp.bfloat16)


def add_and_join(mine_ref, got_ref, one_ref, two_ref, out_ref, joined_ref):
    out_ref[...] = mine_ref[...] + got_ref[...]
    half = one_ref.shape[0]
    joined_ref[:half] = one_ref[...]
    joined_ref[half:] = two_ref[...]


def weigh(mine_ref, got_ref, low_ref, weighted_ref):
    comps, sensors, real = weighted_ref.shape
    points = comps * sensors
    total = mine_ref[...] + got_ref[...]
    chunk = min(sensors, real)
    eye = lax.broadcasted_iota(jnp.int32, (chunk, real), 0) == lax.broadcasted_iota(
        jnp.int32, (chunk, real), 1
    )
    for k in range(sensors // chunk):
        row = total[points + k : points + k + 1]
        noise = jnp.sum(jnp.where(eye, row, 0.0), axis=1, keepdims=True)
        inverse = 1.0 / (noise * noise)
        misfit = [total[c * sensors + k * chunk : c * sensors + (k + 1) * chunk] for c in range(comps)]
        spread = sum(part * part for part in misfit) * inverse
        factor = (FREEDOM + 2.0) / (FREEDOM + spread) * inverse
        for c in range(comps):
            weighted = misfit[c] * factor
            weighted_ref[c, k * chunk : (k + 1) * chunk] = weighted
            for f in range(low_ref.shape[0]):
                low_ref[f, c * sensors + k * chunk : c * sensors + (k + 1) * chunk] = (
                    weighted.astype(jnp.bfloat16)
                )


def prior(
    field_ref,
    side_ref,
    wide_ref,
    near_ref,
    far_ref,
    table_ref,
    weighted_ref,
    prior_ref,
    own_out,
    state_ref,
    coef_ref,
    own_ref,
    sem,
):
    own, comps, real = own_ref.shape
    sensors = weighted_ref.shape[1]
    place = lax.axis_index("px") * lax.axis_size("py") + lax.axis_index("py")
    spot = lax.broadcasted_iota(jnp.int32, (sensors, real), 0)
    for c in range(comps):
        for k in range(own):
            own_ref[k, c : c + 1] = jnp.sum(
                jnp.where(spot == place * own + k, weighted_ref[c], 0.0), axis=0, keepdims=True
            )
    out = pltpu.make_async_copy(own_ref, own_out, sem)
    out.start()
    rows, cols, _ = field_ref.shape
    wide = cols + 2 * SWEEPS
    step = near_ref.shape[0] // SWEEPS
    before, after = sides_of(
        near_ref[...].astype(jnp.float32), far_ref[...].astype(jnp.float32), "px"
    )
    marks = []
    for k in range(SWEEPS):
        state_ref[0, k] = before[k * step : k * step + wide]
        state_ref[0, SWEEPS + rows + k] = after[k * step : k * step + wide]
    for x in range(rows):
        state_ref[0, SWEEPS + x] = jnp.concatenate([field_ref[x], side_ref[x]], axis=0)
    marks = (
        [before[k * step + wide : k * step + wide + 1] for k in range(SWEEPS)]
        + [wide_ref[x : x + 1] for x in range(rows)]
        + [after[k * step + wide : k * step + wide + 1] for k in range(SWEEPS)]
    )
    count, levels = table_ref.shape
    spread = (
        lax.broadcasted_iota(jnp.int32, (count, count * real), 1) // real
        == lax.broadcasted_iota(jnp.int32, (count, count * real), 0)
    ).astype(jnp.float32)
    turn = (((0,), (0,)), ((), ()))
    table = lax.dot_general(
        table_ref[...],
        spread,
        turn,
        precision=lax.Precision.HIGHEST,
        preferred_element_type=jnp.float32,
    )
    high = table.astype(jnp.bfloat16)
    rest = table - high.astype(jnp.float32)
    middle = rest.astype(jnp.bfloat16)
    low = (rest - middle.astype(jnp.float32)).astype(jnp.bfloat16)
    table = jnp.concatenate([high, middle, low], axis=0)
    level = lax.broadcasted_iota(jnp.int32, (levels, real), 0).astype(jnp.float32) + 1.0
    for x in range(1, 2 * SWEEPS + rows - 1):
        onehot = (level == marks[x]).astype(jnp.float32).astype(jnp.bfloat16)
        onehot = jnp.concatenate([onehot] * 3, axis=0)[:, :wide]
        coef = lax.dot_general(onehot, table, turn, preferred_element_type=jnp.float32)
        for c in range(count):
            coef_ref[x, c] = coef[:, c * real : (c + 1) * real]
    for sweep in range(SWEEPS):
        now, later = sweep % 2, (sweep + 1) % 2
        for x in range(sweep + 1, 2 * SWEEPS + rows - sweep - 1):
            center = state_ref[now, x]
            beside = (
                coef_ref[x, 1] * state_ref[now, x - 1]
                + coef_ref[x, 2] * state_ref[now, x + 1]
                + coef_ref[x, 3] * pltpu.roll(center, 1, 0)
                + coef_ref[x, 4] * pltpu.roll(center, wide - 1, 0)
            )
            new = coef_ref[x, 0] * center - beside
            if sweep < SWEEPS - 1:
                state_ref[later, x] = new
            else:
                prior_ref[x - SWEEPS] = PRIOR_WEIGHT * new[:cols]
    out.wait()


def finish(pair_ref, far_ref, low_ref, prior_ref, out, held_ref, sems):
    rows, cols, real = held_ref.shape
    beside = pair_ref.shape[0] // 2
    side = rows // beside
    me = lax.axis_index("freq")
    low = jnp.concatenate([low_ref[me ^ k] for k in range(low_ref.shape[0])], axis=0)
    copies = []
    for x in range(beside):
        kernel = jnp.concatenate(
            [pair_ref[x], pair_ref[beside + x], far_ref[x], far_ref[beside + x]], axis=0
        )
        grad = lax.dot_general(
            kernel, low, (((0,), (0,)), ((), ())), preferred_element_type=jnp.float32
        )
        for k in range(side):
            row = k * beside + x
            held_ref[row] = grad[k * cols : (k + 1) * cols] + prior_ref[row]
            copies.append(pltpu.make_async_copy(held_ref.at[row], out.at[row], sems.at[row]))
            copies[-1].start()
    for copy in copies:
        copy.wait()


def local(observed, noise_scale, forward_kernel, model_field, classes, kappa_table, coupling_table):
    rows, cols, real = model_field.shape
    comps, sensors = forward_kernel.shape[3:]
    own = observed.shape[1]
    points = comps * sensors
    kernel_own = forward_kernel[0].transpose(0, 2, 3, 1).reshape(rows, points, cols)
    beside = rows // max(1, min(rows, LANES // cols))
    side = rows // beside
    assert sensors <= TILE * real and cols + 2 * SWEEPS <= LANES
    assert rows >= SWEEPS and (cols + 2 * SWEEPS + TILE) % 16 == 0
    rim_rows = rows * (SWEEPS + 1)
    wide_py, wide_px = lax.axis_size("py") > 2, lax.axis_size("px") > 2
    payload, kernel_own, model_field, marks, table, *far_rim = call(
        prepare,
        ((points + TILE + rim_rows, real), jnp.float32),
        ((beside, points, side * cols), jnp.bfloat16),
        (model_field.shape, jnp.float32),
        ((rows, LANES), jnp.float32),
        ((1 + coupling_table.shape[0], coupling_table.shape[1]), jnp.float32),
        *[((rim_rows, real), jnp.float32)] * wide_py,
        fetch=True,
    )(
        noise_scale,
        observed[0],
        kernel_own,
        model_field,
        classes,
        kappa_table[None],
        coupling_table,
    )
    got = swap(payload, "py", near)
    kernel_next = swap(kernel_own, "freq", near)
    two = [swap(rim, "py", far("py")) for rim in far_rim]
    step = cols + 2 * SWEEPS + TILE
    total, side_rim, wide_marks, near_rows, far_rows = call(
        add_and_edge,
        ((points + TILE, real), jnp.float32),
        ((rows, 2 * SWEEPS, real), jnp.float32),
        ((rows, LANES), jnp.float32),
        ((SWEEPS * step, real), jnp.bfloat16),
        ((SWEEPS * step, real), jnp.bfloat16),
    )(payload, got, model_field, marks, *two)
    for bit in bits("py")[1:]:
        total = total + swap(total, "py", lambda i: i ^ bit)
    near_rows = swap(near_rows, "px", near)
    far_rows = swap(far_rows, "px", far("px")) if wide_px else near_rows

    steps = bits("px")
    for bit in steps[:-1]:
        got = swap(total, "px", lambda i: i ^ bit)
        if bit == steps[-2]:
            total, kernel_pair = call(
                add_and_join,
                ((points + TILE, real), jnp.float32),
                ((2 * beside, points, side * cols), jnp.bfloat16),
            )(total, got, kernel_own, kernel_next)
        else:
            total = total + got
    kernel_far = swap(kernel_pair, "freq", lambda i: i ^ 2)
    got = swap(total, "px", lambda i: i ^ steps[-1])
    freqs = lax.axis_size("freq")
    assert freqs == 4
    weighted_low, weighted = call(
        weigh,
        ((freqs, points, real), jnp.bfloat16),
        ((comps, sensors, real), jnp.float32),
    )(total, got)
    low_all = lax.all_to_all(weighted_low, "freq", split_axis=0, concat_axis=0, tiled=True)
    wide = cols + 2 * SWEEPS
    prior_term, weighted_own = call(
        prior,
        (model_field.shape, jnp.float32),
        ((own, comps, real), jnp.float32),
        stored=(1,),
        scratch=(
            pltpu.VMEM((2, rows + 2 * SWEEPS, wide, real), jnp.float32),
            pltpu.VMEM((rows + 2 * SWEEPS, table.shape[0], wide, real), jnp.float32),
            pltpu.VMEM((own, comps, real), jnp.float32),
            pltpu.SemaphoreType.DMA(()),
        ),
        flops=PRIOR_FLOPS,
    )(model_field, side_rim, wide_marks, near_rows, far_rows, table, weighted)
    (gradient,) = call(
        finish,
        (model_field.shape, jnp.float32),
        stored=(0,),
        scratch=(
            pltpu.VMEM(model_field.shape, jnp.float32),
            pltpu.SemaphoreType.DMA((rows,)),
        ),
    )(kernel_pair, kernel_far, low_all, prior_term)
    return weighted_own[None], gradient


def solution(mesh):
    in_specs = (
        P("freq", ("px", "py"), None, None),
        P("freq", ("px", "py")),
        P("freq", "px", "py", None, None),
        P("px", "py", None),
        P("px", "py"),
        P(),
        P(),
    )
    out_specs = (P("freq", ("px", "py"), None, None), P("px", "py", None))
    return jax.shard_map(local, mesh=mesh, in_specs=in_specs, out_specs=out_specs, check_vma=False)
```

```python
import jax
import jax.numpy as jnp
from jax import lax
from jax.experimental import pallas as pl
from jax.experimental.pallas import tpu as pltpu
from jax.sharding import PartitionSpec as P

SWEEPS = 4
FREEDOM = 4.0
PRIOR_WEIGHT = 0.04
LANES = 128
TILE = 8
VMEM_BYTES = 40 << 20
PRIOR_FLOPS = 1 << 30
EDGE_FLOPS = 1 << 30


def swap(own, axis, partner):
    return lax.ppermute(own, axis, [(i, partner(i)) for i in range(lax.axis_size(axis))])


def bits(axis):
    size = lax.axis_size(axis)
    assert size & (size - 1) == 0
    return [1 << k for k in range(size.bit_length() - 1)]


def near(i):
    return i ^ 1


def far(axis):
    return lambda i: (((i + 1) ^ 1) - 1) % lax.axis_size(axis)


def call(body, *out_shapes, fetch=False, scratch=(), stored=(), flops=0):
    def run(*operands):
        count = len(operands)
        if fetch:
            operands = [pltpu.with_memory_space_constraint(x, pltpu.HBM) for x in operands]

        def fetched(*refs):
            outs, held, sems = (
                refs[count : count + len(out_shapes)],
                refs[count + len(out_shapes) : -1],
                refs[-1],
            )
            copies = [
                pltpu.make_async_copy(src, dst, sems.at[k])
                for k, (src, dst) in enumerate(zip(refs[:count], held))
            ]
            for copy in copies:
                copy.start()
            for copy in copies:
                copy.wait()
            body(*held, *outs)

        return pl.pallas_call(
            fetched if fetch else body,
            out_shape=[jax.ShapeDtypeStruct(shape, dtype) for shape, dtype in out_shapes],
            in_specs=[pl.BlockSpec(memory_space=pltpu.HBM if fetch else pltpu.VMEM)] * count,
            out_specs=[
                pl.BlockSpec(memory_space=pltpu.HBM if k in stored else pltpu.VMEM)
                for k in range(len(out_shapes))
            ],
            scratch_shapes=list(scratch)
            + [pltpu.VMEM(x.shape, x.dtype) for x in operands] * fetch
            + [pltpu.SemaphoreType.DMA((count,))] * fetch,
            compiler_params=pltpu.CompilerParams(vmem_limit_bytes=VMEM_BYTES),
            cost_estimate=pl.CostEstimate(flops=flops, bytes_accessed=0, transcendentals=0),
        )(*operands)

    return run


def prepare(
    noise_ref,
    observed_ref,
    kernel_ref,
    field_ref,
    classes_ref,
    kappa_ref,
    coupling_ref,
    pay_ref,
    packed_ref,
    held_ref,
    marks_ref,
    table_ref,
    *far_ref,
):
    beside, points, width = packed_ref.shape
    rows, cols, real = field_ref.shape
    own, comps = observed_ref.shape[:2]
    sensors = points // comps
    place = lax.axis_index("px") * lax.axis_size("py") + lax.axis_index("py")
    even = lax.axis_index("py") % 2 == 0
    total = jnp.zeros((points, real), jnp.float32)
    for x in range(beside):
        picks = range(x, rows, beside)
        packed = jnp.concatenate([kernel_ref[k] for k in picks], axis=1)
        packed_ref[x] = packed
        field = jnp.concatenate([field_ref[k].astype(jnp.bfloat16) for k in picks], axis=0)
        total = total + jnp.dot(packed, field, preferred_element_type=jnp.float32)
    spot = lax.broadcasted_iota(jnp.int32, (points, real), 0)
    for c in range(comps):
        for k in range(own):
            row = c * sensors + place * own + k
            total = total - jnp.where(spot == row, observed_ref[k, c : c + 1, :], 0.0)
    pay_ref[:points] = total
    spot = lax.broadcasted_iota(jnp.int32, (TILE, real), 0) * real + lax.broadcasted_iota(
        jnp.int32, (TILE, real), 1
    )
    noise = jnp.zeros((TILE, real), jnp.float32)
    for k in range(own):
        noise = noise + jnp.where(spot == place * own + k, noise_ref[0:1, k : k + 1], 0.0)
    pay_ref[points : points + TILE] = noise
    held_ref[...] = field_ref[...]
    coupling = coupling_ref[...]
    table_ref[0:1] = kappa_ref[...] + jnp.sum(coupling, axis=0, keepdims=True)
    table_ref[1:] = coupling
    marks = (classes_ref[...] + 1).astype(jnp.float32)
    marks_ref[...] = jnp.zeros_like(marks_ref)
    marks_ref[:, :cols] = marks
    edges = [
        (field_ref[:, cols - SWEEPS :, :], marks[:, cols - SWEEPS :]),
        (field_ref[:, :SWEEPS, :], marks[:, :SWEEPS]),
    ]

    def put(ref, start, chosen):
        for x in range(rows):
            ref[start + x * SWEEPS : start + (x + 1) * SWEEPS] = jnp.where(
                chosen, edges[0][0][x], edges[1][0][x]
            )
        start = start + rows * SWEEPS
        ref[start : start + rows] = jnp.zeros((rows, real), jnp.float32)
        ref[start : start + rows, :SWEEPS] = jnp.where(chosen, edges[0][1], edges[1][1])

    put(pay_ref, points + TILE, even)
    for ref in far_ref:
        put(ref, 0, jnp.logical_not(even))


def sides_of(one, two, axis):
    me = lax.axis_index(axis)
    even = me % 2 == 0
    before = jnp.where(me == 0, 0.0, jnp.where(even, two, one))
    after = jnp.where(me == lax.axis_size(axis) - 1, 0.0, jnp.where(even, one, two))
    return before, after


def add(mine_ref, got_ref, out_ref):
    size = out_ref.shape[0]
    out_ref[...] = mine_ref[:size] + got_ref[:size]


def add_and_join(mine_ref, got_ref, one_ref, two_ref, out_ref, joined_ref):
    out_ref[...] = mine_ref[...] + got_ref[...]
    half = one_ref.shape[0]
    joined_ref[:half] = one_ref[...]
    joined_ref[half:] = two_ref[...]


def edge(after_ref, got_ref, field_ref, marks_ref, *refs):
    *far_ref, side_ref, wide_ref, near_ref = refs
    rows, cols, real = field_ref.shape
    one = got_ref[got_ref.shape[0] - rows * (SWEEPS + 1) :]
    before, after = sides_of(one, far_ref[0][...] if far_ref else one, "py")
    fields = rows * SWEEPS
    wide_ref[...] = (
        marks_ref[...]
        + pltpu.roll(after[fields:], cols, 1)
        + pltpu.roll(before[fields:], cols + SWEEPS, 1)
    )
    for x in range(rows):
        pick = slice(x * SWEEPS, (x + 1) * SWEEPS)
        side_ref[x] = jnp.concatenate([after[pick], before[pick]], axis=0)
    lay_rows(near_ref, lax.axis_index("px") % 2 == 0, field_ref, side_ref, wide_ref)


def lay_rows(ref, chosen, field_ref, side_ref, wide_ref):
    rows, _, real = field_ref.shape
    top = lax.broadcasted_iota(jnp.int32, (TILE, real), 0) == 0
    step = ref.shape[0] // SWEEPS
    for k in range(SWEEPS):
        last = rows - SWEEPS + k
        marks = jnp.where(chosen, wide_ref[last : last + 1], wide_ref[k : k + 1])
        ref[k * step : (k + 1) * step] = jnp.concatenate(
            [
                jnp.where(chosen, field_ref[last], field_ref[k]),
                jnp.where(chosen, side_ref[last], side_ref[k]),
                jnp.where(top, marks, 0.0),
            ],
            axis=0,
        ).astype(jnp.bfloat16)


def far_edge(after_ref, field_ref, side_ref, wide_ref, out_ref):
    lay_rows(out_ref, lax.axis_index("px") % 2 != 0, field_ref, side_ref, wide_ref)


def weigh(mine_ref, got_ref, low_ref, weighted_ref):
    comps, sensors, real = weighted_ref.shape
    points = comps * sensors
    total = mine_ref[...] + got_ref[...]
    chunk = min(sensors, real)
    eye = lax.broadcasted_iota(jnp.int32, (chunk, real), 0) == lax.broadcasted_iota(
        jnp.int32, (chunk, real), 1
    )
    for k in range(sensors // chunk):
        row = total[points + k : points + k + 1]
        noise = jnp.sum(jnp.where(eye, row, 0.0), axis=1, keepdims=True)
        inverse = 1.0 / (noise * noise)
        misfit = [total[c * sensors + k * chunk : c * sensors + (k + 1) * chunk] for c in range(comps)]
        spread = sum(part * part for part in misfit) * inverse
        factor = (FREEDOM + 2.0) / (FREEDOM + spread) * inverse
        for c in range(comps):
            weighted = misfit[c] * factor
            weighted_ref[c, k * chunk : (k + 1) * chunk] = weighted
            low_ref[c * sensors + k * chunk : c * sensors + (k + 1) * chunk] = weighted.astype(
                jnp.bfloat16
            )


def prior(
    field_ref,
    side_ref,
    wide_ref,
    near_ref,
    far_ref,
    table_ref,
    weighted_ref,
    prior_ref,
    own_out,
    state_ref,
    coef_ref,
    own_ref,
    sem,
):
    own, comps, real = own_ref.shape
    sensors = weighted_ref.shape[1]
    place = lax.axis_index("px") * lax.axis_size("py") + lax.axis_index("py")
    spot = lax.broadcasted_iota(jnp.int32, (sensors, real), 0)
    for c in range(comps):
        for k in range(own):
            own_ref[k, c : c + 1] = jnp.sum(
                jnp.where(spot == place * own + k, weighted_ref[c], 0.0), axis=0, keepdims=True
            )
    out = pltpu.make_async_copy(own_ref, own_out, sem)
    out.start()
    rows, cols, _ = field_ref.shape
    wide = cols + 2 * SWEEPS
    step = near_ref.shape[0] // SWEEPS
    before, after = sides_of(
        near_ref[...].astype(jnp.float32), far_ref[...].astype(jnp.float32), "px"
    )
    marks = []
    for k in range(SWEEPS):
        state_ref[0, k] = before[k * step : k * step + wide]
        state_ref[0, SWEEPS + rows + k] = after[k * step : k * step + wide]
    for x in range(rows):
        state_ref[0, SWEEPS + x] = jnp.concatenate([field_ref[x], side_ref[x]], axis=0)
    marks = (
        [before[k * step + wide : k * step + wide + 1] for k in range(SWEEPS)]
        + [wide_ref[x : x + 1] for x in range(rows)]
        + [after[k * step + wide : k * step + wide + 1] for k in range(SWEEPS)]
    )
    count, levels = table_ref.shape
    spread = (
        lax.broadcasted_iota(jnp.int32, (count, count * real), 1) // real
        == lax.broadcasted_iota(jnp.int32, (count, count * real), 0)
    ).astype(jnp.float32)
    turn = (((0,), (0,)), ((), ()))
    table = lax.dot_general(
        table_ref[...],
        spread,
        turn,
        precision=lax.Precision.HIGHEST,
        preferred_element_type=jnp.float32,
    )
    high = table.astype(jnp.bfloat16)
    rest = table - high.astype(jnp.float32)
    middle = rest.astype(jnp.bfloat16)
    low = (rest - middle.astype(jnp.float32)).astype(jnp.bfloat16)
    table = jnp.concatenate([high, middle, low], axis=0)
    level = lax.broadcasted_iota(jnp.int32, (levels, real), 0).astype(jnp.float32) + 1.0
    for x in range(1, 2 * SWEEPS + rows - 1):
        onehot = (level == marks[x]).astype(jnp.float32).astype(jnp.bfloat16)
        onehot = jnp.concatenate([onehot] * 3, axis=0)[:, :wide]
        coef = lax.dot_general(onehot, table, turn, preferred_element_type=jnp.float32)
        for c in range(count):
            coef_ref[x, c] = coef[:, c * real : (c + 1) * real]
    for sweep in range(SWEEPS):
        now, later = sweep % 2, (sweep + 1) % 2
        for x in range(sweep + 1, 2 * SWEEPS + rows - sweep - 1):
            center = state_ref[now, x]
            beside = (
                coef_ref[x, 1] * state_ref[now, x - 1]
                + coef_ref[x, 2] * state_ref[now, x + 1]
                + coef_ref[x, 3] * pltpu.roll(center, 1, 0)
                + coef_ref[x, 4] * pltpu.roll(center, wide - 1, 0)
            )
            new = coef_ref[x, 0] * center - beside
            if sweep < SWEEPS - 1:
                state_ref[later, x] = new
            else:
                prior_ref[x - SWEEPS] = PRIOR_WEIGHT * new[:cols]
    out.wait()


def finish(pair_ref, far_ref, low0_ref, low1_ref, low2_ref, low3_ref, prior_ref, out, held_ref, sems):
    rows, cols, real = held_ref.shape
    beside = pair_ref.shape[0] // 2
    side = rows // beside
    low = jnp.concatenate([low0_ref[...], low1_ref[...], low2_ref[...], low3_ref[...]], axis=0)
    copies = []
    for x in range(beside):
        kernel = jnp.concatenate(
            [pair_ref[x], pair_ref[beside + x], far_ref[x], far_ref[beside + x]], axis=0
        )
        grad = lax.dot_general(
            kernel, low, (((0,), (0,)), ((), ())), preferred_element_type=jnp.float32
        )
        for k in range(side):
            row = k * beside + x
            held_ref[row] = grad[k * cols : (k + 1) * cols] + prior_ref[row]
            copies.append(pltpu.make_async_copy(held_ref.at[row], out.at[row], sems.at[row]))
            copies[-1].start()
    for copy in copies:
        copy.wait()


def local(observed, noise_scale, forward_kernel, model_field, classes, kappa_table, coupling_table):
    rows, cols, real = model_field.shape
    comps, sensors = forward_kernel.shape[3:]
    own = observed.shape[1]
    points = comps * sensors
    kernel_own = forward_kernel[0].transpose(0, 2, 3, 1).reshape(rows, points, cols)
    beside = rows // max(1, min(rows, LANES // cols))
    side = rows // beside
    assert sensors <= TILE * real and cols + 2 * SWEEPS <= LANES
    assert rows >= SWEEPS and (cols + 2 * SWEEPS + TILE) % 16 == 0
    rim_rows = rows * (SWEEPS + 1)
    wide_py, wide_px = lax.axis_size("py") > 2, lax.axis_size("px") > 2
    payload, kernel_own, model_field, marks, table, *far_rim = call(
        prepare,
        ((points + TILE + rim_rows, real), jnp.float32),
        ((beside, points, side * cols), jnp.bfloat16),
        (model_field.shape, jnp.float32),
        ((rows, LANES), jnp.float32),
        ((1 + coupling_table.shape[0], coupling_table.shape[1]), jnp.float32),
        *[((rim_rows, real), jnp.float32)] * wide_py,
        fetch=True,
    )(
        noise_scale,
        observed[0],
        kernel_own,
        model_field,
        classes,
        kappa_table[None],
        coupling_table,
    )
    got = swap(payload, "py", near)
    kernel_next = swap(kernel_own, "freq", near)
    two = [swap(rim, "py", far("py")) for rim in far_rim]
    summed = ((points + TILE, real), jnp.float32)
    (total,) = call(add, summed)(payload, got)
    for bit in bits("py")[1:]:
        (total,) = call(add, summed)(total, swap(total, "py", lambda i: i ^ bit))
    step = cols + 2 * SWEEPS + TILE
    side_rim, wide_marks, near_rows = call(
        edge,
        ((rows, 2 * SWEEPS, real), jnp.float32),
        ((rows, LANES), jnp.float32),
        ((SWEEPS * step, real), jnp.bfloat16),
        flops=EDGE_FLOPS,
    )(total, got, model_field, marks, *two)
    near_rows = swap(near_rows, "px", near)
    *steps, last = bits("px")
    for bit in steps[:-1]:
        (total,) = call(add, summed)(total, swap(total, "px", lambda i: i ^ bit))
    total, kernel_pair = call(
        add_and_join, summed, ((2 * beside, points, side * cols), jnp.bfloat16)
    )(total, swap(total, "px", lambda i: i ^ steps[-1]), kernel_own, kernel_next)
    kernel_far = swap(kernel_pair, "freq", lambda i: i ^ 2)
    (far_rows,) = call(far_edge, ((SWEEPS * step, real), jnp.bfloat16), flops=EDGE_FLOPS)(
        total, model_field, side_rim, wide_marks
    )
    far_rows = swap(far_rows, "px", far("px")) if wide_px else near_rows
    assert lax.axis_size("freq") == 4
    weighted_low, weighted = call(
        weigh,
        ((points, real), jnp.bfloat16),
        ((comps, sensors, real), jnp.float32),
    )(total, swap(total, "px", lambda i: i ^ last))
    lows = [swap(weighted_low, "freq", lambda i: i ^ k) for k in (3, 2, 1)][::-1]
    wide = cols + 2 * SWEEPS
    prior_term, weighted_own = call(
        prior,
        (model_field.shape, jnp.float32),
        ((own, comps, real), jnp.float32),
        stored=(1,),
        scratch=(
            pltpu.VMEM((2, rows + 2 * SWEEPS, wide, real), jnp.float32),
            pltpu.VMEM((rows + 2 * SWEEPS, table.shape[0], wide, real), jnp.float32),
            pltpu.VMEM((own, comps, real), jnp.float32),
            pltpu.SemaphoreType.DMA(()),
        ),
        flops=PRIOR_FLOPS,
    )(model_field, side_rim, wide_marks, near_rows, far_rows, table, weighted)
    (gradient,) = call(
        finish,
        (model_field.shape, jnp.float32),
        stored=(0,),
        scratch=(
            pltpu.VMEM(model_field.shape, jnp.float32),
            pltpu.SemaphoreType.DMA((rows,)),
        ),
    )(kernel_pair, kernel_far, weighted_low, *lows, prior_term)
    return weighted_own[None], gradient


def solution(mesh):
    in_specs = (
        P("freq", ("px", "py"), None, None),
        P("freq", ("px", "py")),
        P("freq", "px", "py", None, None),
        P("px", "py", None),
        P("px", "py"),
        P(),
        P(),
    )
    out_specs = (P("freq", ("px", "py"), None, None), P("px", "py", None))
    return jax.shard_map(local, mesh=mesh, in_specs=in_specs, out_specs=out_specs, check_vma=False)
```

```python
import jax
import jax.numpy as jnp
from jax import lax
from jax.experimental import pallas as pl
from jax.experimental.pallas import tpu as pltpu
from jax.sharding import PartitionSpec as P

SWEEPS = 4
FREEDOM = 4.0
PRIOR_WEIGHT = 0.04
LANES = 128
TILE = 8
VMEM_BYTES = 40 << 20
PRIOR_FLOPS = 1 << 30
EDGE_FLOPS = 1 << 30
ORDER_FLOPS = 1 << 32


def swap(own, axis, partner):
    return lax.ppermute(own, axis, [(i, partner(i)) for i in range(lax.axis_size(axis))])


def bits(axis):
    size = lax.axis_size(axis)
    assert size & (size - 1) == 0
    return [1 << k for k in range(size.bit_length() - 1)]


def near(i):
    return i ^ 1


def far(axis):
    return lambda i: (((i + 1) ^ 1) - 1) % lax.axis_size(axis)


def call(body, *out_shapes, fetch=False, scratch=(), stored=(), flops=0):
    def run(*operands):
        count = len(operands)
        if fetch:
            operands = [pltpu.with_memory_space_constraint(x, pltpu.HBM) for x in operands]

        def fetched(*refs):
            outs, held, sems = (
                refs[count : count + len(out_shapes)],
                refs[count + len(out_shapes) : -1],
                refs[-1],
            )
            copies = [
                pltpu.make_async_copy(src, dst, sems.at[k])
                for k, (src, dst) in enumerate(zip(refs[:count], held))
            ]
            for copy in copies:
                copy.start()
            for copy in copies:
                copy.wait()
            body(*held, *outs)

        return pl.pallas_call(
            fetched if fetch else body,
            out_shape=[jax.ShapeDtypeStruct(shape, dtype) for shape, dtype in out_shapes],
            in_specs=[pl.BlockSpec(memory_space=pltpu.HBM if fetch else pltpu.VMEM)] * count,
            out_specs=[
                pl.BlockSpec(memory_space=pltpu.HBM if k in stored else pltpu.VMEM)
                for k in range(len(out_shapes))
            ],
            scratch_shapes=list(scratch)
            + [pltpu.VMEM(x.shape, x.dtype) for x in operands] * fetch
            + [pltpu.SemaphoreType.DMA((count,))] * fetch,
            compiler_params=pltpu.CompilerParams(vmem_limit_bytes=VMEM_BYTES),
            cost_estimate=pl.CostEstimate(flops=flops, bytes_accessed=0, transcendentals=0),
        )(*operands)

    return run


def prepare(
    noise_ref,
    observed_ref,
    kernel_ref,
    field_ref,
    classes_ref,
    kappa_ref,
    coupling_ref,
    pay_ref,
    packed_ref,
    held_ref,
    marks_ref,
    table_ref,
    *far_ref,
):
    beside, points, width = packed_ref.shape
    rows, cols, real = field_ref.shape
    own, comps = observed_ref.shape[:2]
    sensors = points // comps
    place = lax.axis_index("px") * lax.axis_size("py") + lax.axis_index("py")
    even = lax.axis_index("py") % 2 == 0
    total = jnp.zeros((points, real), jnp.float32)
    for x in range(beside):
        picks = range(x, rows, beside)
        packed = jnp.concatenate([kernel_ref[k] for k in picks], axis=1)
        packed_ref[x] = packed
        field = jnp.concatenate([field_ref[k].astype(jnp.bfloat16) for k in picks], axis=0)
        total = total + jnp.dot(packed, field, preferred_element_type=jnp.float32)
    spot = lax.broadcasted_iota(jnp.int32, (points, real), 0)
    for c in range(comps):
        for k in range(own):
            row = c * sensors + place * own + k
            total = total - jnp.where(spot == row, observed_ref[k, c : c + 1, :], 0.0)
    pay_ref[:points] = total
    spot = lax.broadcasted_iota(jnp.int32, (TILE, real), 0) * real + lax.broadcasted_iota(
        jnp.int32, (TILE, real), 1
    )
    noise = jnp.zeros((TILE, real), jnp.float32)
    for k in range(own):
        noise = noise + jnp.where(spot == place * own + k, noise_ref[0:1, k : k + 1], 0.0)
    pay_ref[points : points + TILE] = noise
    held_ref[...] = field_ref[...]
    coupling = coupling_ref[...]
    table_ref[0:1] = kappa_ref[...] + jnp.sum(coupling, axis=0, keepdims=True)
    table_ref[1:] = coupling
    marks = (classes_ref[...] + 1).astype(jnp.float32)
    marks_ref[...] = jnp.zeros_like(marks_ref)
    marks_ref[:, :cols] = marks
    edges = [
        (field_ref[:, cols - SWEEPS :, :], marks[:, cols - SWEEPS :]),
        (field_ref[:, :SWEEPS, :], marks[:, :SWEEPS]),
    ]

    def put(ref, start, chosen):
        for x in range(rows):
            ref[start + x * SWEEPS : start + (x + 1) * SWEEPS] = jnp.where(
                chosen, edges[0][0][x], edges[1][0][x]
            )
        start = start + rows * SWEEPS
        ref[start : start + rows] = jnp.zeros((rows, real), jnp.float32)
        ref[start : start + rows, :SWEEPS] = jnp.where(chosen, edges[0][1], edges[1][1])

    put(pay_ref, points + TILE, even)
    for ref in far_ref:
        put(ref, 0, jnp.logical_not(even))


def sides_of(one, two, axis):
    me = lax.axis_index(axis)
    even = me % 2 == 0
    before = jnp.where(me == 0, 0.0, jnp.where(even, two, one))
    after = jnp.where(me == lax.axis_size(axis) - 1, 0.0, jnp.where(even, one, two))
    return before, after


def add(mine_ref, got_ref, out_ref):
    size = out_ref.shape[0]
    out_ref[...] = mine_ref[:size] + got_ref[:size]


def add_and_join(mine_ref, got_ref, one_ref, two_ref, out_ref, joined_ref):
    out_ref[...] = mine_ref[...] + got_ref[...]
    half = one_ref.shape[0]
    joined_ref[:half] = one_ref[...]
    joined_ref[half:] = two_ref[...]


def edge(after_ref, got_ref, field_ref, marks_ref, *refs):
    *far_ref, side_ref, wide_ref, rows_ref = refs
    rows, cols, real = field_ref.shape
    one = got_ref[got_ref.shape[0] - rows * (SWEEPS + 1) :]
    before, after = sides_of(one, far_ref[0][...] if far_ref else one, "py")
    fields = rows * SWEEPS
    wide_ref[...] = (
        marks_ref[...]
        + pltpu.roll(after[fields:], cols, 1)
        + pltpu.roll(before[fields:], cols + SWEEPS, 1)
    )
    for x in range(rows):
        pick = slice(x * SWEEPS, (x + 1) * SWEEPS)
        side_ref[x] = jnp.concatenate([after[pick], before[pick]], axis=0)
    chosen = lax.axis_index("px") % 2 == 0
    if lax.axis_size("px") > 2:
        chosen = chosen == (lax.axis_index("freq") % 2 == 0)
    top = lax.broadcasted_iota(jnp.int32, (TILE, real), 0) == 0
    step = rows_ref.shape[0] // SWEEPS
    for k in range(SWEEPS):
        last = rows - SWEEPS + k
        marks = jnp.where(chosen, wide_ref[last : last + 1], wide_ref[k : k + 1])
        rows_ref[k * step : (k + 1) * step] = jnp.concatenate(
            [
                jnp.where(chosen, field_ref[last], field_ref[k]),
                jnp.where(chosen, side_ref[last], side_ref[k]),
                jnp.where(top, marks, 0.0),
            ],
            axis=0,
        ).astype(jnp.bfloat16)


def weigh(mine_ref, got_ref, rows_ref, low_ref, both_ref, weighted_ref):
    comps, sensors, real = weighted_ref.shape
    points = comps * sensors
    total = mine_ref[...] + got_ref[...]
    chunk = min(sensors, real)
    eye = lax.broadcasted_iota(jnp.int32, (chunk, real), 0) == lax.broadcasted_iota(
        jnp.int32, (chunk, real), 1
    )
    for k in range(sensors // chunk):
        row = total[points + k : points + k + 1]
        noise = jnp.sum(jnp.where(eye, row, 0.0), axis=1, keepdims=True)
        inverse = 1.0 / (noise * noise)
        misfit = [total[c * sensors + k * chunk : c * sensors + (k + 1) * chunk] for c in range(comps)]
        spread = sum(part * part for part in misfit) * inverse
        factor = (FREEDOM + 2.0) / (FREEDOM + spread) * inverse
        for c in range(comps):
            weighted = misfit[c] * factor
            weighted_ref[c, k * chunk : (k + 1) * chunk] = weighted
            low_ref[c * sensors + k * chunk : c * sensors + (k + 1) * chunk] = weighted.astype(
                jnp.bfloat16
            )
    both_ref[:points] = low_ref[...]
    both_ref[points:] = rows_ref[...]


def prior(
    field_ref,
    side_ref,
    wide_ref,
    rows_ref,
    both_ref,
    table_ref,
    weighted_ref,
    after_ref,
    prior_ref,
    own_out,
    state_ref,
    coef_ref,
    own_ref,
    sem,
):
    own, comps, real = own_ref.shape
    sensors = weighted_ref.shape[1]
    place = lax.axis_index("px") * lax.axis_size("py") + lax.axis_index("py")
    spot = lax.broadcasted_iota(jnp.int32, (sensors, real), 0)
    for c in range(comps):
        for k in range(own):
            own_ref[k, c : c + 1] = jnp.sum(
                jnp.where(spot == place * own + k, weighted_ref[c], 0.0), axis=0, keepdims=True
            )
    out = pltpu.make_async_copy(own_ref, own_out, sem)
    out.start()
    rows, cols, _ = field_ref.shape
    wide = cols + 2 * SWEEPS
    step = rows_ref.shape[0] // SWEEPS
    mine = rows_ref[...].astype(jnp.float32)
    other = both_ref[both_ref.shape[0] - rows_ref.shape[0] :].astype(jnp.float32)
    even = lax.axis_index("freq") % 2 == 0
    before, after = sides_of(
        jnp.where(even, mine, other), jnp.where(even, other, mine), "px"
    )
    for k in range(SWEEPS):
        state_ref[0, k] = before[k * step : k * step + wide]
        state_ref[0, SWEEPS + rows + k] = after[k * step : k * step + wide]
    for x in range(rows):
        state_ref[0, SWEEPS + x] = jnp.concatenate([field_ref[x], side_ref[x]], axis=0)
    marks = (
        [before[k * step + wide : k * step + wide + 1] for k in range(SWEEPS)]
        + [wide_ref[x : x + 1] for x in range(rows)]
        + [after[k * step + wide : k * step + wide + 1] for k in range(SWEEPS)]
    )
    count, levels = table_ref.shape
    spread = (
        lax.broadcasted_iota(jnp.int32, (count, count * real), 1) // real
        == lax.broadcasted_iota(jnp.int32, (count, count * real), 0)
    ).astype(jnp.float32)
    turn = (((0,), (0,)), ((), ()))
    table = lax.dot_general(
        table_ref[...],
        spread,
        turn,
        precision=lax.Precision.HIGHEST,
        preferred_element_type=jnp.float32,
    )
    high = table.astype(jnp.bfloat16)
    rest = table - high.astype(jnp.float32)
    middle = rest.astype(jnp.bfloat16)
    low = (rest - middle.astype(jnp.float32)).astype(jnp.bfloat16)
    table = jnp.concatenate([high, middle, low], axis=0)
    level = lax.broadcasted_iota(jnp.int32, (levels, real), 0).astype(jnp.float32) + 1.0
    for x in range(1, 2 * SWEEPS + rows - 1):
        onehot = (level == marks[x]).astype(jnp.float32).astype(jnp.bfloat16)
        onehot = jnp.concatenate([onehot] * 3, axis=0)[:, :wide]
        coef = lax.dot_general(onehot, table, turn, preferred_element_type=jnp.float32)
        for c in range(count):
            coef_ref[x, c] = coef[:, c * real : (c + 1) * real]
    for sweep in range(SWEEPS):
        now, later = sweep % 2, (sweep + 1) % 2
        for x in range(sweep + 1, 2 * SWEEPS + rows - sweep - 1):
            center = state_ref[now, x]
            beside = (
                coef_ref[x, 1] * state_ref[now, x - 1]
                + coef_ref[x, 2] * state_ref[now, x + 1]
                + coef_ref[x, 3] * pltpu.roll(center, 1, 0)
                + coef_ref[x, 4] * pltpu.roll(center, wide - 1, 0)
            )
            new = coef_ref[x, 0] * center - beside
            if sweep < SWEEPS - 1:
                state_ref[later, x] = new
            else:
                prior_ref[x - SWEEPS] = PRIOR_WEIGHT * new[:cols]
    out.wait()


def finish(pair_ref, far_ref, prior_ref, low0_ref, low1_ref, low3_ref, low2_ref, out, held_ref, sems):
    rows, cols, real = held_ref.shape
    beside = pair_ref.shape[0] // 2
    side = rows // beside
    points = low0_ref.shape[0]
    low = jnp.concatenate(
        [low0_ref[...], low1_ref[:points], low2_ref[...], low3_ref[...]], axis=0
    )
    copies = []
    for x in range(beside):
        kernel = jnp.concatenate(
            [pair_ref[x], pair_ref[beside + x], far_ref[x], far_ref[beside + x]], axis=0
        )
        grad = lax.dot_general(
            kernel, low, (((0,), (0,)), ((), ())), preferred_element_type=jnp.float32
        )
        for k in range(side):
            row = k * beside + x
            held_ref[row] = grad[k * cols : (k + 1) * cols] + prior_ref[row]
            copies.append(pltpu.make_async_copy(held_ref.at[row], out.at[row], sems.at[row]))
            copies[-1].start()
    for copy in copies:
        copy.wait()


def local(observed, noise_scale, forward_kernel, model_field, classes, kappa_table, coupling_table):
    rows, cols, real = model_field.shape
    comps, sensors = forward_kernel.shape[3:]
    own = observed.shape[1]
    points = comps * sensors
    kernel_own = forward_kernel[0].transpose(0, 2, 3, 1).reshape(rows, points, cols)
    beside = rows // max(1, min(rows, LANES // cols))
    side = rows // beside
    assert sensors <= TILE * real and cols + 2 * SWEEPS <= LANES
    assert rows >= SWEEPS and (cols + 2 * SWEEPS + TILE) % 16 == 0
    rim_rows = rows * (SWEEPS + 1)
    wide_py, wide_px = lax.axis_size("py") > 2, lax.axis_size("px") > 2
    payload, kernel_own, model_field, marks, table, *far_rim = call(
        prepare,
        ((points + TILE + rim_rows, real), jnp.float32),
        ((beside, points, side * cols), jnp.bfloat16),
        (model_field.shape, jnp.float32),
        ((rows, LANES), jnp.float32),
        ((1 + coupling_table.shape[0], coupling_table.shape[1]), jnp.float32),
        *[((rim_rows, real), jnp.float32)] * wide_py,
        fetch=True,
    )(
        noise_scale,
        observed[0],
        kernel_own,
        model_field,
        classes,
        kappa_table[None],
        coupling_table,
    )
    got = swap(payload, "py", near)
    kernel_next = swap(kernel_own, "freq", near)
    two = [swap(rim, "py", far("py")) for rim in far_rim]
    summed = ((points + TILE, real), jnp.float32)
    (total,) = call(add, summed)(payload, got)
    for bit in bits("py")[1:]:
        (total,) = call(add, summed)(total, swap(total, "py", lambda i: i ^ bit))
    step = cols + 2 * SWEEPS + TILE
    side_rim, wide_marks, rim_rows = call(
        edge,
        ((rows, 2 * SWEEPS, real), jnp.float32),
        ((rows, LANES), jnp.float32),
        ((SWEEPS * step, real), jnp.bfloat16),
        flops=EDGE_FLOPS,
    )(total, got, model_field, marks, *two)
    peers = lax.axis_size("px")
    rim_rows = lax.ppermute(
        rim_rows,
        ("freq", "px"),
        [
            (f * peers + i, f * peers + (far("px")(i) if f % 2 and wide_px else near(i)))
            for f in range(lax.axis_size("freq"))
            for i in range(peers)
        ],
    )
    *steps, last = bits("px")
    for bit in steps[:-1]:
        (total,) = call(add, summed)(total, swap(total, "px", lambda i: i ^ bit))
    total, kernel_pair = call(
        add_and_join, summed, ((2 * beside, points, side * cols), jnp.bfloat16), flops=ORDER_FLOPS
    )(total, swap(total, "px", lambda i: i ^ steps[-1]), kernel_own, kernel_next)
    kernel_far = swap(kernel_pair, "freq", lambda i: i ^ 2)
    assert lax.axis_size("freq") == 4
    weighted_low, weighted_both, weighted = call(
        weigh,
        ((points, real), jnp.bfloat16),
        ((points + SWEEPS * step, real), jnp.bfloat16),
        ((comps, sensors, real), jnp.float32),
    )(total, swap(total, "px", lambda i: i ^ last), rim_rows)
    both_next = swap(weighted_both, "freq", near)
    low_three = swap(weighted_low, "freq", lambda i: i ^ 3)
    low_two = swap(weighted_low, "freq", lambda i: i ^ 2)
    wide = cols + 2 * SWEEPS
    prior_term, weighted_own = call(
        prior,
        (model_field.shape, jnp.float32),
        ((own, comps, real), jnp.float32),
        stored=(1,),
        scratch=(
            pltpu.VMEM((2, rows + 2 * SWEEPS, wide, real), jnp.float32),
            pltpu.VMEM((rows + 2 * SWEEPS, table.shape[0], wide, real), jnp.float32),
            pltpu.VMEM((own, comps, real), jnp.float32),
            pltpu.SemaphoreType.DMA(()),
        ),
        flops=PRIOR_FLOPS,
    )(model_field, side_rim, wide_marks, rim_rows, both_next, table, weighted, kernel_far)
    (gradient,) = call(
        finish,
        (model_field.shape, jnp.float32),
        stored=(0,),
        scratch=(
            pltpu.VMEM(model_field.shape, jnp.float32),
            pltpu.SemaphoreType.DMA((rows,)),
        ),
    )(kernel_pair, kernel_far, prior_term, weighted_low, both_next, low_three, low_two)
    return weighted_own[None], gradient


def solution(mesh):
    in_specs = (
        P("freq", ("px", "py"), None, None),
        P("freq", ("px", "py")),
        P("freq", "px", "py", None, None),
        P("px", "py", None),
        P("px", "py"),
        P(),
        P(),
    )
    out_specs = (P("freq", ("px", "py"), None, None), P("px", "py", None))
    return jax.shard_map(local, mesh=mesh, in_specs=in_specs, out_specs=out_specs, check_vma=False)
```

```python
import jax
import jax.numpy as jnp
from jax import lax
from jax.experimental import pallas as pl
from jax.experimental.pallas import tpu as pltpu
from jax.sharding import PartitionSpec as P

SWEEPS = 4
FREEDOM = 4.0
PRIOR_WEIGHT = 0.04
LANES = 128
TILE = 8
VMEM_BYTES = 40 << 20
PRIOR_FLOPS = 1 << 30
EDGE_FLOPS = 1 << 30
ORDER_FLOPS = 1 << 32


def swap(own, axis, partner):
    return lax.ppermute(own, axis, [(i, partner(i)) for i in range(lax.axis_size(axis))])


def bits(axis):
    size = lax.axis_size(axis)
    assert size & (size - 1) == 0
    return [1 << k for k in range(size.bit_length() - 1)]


def near(i):
    return i ^ 1


def far(axis):
    return lambda i: (((i + 1) ^ 1) - 1) % lax.axis_size(axis)


def call(body, *out_shapes, fetch=False, scratch=(), stored=(), flops=0):
    def run(*operands):
        count = len(operands)
        if fetch:
            operands = [pltpu.with_memory_space_constraint(x, pltpu.HBM) for x in operands]

        def fetched(*refs):
            outs, held, sems = (
                refs[count : count + len(out_shapes)],
                refs[count + len(out_shapes) : -1],
                refs[-1],
            )
            copies = [
                pltpu.make_async_copy(src, dst, sems.at[k])
                for k, (src, dst) in enumerate(zip(refs[:count], held))
            ]
            for copy in copies:
                copy.start()
            for copy in copies:
                copy.wait()
            body(*held, *outs)

        return pl.pallas_call(
            fetched if fetch else body,
            out_shape=[jax.ShapeDtypeStruct(shape, dtype) for shape, dtype in out_shapes],
            in_specs=[pl.BlockSpec(memory_space=pltpu.HBM if fetch else pltpu.VMEM)] * count,
            out_specs=[
                pl.BlockSpec(memory_space=pltpu.HBM if k in stored else pltpu.VMEM)
                for k in range(len(out_shapes))
            ],
            scratch_shapes=list(scratch)
            + [pltpu.VMEM(x.shape, x.dtype) for x in operands] * fetch
            + [pltpu.SemaphoreType.DMA((count,))] * fetch,
            compiler_params=pltpu.CompilerParams(vmem_limit_bytes=VMEM_BYTES),
            cost_estimate=pl.CostEstimate(flops=flops, bytes_accessed=0, transcendentals=0),
        )(*operands)

    return run


def prepare(
    noise_ref,
    observed_ref,
    kernel_ref,
    field_ref,
    classes_ref,
    kappa_ref,
    coupling_ref,
    pay_ref,
    packed_ref,
    held_ref,
    marks_ref,
    table_ref,
    *far_ref,
):
    beside, points, width = packed_ref.shape
    rows, cols, real = field_ref.shape
    own, comps = observed_ref.shape[:2]
    sensors = points // comps
    place = lax.axis_index("px") * lax.axis_size("py") + lax.axis_index("py")
    even = lax.axis_index("py") % 2 == 0
    total = jnp.zeros((points, real), jnp.float32)
    for x in range(beside):
        picks = range(x, rows, beside)
        packed = jnp.concatenate([kernel_ref[k] for k in picks], axis=1)
        packed_ref[x] = packed
        field = jnp.concatenate([field_ref[k].astype(jnp.bfloat16) for k in picks], axis=0)
        total = total + jnp.dot(packed, field, preferred_element_type=jnp.float32)
    spot = lax.broadcasted_iota(jnp.int32, (points, real), 0)
    for c in range(comps):
        for k in range(own):
            row = c * sensors + place * own + k
            total = total - jnp.where(spot == row, observed_ref[k, c : c + 1, :], 0.0)
    pay_ref[:points] = total
    spot = lax.broadcasted_iota(jnp.int32, (TILE, real), 0) * real + lax.broadcasted_iota(
        jnp.int32, (TILE, real), 1
    )
    noise = jnp.zeros((TILE, real), jnp.float32)
    for k in range(own):
        noise = noise + jnp.where(spot == place * own + k, noise_ref[0:1, k : k + 1], 0.0)
    pay_ref[points : points + TILE] = noise
    held_ref[...] = field_ref[...]
    coupling = coupling_ref[...]
    table_ref[0:1] = kappa_ref[...] + jnp.sum(coupling, axis=0, keepdims=True)
    table_ref[1:] = coupling
    marks = (classes_ref[...] + 1).astype(jnp.float32)
    marks_ref[...] = jnp.zeros_like(marks_ref)
    marks_ref[:, :cols] = marks
    edges = [
        (field_ref[:, cols - SWEEPS :, :], marks[:, cols - SWEEPS :]),
        (field_ref[:, :SWEEPS, :], marks[:, :SWEEPS]),
    ]

    def put(ref, start, chosen):
        for x in range(rows):
            ref[start + x * SWEEPS : start + (x + 1) * SWEEPS] = jnp.where(
                chosen, edges[0][0][x], edges[1][0][x]
            )
        start = start + rows * SWEEPS
        ref[start : start + rows] = jnp.zeros((rows, real), jnp.float32)
        ref[start : start + rows, :SWEEPS] = jnp.where(chosen, edges[0][1], edges[1][1])

    put(pay_ref, points + TILE, even)
    for ref in far_ref:
        put(ref, 0, jnp.logical_not(even))


def sides_of(one, two, axis):
    me = lax.axis_index(axis)
    even = me % 2 == 0
    before = jnp.where(me == 0, 0.0, jnp.where(even, two, one))
    after = jnp.where(me == lax.axis_size(axis) - 1, 0.0, jnp.where(even, one, two))
    return before, after


def add(mine_ref, got_ref, out_ref):
    size = out_ref.shape[0]
    out_ref[...] = mine_ref[:size] + got_ref[:size]


def add_and_join(mine_ref, got_ref, one_ref, two_ref, out_ref, joined_ref):
    out_ref[...] = mine_ref[...] + got_ref[...]
    half = one_ref.shape[0]
    joined_ref[:half] = one_ref[...]
    joined_ref[half:] = two_ref[...]


def edge(after_ref, got_ref, field_ref, marks_ref, *refs):
    *far_ref, side_ref, wide_ref, rows_ref = refs
    rows, cols, real = field_ref.shape
    one = got_ref[got_ref.shape[0] - rows * (SWEEPS + 1) :]
    before, after = sides_of(one, far_ref[0][...] if far_ref else one, "py")
    fields = rows * SWEEPS
    wide_ref[...] = (
        marks_ref[...]
        + pltpu.roll(after[fields:], cols, 1)
        + pltpu.roll(before[fields:], cols + SWEEPS, 1)
    )
    for x in range(rows):
        pick = slice(x * SWEEPS, (x + 1) * SWEEPS)
        side_ref[x] = jnp.concatenate([after[pick], before[pick]], axis=0)
    chosen = lax.axis_index("px") % 2 == 0
    if lax.axis_size("px") > 2:
        chosen = chosen == (lax.axis_index("freq") % 2 == 0)
    top = lax.broadcasted_iota(jnp.int32, (TILE, real), 0) == 0
    step = rows_ref.shape[0] // SWEEPS
    for k in range(SWEEPS):
        last = rows - SWEEPS + k
        marks = jnp.where(chosen, wide_ref[last : last + 1], wide_ref[k : k + 1])
        rows_ref[k * step : (k + 1) * step] = jnp.concatenate(
            [
                jnp.where(chosen, field_ref[last], field_ref[k]),
                jnp.where(chosen, side_ref[last], side_ref[k]),
                jnp.where(top, marks, 0.0),
            ],
            axis=0,
        ).astype(jnp.bfloat16)


def weigh(mine_ref, got_ref, low_ref, weighted_ref):
    comps, sensors, real = weighted_ref.shape
    points = comps * sensors
    total = mine_ref[...] + got_ref[...]
    chunk = min(sensors, real)
    eye = lax.broadcasted_iota(jnp.int32, (chunk, real), 0) == lax.broadcasted_iota(
        jnp.int32, (chunk, real), 1
    )
    for k in range(sensors // chunk):
        row = total[points + k : points + k + 1]
        noise = jnp.sum(jnp.where(eye, row, 0.0), axis=1, keepdims=True)
        inverse = 1.0 / (noise * noise)
        misfit = [total[c * sensors + k * chunk : c * sensors + (k + 1) * chunk] for c in range(comps)]
        spread = sum(part * part for part in misfit) * inverse
        factor = (FREEDOM + 2.0) / (FREEDOM + spread) * inverse
        for c in range(comps):
            weighted = misfit[c] * factor
            weighted_ref[c, k * chunk : (k + 1) * chunk] = weighted
            low_ref[c * sensors + k * chunk : c * sensors + (k + 1) * chunk] = weighted.astype(
                jnp.bfloat16
            )


def prior(
    field_ref,
    side_ref,
    wide_ref,
    rows_ref,
    other_ref,
    table_ref,
    weighted_ref,
    prior_ref,
    own_out,
    state_ref,
    coef_ref,
    own_ref,
    sem,
):
    own, comps, real = own_ref.shape
    sensors = weighted_ref.shape[1]
    place = lax.axis_index("px") * lax.axis_size("py") + lax.axis_index("py")
    spot = lax.broadcasted_iota(jnp.int32, (sensors, real), 0)
    for c in range(comps):
        for k in range(own):
            own_ref[k, c : c + 1] = jnp.sum(
                jnp.where(spot == place * own + k, weighted_ref[c], 0.0), axis=0, keepdims=True
            )
    out = pltpu.make_async_copy(own_ref, own_out, sem)
    out.start()
    rows, cols, _ = field_ref.shape
    wide = cols + 2 * SWEEPS
    step = rows_ref.shape[0] // SWEEPS
    mine = rows_ref[...].astype(jnp.float32)
    other = other_ref[...].astype(jnp.float32)
    even = lax.axis_index("freq") % 2 == 0
    before, after = sides_of(
        jnp.where(even, mine, other), jnp.where(even, other, mine), "px"
    )
    for k in range(SWEEPS):
        state_ref[0, k] = before[k * step : k * step + wide]
        state_ref[0, SWEEPS + rows + k] = after[k * step : k * step + wide]
    for x in range(rows):
        state_ref[0, SWEEPS + x] = jnp.concatenate([field_ref[x], side_ref[x]], axis=0)
    marks = (
        [before[k * step + wide : k * step + wide + 1] for k in range(SWEEPS)]
        + [wide_ref[x : x + 1] for x in range(rows)]
        + [after[k * step + wide : k * step + wide + 1] for k in range(SWEEPS)]
    )
    count, levels = table_ref.shape
    spread = (
        lax.broadcasted_iota(jnp.int32, (count, count * real), 1) // real
        == lax.broadcasted_iota(jnp.int32, (count, count * real), 0)
    ).astype(jnp.float32)
    turn = (((0,), (0,)), ((), ()))
    table = lax.dot_general(
        table_ref[...],
        spread,
        turn,
        precision=lax.Precision.HIGHEST,
        preferred_element_type=jnp.float32,
    )
    high = table.astype(jnp.bfloat16)
    rest = table - high.astype(jnp.float32)
    middle = rest.astype(jnp.bfloat16)
    low = (rest - middle.astype(jnp.float32)).astype(jnp.bfloat16)
    table = jnp.concatenate([high, middle, low], axis=0)
    level = lax.broadcasted_iota(jnp.int32, (levels, real), 0).astype(jnp.float32) + 1.0
    for x in range(1, 2 * SWEEPS + rows - 1):
        onehot = (level == marks[x]).astype(jnp.float32).astype(jnp.bfloat16)
        onehot = jnp.concatenate([onehot] * 3, axis=0)[:, :wide]
        coef = lax.dot_general(onehot, table, turn, preferred_element_type=jnp.float32)
        for c in range(count):
            coef_ref[x, c] = coef[:, c * real : (c + 1) * real]
    for sweep in range(SWEEPS):
        now, later = sweep % 2, (sweep + 1) % 2
        for x in range(sweep + 1, 2 * SWEEPS + rows - sweep - 1):
            center = state_ref[now, x]
            beside = (
                coef_ref[x, 1] * state_ref[now, x - 1]
                + coef_ref[x, 2] * state_ref[now, x + 1]
                + coef_ref[x, 3] * pltpu.roll(center, 1, 0)
                + coef_ref[x, 4] * pltpu.roll(center, wide - 1, 0)
            )
            new = coef_ref[x, 0] * center - beside
            if sweep < SWEEPS - 1:
                state_ref[later, x] = new
            else:
                prior_ref[x - SWEEPS] = PRIOR_WEIGHT * new[:cols]
    out.wait()


def finish(pair_ref, far_ref, prior_ref, low0_ref, low3_ref, low2_ref, low1_ref, out, held_ref, sems):
    rows, cols, real = held_ref.shape
    beside = pair_ref.shape[0] // 2
    side = rows // beside
    low = jnp.concatenate([low0_ref[...], low1_ref[...], low2_ref[...], low3_ref[...]], axis=0)
    copies = []
    for x in range(beside):
        kernel = jnp.concatenate(
            [pair_ref[x], pair_ref[beside + x], far_ref[x], far_ref[beside + x]], axis=0
        )
        grad = lax.dot_general(
            kernel, low, (((0,), (0,)), ((), ())), preferred_element_type=jnp.float32
        )
        for k in range(side):
            row = k * beside + x
            held_ref[row] = grad[k * cols : (k + 1) * cols] + prior_ref[row]
            copies.append(pltpu.make_async_copy(held_ref.at[row], out.at[row], sems.at[row]))
            copies[-1].start()
    for copy in copies:
        copy.wait()


def local(observed, noise_scale, forward_kernel, model_field, classes, kappa_table, coupling_table):
    rows, cols, real = model_field.shape
    comps, sensors = forward_kernel.shape[3:]
    own = observed.shape[1]
    points = comps * sensors
    kernel_own = forward_kernel[0].transpose(0, 2, 3, 1).reshape(rows, points, cols)
    beside = rows // max(1, min(rows, LANES // cols))
    side = rows // beside
    assert sensors <= TILE * real and cols + 2 * SWEEPS <= LANES
    assert rows >= SWEEPS and (cols + 2 * SWEEPS + TILE) % 16 == 0
    rim_rows = rows * (SWEEPS + 1)
    wide_py, wide_px = lax.axis_size("py") > 2, lax.axis_size("px") > 2
    payload, kernel_own, model_field, marks, table, *far_rim = call(
        prepare,
        ((points + TILE + rim_rows, real), jnp.float32),
        ((beside, points, side * cols), jnp.bfloat16),
        (model_field.shape, jnp.float32),
        ((rows, LANES), jnp.float32),
        ((1 + coupling_table.shape[0], coupling_table.shape[1]), jnp.float32),
        *[((rim_rows, real), jnp.float32)] * wide_py,
        fetch=True,
    )(
        noise_scale,
        observed[0],
        kernel_own,
        model_field,
        classes,
        kappa_table[None],
        coupling_table,
    )
    got = swap(payload, "py", near)
    kernel_next = swap(kernel_own, "freq", near)
    two = [swap(rim, "py", far("py")) for rim in far_rim]
    summed = ((points + TILE, real), jnp.float32)
    (total,) = call(add, summed)(payload, got)
    for bit in bits("py")[1:]:
        (total,) = call(add, summed)(total, swap(total, "py", lambda i: i ^ bit))
    step = cols + 2 * SWEEPS + TILE
    side_rim, wide_marks, rim_rows = call(
        edge,
        ((rows, 2 * SWEEPS, real), jnp.float32),
        ((rows, LANES), jnp.float32),
        ((SWEEPS * step, real), jnp.bfloat16),
        flops=EDGE_FLOPS,
    )(total, got, model_field, marks, *two)
    peers = lax.axis_size("px")
    rim_rows = lax.ppermute(
        rim_rows,
        ("freq", "px"),
        [
            (f * peers + i, f * peers + (far("px")(i) if f % 2 and wide_px else near(i)))
            for f in range(lax.axis_size("freq"))
            for i in range(peers)
        ],
    )
    *steps, last = bits("px")
    for bit in steps[:-1]:
        (total,) = call(add, summed)(total, swap(total, "px", lambda i: i ^ bit))
    total, kernel_pair = call(
        add_and_join, summed, ((2 * beside, points, side * cols), jnp.bfloat16), flops=ORDER_FLOPS
    )(total, swap(total, "px", lambda i: i ^ steps[-1]), kernel_own, kernel_next)
    kernel_far = swap(kernel_pair, "freq", lambda i: i ^ 2)
    assert lax.axis_size("freq") == 4
    weighted_low, weighted = call(
        weigh,
        ((points, real), jnp.bfloat16),
        ((comps, sensors, real), jnp.float32),
        flops=ORDER_FLOPS,
    )(total, swap(total, "px", lambda i: i ^ last))
    other_rows = swap(rim_rows, "freq", near)
    low_one = swap(weighted_low, "freq", near)
    low_three = swap(weighted_low, "freq", lambda i: i ^ 3)
    low_two = swap(weighted_low, "freq", lambda i: i ^ 2)
    wide = cols + 2 * SWEEPS
    prior_term, weighted_own = call(
        prior,
        (model_field.shape, jnp.float32),
        ((own, comps, real), jnp.float32),
        stored=(1,),
        scratch=(
            pltpu.VMEM((2, rows + 2 * SWEEPS, wide, real), jnp.float32),
            pltpu.VMEM((rows + 2 * SWEEPS, table.shape[0], wide, real), jnp.float32),
            pltpu.VMEM((own, comps, real), jnp.float32),
            pltpu.SemaphoreType.DMA(()),
        ),
        flops=PRIOR_FLOPS,
    )(model_field, side_rim, wide_marks, rim_rows, other_rows, table, weighted)
    (gradient,) = call(
        finish,
        (model_field.shape, jnp.float32),
        stored=(0,),
        scratch=(
            pltpu.VMEM(model_field.shape, jnp.float32),
            pltpu.SemaphoreType.DMA((rows,)),
        ),
    )(kernel_pair, kernel_far, prior_term, weighted_low, low_three, low_two, low_one)
    return weighted_own[None], gradient


def solution(mesh):
    in_specs = (
        P("freq", ("px", "py"), None, None),
        P("freq", ("px", "py")),
        P("freq", "px", "py", None, None),
        P("px", "py", None),
        P("px", "py"),
        P(),
        P(),
    )
    out_specs = (P("freq", ("px", "py"), None, None), P("px", "py", None))
    return jax.shard_map(local, mesh=mesh, in_specs=in_specs, out_specs=out_specs, check_vma=False)
```

```python
import jax
import jax.numpy as jnp
from jax import lax
from jax.experimental import pallas as pl
from jax.experimental.pallas import tpu as pltpu
from jax.sharding import PartitionSpec as P

SWEEPS = 4
FREEDOM = 4.0
PRIOR_WEIGHT = 0.04
LANES = 128
TILE = 8
VMEM_BYTES = 40 << 20
PRIOR_FLOPS = 1 << 30
EDGE_FLOPS = 1 << 30
JOIN_FLOPS = 1 << 30
ORDER_FLOPS = 1 << 32


def swap(own, axis, partner):
    return lax.ppermute(own, axis, [(i, partner(i)) for i in range(lax.axis_size(axis))])


def bits(axis):
    size = lax.axis_size(axis)
    assert size & (size - 1) == 0
    return [1 << k for k in range(size.bit_length() - 1)]


def near(i):
    return i ^ 1


def far(axis):
    return lambda i: (((i + 1) ^ 1) - 1) % lax.axis_size(axis)


def call(body, *out_shapes, fetch=False, scratch=(), stored=(), flops=0):
    def run(*operands):
        count = len(operands)
        if fetch:
            operands = [pltpu.with_memory_space_constraint(x, pltpu.HBM) for x in operands]

        def fetched(*refs):
            outs, held, sems = (
                refs[count : count + len(out_shapes)],
                refs[count + len(out_shapes) : -1],
                refs[-1],
            )
            copies = [
                pltpu.make_async_copy(src, dst, sems.at[k])
                for k, (src, dst) in enumerate(zip(refs[:count], held))
            ]
            for copy in copies:
                copy.start()
            for copy in copies:
                copy.wait()
            body(*held, *outs)

        return pl.pallas_call(
            fetched if fetch else body,
            out_shape=[jax.ShapeDtypeStruct(shape, dtype) for shape, dtype in out_shapes],
            in_specs=[pl.BlockSpec(memory_space=pltpu.HBM if fetch else pltpu.VMEM)] * count,
            out_specs=[
                pl.BlockSpec(memory_space=pltpu.HBM if k in stored else pltpu.VMEM)
                for k in range(len(out_shapes))
            ],
            scratch_shapes=list(scratch)
            + [pltpu.VMEM(x.shape, x.dtype) for x in operands] * fetch
            + [pltpu.SemaphoreType.DMA((count,))] * fetch,
            compiler_params=pltpu.CompilerParams(vmem_limit_bytes=VMEM_BYTES),
            cost_estimate=pl.CostEstimate(flops=flops, bytes_accessed=0, transcendentals=0),
        )(*operands)

    return run


def prepare(
    noise_ref,
    observed_ref,
    kernel_ref,
    field_ref,
    classes_ref,
    kappa_ref,
    coupling_ref,
    pay_ref,
    packed_ref,
    held_ref,
    marks_ref,
    table_ref,
    *far_ref,
):
    beside, points, width = packed_ref.shape
    rows, cols, real = field_ref.shape
    own, comps = observed_ref.shape[:2]
    sensors = points // comps
    place = lax.axis_index("px") * lax.axis_size("py") + lax.axis_index("py")
    even = lax.axis_index("py") % 2 == 0
    total = jnp.zeros((points, real), jnp.float32)
    for x in range(beside):
        picks = range(x, rows, beside)
        packed = jnp.concatenate([kernel_ref[k] for k in picks], axis=1)
        packed_ref[x] = packed
        field = jnp.concatenate([field_ref[k].astype(jnp.bfloat16) for k in picks], axis=0)
        total = total + jnp.dot(packed, field, preferred_element_type=jnp.float32)
    spot = lax.broadcasted_iota(jnp.int32, (points, real), 0)
    for c in range(comps):
        for k in range(own):
            row = c * sensors + place * own + k
            total = total - jnp.where(spot == row, observed_ref[k, c : c + 1, :], 0.0)
    pay_ref[:points] = total
    spot = lax.broadcasted_iota(jnp.int32, (TILE, real), 0) * real + lax.broadcasted_iota(
        jnp.int32, (TILE, real), 1
    )
    noise = jnp.zeros((TILE, real), jnp.float32)
    for k in range(own):
        noise = noise + jnp.where(spot == place * own + k, noise_ref[0:1, k : k + 1], 0.0)
    pay_ref[points : points + TILE] = noise
    held_ref[...] = field_ref[...]
    coupling = coupling_ref[...]
    table_ref[0:1] = kappa_ref[...] + jnp.sum(coupling, axis=0, keepdims=True)
    table_ref[1:] = coupling
    marks = (classes_ref[...] + 1).astype(jnp.float32)
    marks_ref[...] = jnp.zeros_like(marks_ref)
    marks_ref[:, :cols] = marks
    edges = [
        (field_ref[:, cols - SWEEPS :, :], marks[:, cols - SWEEPS :]),
        (field_ref[:, :SWEEPS, :], marks[:, :SWEEPS]),
    ]

    def put(ref, start, chosen):
        for x in range(rows):
            ref[start + x * SWEEPS : start + (x + 1) * SWEEPS] = jnp.where(
                chosen, edges[0][0][x], edges[1][0][x]
            )
        start = start + rows * SWEEPS
        ref[start : start + rows] = jnp.zeros((rows, real), jnp.float32)
        ref[start : start + rows, :SWEEPS] = jnp.where(chosen, edges[0][1], edges[1][1])

    put(pay_ref, points + TILE, even)
    for ref in far_ref:
        put(ref, 0, jnp.logical_not(even))


def sides_of(one, two, axis):
    me = lax.axis_index(axis)
    even = me % 2 == 0
    before = jnp.where(me == 0, 0.0, jnp.where(even, two, one))
    after = jnp.where(me == lax.axis_size(axis) - 1, 0.0, jnp.where(even, one, two))
    return before, after


def add(mine_ref, got_ref, out_ref):
    size = out_ref.shape[0]
    out_ref[...] = mine_ref[:size] + got_ref[:size]


def add_and_join(mine_ref, got_ref, one_ref, two_ref, out_ref, joined_ref):
    out_ref[...] = mine_ref[...] + got_ref[...]
    half = one_ref.shape[0]
    joined_ref[:half] = one_ref[...]
    joined_ref[half:] = two_ref[...]


def lay(got_ref, field_ref, marks_ref, far_ref, side_ref, wide_ref, rows_ref, base):
    rows, cols, real = field_ref.shape
    one = got_ref[got_ref.shape[0] - rows * (SWEEPS + 1) :]
    before, after = sides_of(one, far_ref[0][...] if far_ref else one, "py")
    fields = rows * SWEEPS
    wide_ref[...] = (
        marks_ref[...]
        + pltpu.roll(after[fields:], cols, 1)
        + pltpu.roll(before[fields:], cols + SWEEPS, 1)
    )
    for x in range(rows):
        pick = slice(x * SWEEPS, (x + 1) * SWEEPS)
        side_ref[x] = jnp.concatenate([after[pick], before[pick]], axis=0)
    chosen = lax.axis_index("px") % 2 == 0
    if lax.axis_size("px") > 2:
        chosen = chosen == (lax.axis_index("freq") % 2 == 0)
    top = lax.broadcasted_iota(jnp.int32, (TILE, real), 0) == 0
    step = (rows_ref.shape[0] - base) // SWEEPS
    for k in range(SWEEPS):
        last = rows - SWEEPS + k
        marks = jnp.where(chosen, wide_ref[last : last + 1], wide_ref[k : k + 1])
        rows_ref[base + k * step : base + (k + 1) * step] = jnp.concatenate(
            [
                jnp.where(chosen, field_ref[last], field_ref[k]),
                jnp.where(chosen, side_ref[last], side_ref[k]),
                jnp.where(top, marks, 0.0),
            ],
            axis=0,
        ).astype(jnp.bfloat16)


def edge(after_ref, got_ref, field_ref, marks_ref, *refs):
    *far_ref, side_ref, wide_ref, rows_ref = refs
    lay(got_ref, field_ref, marks_ref, far_ref, side_ref, wide_ref, rows_ref, 0)


def packed_rows(size):
    return -(-size // 16) * 16


def spread(mine_ref, got_ref, field_ref, marks_ref, *refs):
    *far_ref, out_ref, side_ref, wide_ref, mixed_ref = refs
    size, real = out_ref.shape
    total = mine_ref[:size] + got_ref[:size]
    out_ref[...] = total
    part = packed_rows(size)
    rest = total
    if part > size:
        rest = jnp.concatenate([total, jnp.zeros((part - size, real), jnp.float32)], axis=0)
    for k in range(3):
        low = rest.astype(jnp.bfloat16)
        mixed_ref[k * part : (k + 1) * part] = low
        rest = rest - low.astype(jnp.float32)
    lay(got_ref, field_ref, marks_ref, far_ref, side_ref, wide_ref, mixed_ref, 3 * part)


def join(one_ref, two_ref, after_ref, out_ref):
    half = one_ref.shape[0]
    out_ref[:half] = one_ref[...]
    out_ref[half:] = two_ref[...]


def weigh(*refs):
    mine_ref, *got_refs, low_ref, weighted_ref = refs
    comps, sensors, real = weighted_ref.shape
    points = comps * sensors
    total = mine_ref[...]
    size = total.shape[0]
    for got_ref in got_refs:
        if got_ref.dtype == jnp.bfloat16:
            part = packed_rows(size)
            three = [got_ref[k * part : (k + 1) * part].astype(jnp.float32) for k in range(3)]
            total = total + (three[0] + three[1] + three[2])[:size]
        else:
            total = total + got_ref[...]
    chunk = min(sensors, real)
    eye = lax.broadcasted_iota(jnp.int32, (chunk, real), 0) == lax.broadcasted_iota(
        jnp.int32, (chunk, real), 1
    )
    for k in range(sensors // chunk):
        row = total[points + k : points + k + 1]
        noise = jnp.sum(jnp.where(eye, row, 0.0), axis=1, keepdims=True)
        inverse = 1.0 / (noise * noise)
        misfit = [total[c * sensors + k * chunk : c * sensors + (k + 1) * chunk] for c in range(comps)]
        spread = sum(part * part for part in misfit) * inverse
        factor = (FREEDOM + 2.0) / (FREEDOM + spread) * inverse
        for c in range(comps):
            weighted = misfit[c] * factor
            weighted_ref[c, k * chunk : (k + 1) * chunk] = weighted
            low_ref[c * sensors + k * chunk : c * sensors + (k + 1) * chunk] = weighted.astype(
                jnp.bfloat16
            )


def prior(
    field_ref,
    side_ref,
    wide_ref,
    rows_ref,
    other_ref,
    table_ref,
    weighted_ref,
    prior_ref,
    own_out,
    state_ref,
    coef_ref,
    own_ref,
    sem,
):
    own, comps, real = own_ref.shape
    sensors = weighted_ref.shape[1]
    place = lax.axis_index("px") * lax.axis_size("py") + lax.axis_index("py")
    spot = lax.broadcasted_iota(jnp.int32, (sensors, real), 0)
    for c in range(comps):
        for k in range(own):
            own_ref[k, c : c + 1] = jnp.sum(
                jnp.where(spot == place * own + k, weighted_ref[c], 0.0), axis=0, keepdims=True
            )
    out = pltpu.make_async_copy(own_ref, own_out, sem)
    out.start()
    rows, cols, _ = field_ref.shape
    wide = cols + 2 * SWEEPS
    step = other_ref.shape[0] // SWEEPS
    mine = rows_ref[rows_ref.shape[0] - other_ref.shape[0] :].astype(jnp.float32)
    other = other_ref[...].astype(jnp.float32)
    even = lax.axis_index("freq") % 2 == 0
    before, after = sides_of(
        jnp.where(even, mine, other), jnp.where(even, other, mine), "px"
    )
    for k in range(SWEEPS):
        state_ref[0, k] = before[k * step : k * step + wide]
        state_ref[0, SWEEPS + rows + k] = after[k * step : k * step + wide]
    for x in range(rows):
        state_ref[0, SWEEPS + x] = jnp.concatenate([field_ref[x], side_ref[x]], axis=0)
    marks = (
        [before[k * step + wide : k * step + wide + 1] for k in range(SWEEPS)]
        + [wide_ref[x : x + 1] for x in range(rows)]
        + [after[k * step + wide : k * step + wide + 1] for k in range(SWEEPS)]
    )
    count, levels = table_ref.shape
    spread = (
        lax.broadcasted_iota(jnp.int32, (count, count * real), 1) // real
        == lax.broadcasted_iota(jnp.int32, (count, count * real), 0)
    ).astype(jnp.float32)
    turn = (((0,), (0,)), ((), ()))
    table = lax.dot_general(
        table_ref[...],
        spread,
        turn,
        precision=lax.Precision.HIGHEST,
        preferred_element_type=jnp.float32,
    )
    high = table.astype(jnp.bfloat16)
    rest = table - high.astype(jnp.float32)
    middle = rest.astype(jnp.bfloat16)
    low = (rest - middle.astype(jnp.float32)).astype(jnp.bfloat16)
    table = jnp.concatenate([high, middle, low], axis=0)
    level = lax.broadcasted_iota(jnp.int32, (levels, real), 0).astype(jnp.float32) + 1.0
    for x in range(1, 2 * SWEEPS + rows - 1):
        onehot = (level == marks[x]).astype(jnp.float32).astype(jnp.bfloat16)
        onehot = jnp.concatenate([onehot] * 3, axis=0)[:, :wide]
        coef = lax.dot_general(onehot, table, turn, preferred_element_type=jnp.float32)
        for c in range(count):
            coef_ref[x, c] = coef[:, c * real : (c + 1) * real]
    for sweep in range(SWEEPS):
        now, later = sweep % 2, (sweep + 1) % 2
        for x in range(sweep + 1, 2 * SWEEPS + rows - sweep - 1):
            center = state_ref[now, x]
            beside = (
                coef_ref[x, 1] * state_ref[now, x - 1]
                + coef_ref[x, 2] * state_ref[now, x + 1]
                + coef_ref[x, 3] * pltpu.roll(center, 1, 0)
                + coef_ref[x, 4] * pltpu.roll(center, wide - 1, 0)
            )
            new = coef_ref[x, 0] * center - beside
            if sweep < SWEEPS - 1:
                state_ref[later, x] = new
            else:
                prior_ref[x - SWEEPS] = PRIOR_WEIGHT * new[:cols]
    out.wait()


def finish(pair_ref, far_ref, prior_ref, low0_ref, low3_ref, low2_ref, low1_ref, out, held_ref, sems):
    rows, cols, real = held_ref.shape
    beside = pair_ref.shape[0] // 2
    side = rows // beside
    low = jnp.concatenate([low0_ref[...], low1_ref[...], low2_ref[...], low3_ref[...]], axis=0)
    copies = []
    for x in range(beside):
        kernel = jnp.concatenate(
            [pair_ref[x], pair_ref[beside + x], far_ref[x], far_ref[beside + x]], axis=0
        )
        grad = lax.dot_general(
            kernel, low, (((0,), (0,)), ((), ())), preferred_element_type=jnp.float32
        )
        for k in range(side):
            row = k * beside + x
            held_ref[row] = grad[k * cols : (k + 1) * cols] + prior_ref[row]
            copies.append(pltpu.make_async_copy(held_ref.at[row], out.at[row], sems.at[row]))
            copies[-1].start()
    for copy in copies:
        copy.wait()


def local(observed, noise_scale, forward_kernel, model_field, classes, kappa_table, coupling_table):
    rows, cols, real = model_field.shape
    comps, sensors = forward_kernel.shape[3:]
    own = observed.shape[1]
    points = comps * sensors
    kernel_own = forward_kernel[0].transpose(0, 2, 3, 1).reshape(rows, points, cols)
    beside = rows // max(1, min(rows, LANES // cols))
    side = rows // beside
    assert sensors <= TILE * real and cols + 2 * SWEEPS <= LANES
    assert rows >= SWEEPS and (cols + 2 * SWEEPS + TILE) % 16 == 0
    rim_rows = rows * (SWEEPS + 1)
    wide_py, wide_px = lax.axis_size("py") > 2, lax.axis_size("px") > 2
    payload, kernel_own, model_field, marks, table, *far_rim = call(
        prepare,
        ((points + TILE + rim_rows, real), jnp.float32),
        ((beside, points, side * cols), jnp.bfloat16),
        (model_field.shape, jnp.float32),
        ((rows, LANES), jnp.float32),
        ((1 + coupling_table.shape[0], coupling_table.shape[1]), jnp.float32),
        *[((rim_rows, real), jnp.float32)] * wide_py,
        fetch=True,
    )(
        noise_scale,
        observed[0],
        kernel_own,
        model_field,
        classes,
        kappa_table[None],
        coupling_table,
    )
    got = swap(payload, "py", near)
    kernel_next = swap(kernel_own, "freq", near)
    two = [swap(rim, "py", far("py")) for rim in far_rim]
    summed = ((points + TILE, real), jnp.float32)
    step = cols + 2 * SWEEPS + TILE
    peers, freqs = lax.axis_size("px"), lax.axis_size("freq")
    side_shapes = (
        ((rows, 2 * SWEEPS, real), jnp.float32),
        ((rows, LANES), jnp.float32),
    )
    pair_shape = ((2 * beside, points, side * cols), jnp.bfloat16)

    def by_parity(own, even_partner, odd_partner):
        return lax.ppermute(
            own,
            ("freq", "px"),
            [
                (f * peers + i, f * peers + (odd_partner if f % 2 else even_partner)(i))
                for f in range(freqs)
                for i in range(peers)
            ],
        )

    if peers == 4 and lax.axis_size("py") == 2:
        part = packed_rows(points + TILE)
        total, side_rim, wide_marks, mixed = call(
            spread,
            summed,
            *side_shapes,
            ((3 * part + SWEEPS * step, real), jnp.bfloat16),
        )(payload, got, model_field, marks)
        mixed = by_parity(mixed, near, far("px"))
        cross = by_parity(total, far("px"), near)
        skip = swap(total, "px", lambda i: i ^ 2)
        (kernel_pair,) = call(join, pair_shape, flops=JOIN_FLOPS)(kernel_own, kernel_next, total)
        sums = (total, cross, skip, mixed)
        rim_rows, sent_rows = mixed, mixed[3 * part :]
    else:
        (total,) = call(add, summed)(payload, got)
        for bit in bits("py")[1:]:
            (total,) = call(add, summed)(total, swap(total, "py", lambda i: i ^ bit))
        side_rim, wide_marks, rim_rows = call(
            edge, *side_shapes, ((SWEEPS * step, real), jnp.bfloat16), flops=EDGE_FLOPS
        )(total, got, model_field, marks, *two)
        rim_rows = sent_rows = by_parity(rim_rows, near, far("px") if wide_px else near)
        *steps, last = bits("px")
        for bit in steps[:-1]:
            (total,) = call(add, summed)(total, swap(total, "px", lambda i: i ^ bit))
        total, kernel_pair = call(add_and_join, summed, pair_shape, flops=ORDER_FLOPS)(
            total, swap(total, "px", lambda i: i ^ steps[-1]), kernel_own, kernel_next
        )
        sums = (total, swap(total, "px", lambda i: i ^ last))
    kernel_far = swap(kernel_pair, "freq", lambda i: i ^ 2)
    assert freqs == 4
    weighted_low, weighted = call(
        weigh,
        ((points, real), jnp.bfloat16),
        ((comps, sensors, real), jnp.float32),
        flops=ORDER_FLOPS,
    )(*sums)
    other_rows = swap(sent_rows, "freq", near)
    low_one = swap(weighted_low, "freq", near)
    low_three = swap(weighted_low, "freq", lambda i: i ^ 3)
    low_two = swap(weighted_low, "freq", lambda i: i ^ 2)
    wide = cols + 2 * SWEEPS
    prior_term, weighted_own = call(
        prior,
        (model_field.shape, jnp.float32),
        ((own, comps, real), jnp.float32),
        stored=(1,),
        scratch=(
            pltpu.VMEM((2, rows + 2 * SWEEPS, wide, real), jnp.float32),
            pltpu.VMEM((rows + 2 * SWEEPS, table.shape[0], wide, real), jnp.float32),
            pltpu.VMEM((own, comps, real), jnp.float32),
            pltpu.SemaphoreType.DMA(()),
        ),
        flops=PRIOR_FLOPS,
    )(model_field, side_rim, wide_marks, rim_rows, other_rows, table, weighted)
    (gradient,) = call(
        finish,
        (model_field.shape, jnp.float32),
        stored=(0,),
        scratch=(
            pltpu.VMEM(model_field.shape, jnp.float32),
            pltpu.SemaphoreType.DMA((rows,)),
        ),
    )(kernel_pair, kernel_far, prior_term, weighted_low, low_three, low_two, low_one)
    return weighted_own[None], gradient


def solution(mesh):
    in_specs = (
        P("freq", ("px", "py"), None, None),
        P("freq", ("px", "py")),
        P("freq", "px", "py", None, None),
        P("px", "py", None),
        P("px", "py"),
        P(),
        P(),
    )
    out_specs = (P("freq", ("px", "py"), None, None), P("px", "py", None))
    return jax.shard_map(local, mesh=mesh, in_specs=in_specs, out_specs=out_specs, check_vma=False)
```

```python
import jax
import jax.numpy as jnp
from jax import lax
from jax.experimental import pallas as pl
from jax.experimental.pallas import tpu as pltpu
from jax.sharding import PartitionSpec as P

SWEEPS = 4
FREEDOM = 4.0
PRIOR_WEIGHT = 0.04
LANES = 128
TILE = 8
VMEM_BYTES = 40 << 20
PRIOR_FLOPS = 1 << 30
EDGE_FLOPS = 1 << 30
JOIN_FLOPS = 1 << 30
PARTS = 2
ORDER_FLOPS = 1 << 32


def swap(own, axis, partner):
    return lax.ppermute(own, axis, [(i, partner(i)) for i in range(lax.axis_size(axis))])


def bits(axis):
    size = lax.axis_size(axis)
    assert size & (size - 1) == 0
    return [1 << k for k in range(size.bit_length() - 1)]


def near(i):
    return i ^ 1


def far(axis):
    return lambda i: (((i + 1) ^ 1) - 1) % lax.axis_size(axis)


def call(body, *out_shapes, fetch=False, scratch=(), stored=(), flops=0):
    def run(*operands):
        count = len(operands)
        if fetch:
            operands = [pltpu.with_memory_space_constraint(x, pltpu.HBM) for x in operands]

        def fetched(*refs):
            outs, held, sems = (
                refs[count : count + len(out_shapes)],
                refs[count + len(out_shapes) : -1],
                refs[-1],
            )
            copies = [
                pltpu.make_async_copy(src, dst, sems.at[k])
                for k, (src, dst) in enumerate(zip(refs[:count], held))
            ]
            for copy in copies:
                copy.start()
            for copy in copies:
                copy.wait()
            body(*held, *outs)

        return pl.pallas_call(
            fetched if fetch else body,
            out_shape=[jax.ShapeDtypeStruct(shape, dtype) for shape, dtype in out_shapes],
            in_specs=[pl.BlockSpec(memory_space=pltpu.HBM if fetch else pltpu.VMEM)] * count,
            out_specs=[
                pl.BlockSpec(memory_space=pltpu.HBM if k in stored else pltpu.VMEM)
                for k in range(len(out_shapes))
            ],
            scratch_shapes=list(scratch)
            + [pltpu.VMEM(x.shape, x.dtype) for x in operands] * fetch
            + [pltpu.SemaphoreType.DMA((count,))] * fetch,
            compiler_params=pltpu.CompilerParams(vmem_limit_bytes=VMEM_BYTES),
            cost_estimate=pl.CostEstimate(flops=flops, bytes_accessed=0, transcendentals=0),
        )(*operands)

    return run


def prepare(
    noise_ref,
    observed_ref,
    kernel_ref,
    field_ref,
    classes_ref,
    kappa_ref,
    coupling_ref,
    pay_ref,
    packed_ref,
    held_ref,
    marks_ref,
    table_ref,
    *far_ref,
):
    beside, points, width = packed_ref.shape
    rows, cols, real = field_ref.shape
    own, comps = observed_ref.shape[:2]
    sensors = points // comps
    place = lax.axis_index("px") * lax.axis_size("py") + lax.axis_index("py")
    even = lax.axis_index("py") % 2 == 0
    packed, field = [], []
    for x in range(beside):
        picks = range(x, rows, beside)
        packed.append(jnp.concatenate([kernel_ref[k] for k in picks], axis=1))
        packed_ref[x] = packed[-1]
        field += [field_ref[k].astype(jnp.bfloat16) for k in picks]
    total = jnp.dot(
        jnp.concatenate(packed, axis=1),
        jnp.concatenate(field, axis=0),
        preferred_element_type=jnp.float32,
    )
    spot = lax.broadcasted_iota(jnp.int32, (points, real), 0)
    for c in range(comps):
        for k in range(own):
            row = c * sensors + place * own + k
            total = total - jnp.where(spot == row, observed_ref[k, c : c + 1, :], 0.0)
    pay_ref[:points] = total
    spot = lax.broadcasted_iota(jnp.int32, (TILE, real), 0) * real + lax.broadcasted_iota(
        jnp.int32, (TILE, real), 1
    )
    noise = jnp.zeros((TILE, real), jnp.float32)
    for k in range(own):
        noise = noise + jnp.where(spot == place * own + k, noise_ref[0:1, k : k + 1], 0.0)
    pay_ref[points : points + TILE] = noise
    held_ref[...] = field_ref[...]
    coupling = coupling_ref[...]
    table_ref[0:1] = kappa_ref[...] + jnp.sum(coupling, axis=0, keepdims=True)
    table_ref[1:] = coupling
    marks = (classes_ref[...] + 1).astype(jnp.float32)
    marks_ref[...] = jnp.zeros_like(marks_ref)
    marks_ref[:, :cols] = marks
    edges = [
        (field_ref[:, cols - SWEEPS :, :], marks[:, cols - SWEEPS :]),
        (field_ref[:, :SWEEPS, :], marks[:, :SWEEPS]),
    ]

    def put(ref, start, chosen):
        for x in range(rows):
            ref[start + x * SWEEPS : start + (x + 1) * SWEEPS] = jnp.where(
                chosen, edges[0][0][x], edges[1][0][x]
            )
        start = start + rows * SWEEPS
        ref[start : start + rows] = jnp.zeros((rows, real), jnp.float32)
        ref[start : start + rows, :SWEEPS] = jnp.where(chosen, edges[0][1], edges[1][1])

    put(pay_ref, points + TILE, even)
    for ref in far_ref:
        put(ref, 0, jnp.logical_not(even))


def sides_of(one, two, axis):
    me = lax.axis_index(axis)
    even = me % 2 == 0
    before = jnp.where(me == 0, 0.0, jnp.where(even, two, one))
    after = jnp.where(me == lax.axis_size(axis) - 1, 0.0, jnp.where(even, one, two))
    return before, after


def add(mine_ref, got_ref, out_ref):
    size = out_ref.shape[0]
    out_ref[...] = mine_ref[:size] + got_ref[:size]


def add_and_join(mine_ref, got_ref, one_ref, two_ref, out_ref, joined_ref):
    out_ref[...] = mine_ref[...] + got_ref[...]
    half = one_ref.shape[0]
    joined_ref[:half] = one_ref[...]
    joined_ref[half:] = two_ref[...]


def lay(got_ref, field_ref, marks_ref, far_ref, side_ref, wide_ref, rows_ref, base):
    rows, cols, real = field_ref.shape
    one = got_ref[got_ref.shape[0] - rows * (SWEEPS + 1) :]
    before, after = sides_of(one, far_ref[0][...] if far_ref else one, "py")
    fields = rows * SWEEPS
    wide_ref[...] = (
        marks_ref[...]
        + pltpu.roll(after[fields:], cols, 1)
        + pltpu.roll(before[fields:], cols + SWEEPS, 1)
    )
    for x in range(rows):
        pick = slice(x * SWEEPS, (x + 1) * SWEEPS)
        side_ref[x] = jnp.concatenate([after[pick], before[pick]], axis=0)
    chosen = lax.axis_index("px") % 2 == 0
    if lax.axis_size("px") > 2:
        chosen = chosen == (lax.axis_index("freq") % 2 == 0)
    spot = lax.broadcasted_iota(jnp.int32, (2 * TILE, real), 0)
    blocks, tile = [], jnp.zeros((2 * TILE, real), jnp.float32)
    for k in range(SWEEPS):
        last = rows - SWEEPS + k
        blocks.append(jnp.where(chosen, field_ref[last], field_ref[k]))
        blocks.append(jnp.where(chosen, side_ref[last], side_ref[k]))
        marks = jnp.where(chosen, wide_ref[last : last + 1], wide_ref[k : k + 1])
        tile = jnp.where(spot == k, marks, tile)
    rows_ref[base:] = jnp.concatenate(blocks + [tile], axis=0).astype(jnp.bfloat16)


def edge(after_ref, got_ref, field_ref, marks_ref, *refs):
    *far_ref, side_ref, wide_ref, rows_ref = refs
    lay(got_ref, field_ref, marks_ref, far_ref, side_ref, wide_ref, rows_ref, 0)


def packed_rows(size):
    return -(-size // 16) * 16


def spread(mine_ref, got_ref, field_ref, marks_ref, *refs):
    *far_ref, out_ref, side_ref, wide_ref, mixed_ref = refs
    size, real = out_ref.shape
    total = mine_ref[:size] + got_ref[:size]
    out_ref[...] = total
    part = packed_rows(size)
    rest = total
    if part > size:
        rest = jnp.concatenate([total, jnp.zeros((part - size, real), jnp.float32)], axis=0)
    for k in range(PARTS):
        low = rest.astype(jnp.bfloat16)
        mixed_ref[k * part : (k + 1) * part] = low
        rest = rest - low.astype(jnp.float32)
    lay(got_ref, field_ref, marks_ref, far_ref, side_ref, wide_ref, mixed_ref, PARTS * part)


def join(one_ref, two_ref, after_ref, out_ref):
    half = one_ref.shape[0]
    out_ref[:half] = one_ref[...]
    out_ref[half:] = two_ref[...]


def weigh(*refs):
    mine_ref, *got_refs, low_ref, weighted_ref = refs
    comps, sensors, real = weighted_ref.shape
    points = comps * sensors
    total = mine_ref[...]
    size = total.shape[0]
    for got_ref in got_refs:
        if got_ref.dtype == jnp.bfloat16:
            part = packed_rows(size)
            parts = [got_ref[k * part : (k + 1) * part].astype(jnp.float32) for k in range(PARTS)]
            total = total + sum(parts)[:size]
        else:
            total = total + got_ref[...]
    chunk = min(sensors, real)
    eye = lax.broadcasted_iota(jnp.int32, (chunk, real), 0) == lax.broadcasted_iota(
        jnp.int32, (chunk, real), 1
    )
    for k in range(sensors // chunk):
        row = total[points + k : points + k + 1]
        noise = jnp.sum(jnp.where(eye, row, 0.0), axis=1, keepdims=True)
        inverse = 1.0 / (noise * noise)
        misfit = [total[c * sensors + k * chunk : c * sensors + (k + 1) * chunk] for c in range(comps)]
        spread = sum(part * part for part in misfit) * inverse
        factor = (FREEDOM + 2.0) / (FREEDOM + spread) * inverse
        for c in range(comps):
            weighted = misfit[c] * factor
            weighted_ref[c, k * chunk : (k + 1) * chunk] = weighted
            low_ref[c * sensors + k * chunk : c * sensors + (k + 1) * chunk] = weighted.astype(
                jnp.bfloat16
            )


def prior(
    field_ref,
    side_ref,
    wide_ref,
    rows_ref,
    other_ref,
    table_ref,
    weighted_ref,
    prior_ref,
    own_out,
    state_ref,
    coef_ref,
    own_ref,
    sem,
):
    own, comps, real = own_ref.shape
    sensors = weighted_ref.shape[1]
    place = lax.axis_index("px") * lax.axis_size("py") + lax.axis_index("py")
    spot = lax.broadcasted_iota(jnp.int32, (sensors, real), 0)
    for c in range(comps):
        for k in range(own):
            own_ref[k, c : c + 1] = jnp.sum(
                jnp.where(spot == place * own + k, weighted_ref[c], 0.0), axis=0, keepdims=True
            )
    out = pltpu.make_async_copy(own_ref, own_out, sem)
    out.start()
    rows, cols, _ = field_ref.shape
    wide = cols + 2 * SWEEPS
    tile = SWEEPS * wide
    mine = rows_ref[rows_ref.shape[0] - other_ref.shape[0] :].astype(jnp.float32)
    other = other_ref[...].astype(jnp.float32)
    even = lax.axis_index("freq") % 2 == 0
    before, after = sides_of(
        jnp.where(even, mine, other), jnp.where(even, other, mine), "px"
    )
    for k in range(SWEEPS):
        state_ref[0, k] = before[k * wide : (k + 1) * wide]
        state_ref[0, SWEEPS + rows + k] = after[k * wide : (k + 1) * wide]
    for x in range(rows):
        state_ref[0, SWEEPS + x] = jnp.concatenate([field_ref[x], side_ref[x]], axis=0)
    marks = (
        [before[tile + k : tile + k + 1] for k in range(SWEEPS)]
        + [wide_ref[x : x + 1] for x in range(rows)]
        + [after[tile + k : tile + k + 1] for k in range(SWEEPS)]
    )
    count, levels = table_ref.shape
    spread = (
        lax.broadcasted_iota(jnp.int32, (count, count * real), 1) // real
        == lax.broadcasted_iota(jnp.int32, (count, count * real), 0)
    ).astype(jnp.float32)
    turn = (((0,), (0,)), ((), ()))
    table = lax.dot_general(
        table_ref[...],
        spread,
        turn,
        precision=lax.Precision.HIGHEST,
        preferred_element_type=jnp.float32,
    )
    high = table.astype(jnp.bfloat16)
    rest = table - high.astype(jnp.float32)
    middle = rest.astype(jnp.bfloat16)
    low = (rest - middle.astype(jnp.float32)).astype(jnp.bfloat16)
    table = jnp.concatenate([high, middle, low], axis=0)
    level = lax.broadcasted_iota(jnp.int32, (levels, real), 0).astype(jnp.float32) + 1.0
    for x in range(1, 2 * SWEEPS + rows - 1):
        onehot = (level == marks[x]).astype(jnp.float32).astype(jnp.bfloat16)
        onehot = jnp.concatenate([onehot] * 3, axis=0)[:, :wide]
        coef = lax.dot_general(onehot, table, turn, preferred_element_type=jnp.float32)
        for c in range(count):
            coef_ref[x, c] = coef[:, c * real : (c + 1) * real]
    for sweep in range(SWEEPS):
        now, later = sweep % 2, (sweep + 1) % 2
        for x in range(sweep + 1, 2 * SWEEPS + rows - sweep - 1):
            center = state_ref[now, x]
            beside = (
                coef_ref[x, 1] * state_ref[now, x - 1]
                + coef_ref[x, 2] * state_ref[now, x + 1]
                + coef_ref[x, 3] * pltpu.roll(center, 1, 0)
                + coef_ref[x, 4] * pltpu.roll(center, wide - 1, 0)
            )
            new = coef_ref[x, 0] * center - beside
            if sweep < SWEEPS - 1:
                state_ref[later, x] = new
            else:
                prior_ref[x - SWEEPS] = PRIOR_WEIGHT * new[:cols]
    out.wait()


def finish(pair_ref, far_ref, prior_ref, low0_ref, low3_ref, low2_ref, low1_ref, out, held_ref, sems):
    rows, cols, real = held_ref.shape
    beside = pair_ref.shape[0] // 2
    side = rows // beside
    low = jnp.concatenate([low0_ref[...], low1_ref[...], low2_ref[...], low3_ref[...]], axis=0)
    copies = []
    for x in range(beside):
        kernel = jnp.concatenate(
            [pair_ref[x], pair_ref[beside + x], far_ref[x], far_ref[beside + x]], axis=0
        )
        grad = lax.dot_general(
            kernel, low, (((0,), (0,)), ((), ())), preferred_element_type=jnp.float32
        )
        for k in range(side):
            row = k * beside + x
            held_ref[row] = grad[k * cols : (k + 1) * cols] + prior_ref[row]
            copies.append(pltpu.make_async_copy(held_ref.at[row], out.at[row], sems.at[row]))
            copies[-1].start()
    for copy in copies:
        copy.wait()


def local(observed, noise_scale, forward_kernel, model_field, classes, kappa_table, coupling_table):
    rows, cols, real = model_field.shape
    comps, sensors = forward_kernel.shape[3:]
    own = observed.shape[1]
    points = comps * sensors
    kernel_own = forward_kernel[0].transpose(0, 2, 3, 1).reshape(rows, points, cols)
    beside = rows // max(1, min(rows, LANES // cols))
    side = rows // beside
    assert sensors <= TILE * real and cols + 2 * SWEEPS <= LANES
    assert rows >= SWEEPS and cols % TILE == 0
    rim_rows = rows * (SWEEPS + 1)
    wide_py, wide_px = lax.axis_size("py") > 2, lax.axis_size("px") > 2
    payload, kernel_own, model_field, marks, table, *far_rim = call(
        prepare,
        ((points + TILE + rim_rows, real), jnp.float32),
        ((beside, points, side * cols), jnp.bfloat16),
        (model_field.shape, jnp.float32),
        ((rows, LANES), jnp.float32),
        ((1 + coupling_table.shape[0], coupling_table.shape[1]), jnp.float32),
        *[((rim_rows, real), jnp.float32)] * wide_py,
        fetch=True,
    )(
        noise_scale,
        observed[0],
        kernel_own,
        model_field,
        classes,
        kappa_table[None],
        coupling_table,
    )
    got = swap(payload, "py", near)
    kernel_next = swap(kernel_own, "freq", near)
    two = [swap(rim, "py", far("py")) for rim in far_rim]
    summed = ((points + TILE, real), jnp.float32)
    rim_size = SWEEPS * (cols + 2 * SWEEPS) + 2 * TILE
    peers, freqs = lax.axis_size("px"), lax.axis_size("freq")
    side_shapes = (
        ((rows, 2 * SWEEPS, real), jnp.float32),
        ((rows, LANES), jnp.float32),
    )
    pair_shape = ((2 * beside, points, side * cols), jnp.bfloat16)

    def by_parity(own, even_partner, odd_partner):
        return lax.ppermute(
            own,
            ("freq", "px"),
            [
                (f * peers + i, f * peers + (odd_partner if f % 2 else even_partner)(i))
                for f in range(freqs)
                for i in range(peers)
            ],
        )

    if peers == 4 and lax.axis_size("py") == 2:
        part = packed_rows(points + TILE)
        total, side_rim, wide_marks, mixed = call(
            spread,
            summed,
            *side_shapes,
            ((PARTS * part + rim_size, real), jnp.bfloat16),
        )(payload, got, model_field, marks)
        mixed = by_parity(mixed, near, far("px"))
        cross = by_parity(total, far("px"), near)
        skip = swap(total, "px", lambda i: i ^ 2)
        (kernel_pair,) = call(join, pair_shape, flops=JOIN_FLOPS)(kernel_own, kernel_next, total)
        sums = (total, cross, skip, mixed)
        rim_rows, sent_rows = mixed, mixed[PARTS * part :]
    else:
        (total,) = call(add, summed)(payload, got)
        for bit in bits("py")[1:]:
            (total,) = call(add, summed)(total, swap(total, "py", lambda i: i ^ bit))
        side_rim, wide_marks, rim_rows = call(
            edge, *side_shapes, ((rim_size, real), jnp.bfloat16), flops=EDGE_FLOPS
        )(total, got, model_field, marks, *two)
        rim_rows = sent_rows = by_parity(rim_rows, near, far("px") if wide_px else near)
        *steps, last = bits("px")
        for bit in steps[:-1]:
            (total,) = call(add, summed)(total, swap(total, "px", lambda i: i ^ bit))
        total, kernel_pair = call(add_and_join, summed, pair_shape, flops=ORDER_FLOPS)(
            total, swap(total, "px", lambda i: i ^ steps[-1]), kernel_own, kernel_next
        )
        sums = (total, swap(total, "px", lambda i: i ^ last))
    kernel_far = swap(kernel_pair, "freq", lambda i: i ^ 2)
    assert freqs == 4
    weighted_low, weighted = call(
        weigh,
        ((points, real), jnp.bfloat16),
        ((comps, sensors, real), jnp.float32),
        flops=ORDER_FLOPS,
    )(*sums)
    other_rows = swap(sent_rows, "freq", near)
    low_one = swap(weighted_low, "freq", near)
    low_three = swap(weighted_low, "freq", lambda i: i ^ 3)
    low_two = swap(weighted_low, "freq", lambda i: i ^ 2)
    wide = cols + 2 * SWEEPS
    prior_term, weighted_own = call(
        prior,
        (model_field.shape, jnp.float32),
        ((own, comps, real), jnp.float32),
        stored=(1,),
        scratch=(
            pltpu.VMEM((2, rows + 2 * SWEEPS, wide, real), jnp.float32),
            pltpu.VMEM((rows + 2 * SWEEPS, table.shape[0], wide, real), jnp.float32),
            pltpu.VMEM((own, comps, real), jnp.float32),
            pltpu.SemaphoreType.DMA(()),
        ),
        flops=PRIOR_FLOPS,
    )(model_field, side_rim, wide_marks, rim_rows, other_rows, table, weighted)
    (gradient,) = call(
        finish,
        (model_field.shape, jnp.float32),
        stored=(0,),
        scratch=(
            pltpu.VMEM(model_field.shape, jnp.float32),
            pltpu.SemaphoreType.DMA((rows,)),
        ),
    )(kernel_pair, kernel_far, prior_term, weighted_low, low_three, low_two, low_one)
    return weighted_own[None], gradient


def solution(mesh):
    in_specs = (
        P("freq", ("px", "py"), None, None),
        P("freq", ("px", "py")),
        P("freq", "px", "py", None, None),
        P("px", "py", None),
        P("px", "py"),
        P(),
        P(),
    )
    out_specs = (P("freq", ("px", "py"), None, None), P("px", "py", None))
    return jax.shard_map(local, mesh=mesh, in_specs=in_specs, out_specs=out_specs, check_vma=False)
```

```python
import jax
import jax.numpy as jnp
from jax import lax
from jax.experimental import pallas as pl
from jax.experimental.pallas import tpu as pltpu
from jax.sharding import PartitionSpec as P

SWEEPS = 4
FREEDOM = 4.0
PRIOR_WEIGHT = 0.04
LANES = 128
TILE = 8
VMEM_BYTES = 40 << 20
PRIOR_FLOPS = 1 << 30
EDGE_FLOPS = 1 << 30
JOIN_FLOPS = 1 << 30
ORDER_FLOPS = 1 << 32


def swap(own, axis, partner):
    return lax.ppermute(own, axis, [(i, partner(i)) for i in range(lax.axis_size(axis))])


def bits(axis):
    size = lax.axis_size(axis)
    assert size & (size - 1) == 0
    return [1 << k for k in range(size.bit_length() - 1)]


def near(i):
    return i ^ 1


def far(axis):
    return lambda i: (((i + 1) ^ 1) - 1) % lax.axis_size(axis)


def call(body, *out_shapes, fetch=False, keep=(), scratch=(), stored=(), flops=0):
    def run(*operands):
        count, kept = len(operands), dict(keep)
        if fetch:
            operands = [pltpu.with_memory_space_constraint(x, pltpu.HBM) for x in operands]

        def fetched(*refs):
            outs = refs[count : count + len(out_shapes)]
            room, sems = iter(refs[count + len(out_shapes) : -1]), refs[-1]
            held = [outs[kept[k]] if k in kept else next(room) for k in range(count)]
            copies = [
                pltpu.make_async_copy(src, dst, sems.at[k])
                for k, (src, dst) in enumerate(zip(refs[:count], held))
            ]
            for k in sorted(range(count), key=lambda k: -operands[k].size):
                copies[k].start()
            for copy in copies:
                copy.wait()
            body(*held, *outs)

        return pl.pallas_call(
            fetched if fetch else body,
            out_shape=[jax.ShapeDtypeStruct(shape, dtype) for shape, dtype in out_shapes],
            in_specs=[pl.BlockSpec(memory_space=pltpu.HBM if fetch else pltpu.VMEM)] * count,
            out_specs=[
                pl.BlockSpec(memory_space=pltpu.HBM if k in stored else pltpu.VMEM)
                for k in range(len(out_shapes))
            ],
            scratch_shapes=list(scratch)
            + [pltpu.VMEM(x.shape, x.dtype) for k, x in enumerate(operands) if k not in kept] * fetch
            + [pltpu.SemaphoreType.DMA((count,))] * fetch,
            compiler_params=pltpu.CompilerParams(vmem_limit_bytes=VMEM_BYTES),
            cost_estimate=pl.CostEstimate(flops=flops, bytes_accessed=0, transcendentals=0),
        )(*operands)

    return run


def prepare(
    noise_ref,
    observed_ref,
    kernel_ref,
    field_ref,
    classes_ref,
    kappa_ref,
    coupling_ref,
    pay_ref,
    packed_ref,
    _,
    marks_ref,
    table_ref,
    *far_ref,
):
    beside, points, width = packed_ref.shape
    rows, cols, real = field_ref.shape
    own, comps = observed_ref.shape[:2]
    sensors = points // comps
    place = lax.axis_index("px") * lax.axis_size("py") + lax.axis_index("py")
    even = lax.axis_index("py") % 2 == 0
    packed, field = [], []
    for x in range(beside):
        picks = range(x, rows, beside)
        packed.append(jnp.concatenate([kernel_ref[k] for k in picks], axis=1))
        packed_ref[x] = packed[-1]
        field += [field_ref[k].astype(jnp.bfloat16) for k in picks]
    total = jnp.dot(
        jnp.concatenate(packed, axis=1),
        jnp.concatenate(field, axis=0),
        preferred_element_type=jnp.float32,
    )
    spot = lax.broadcasted_iota(jnp.int32, (points, real), 0)
    for c in range(comps):
        for k in range(own):
            row = c * sensors + place * own + k
            total = total - jnp.where(spot == row, observed_ref[k, c : c + 1, :], 0.0)
    pay_ref[:points] = total
    spot = lax.broadcasted_iota(jnp.int32, (TILE, real), 0) * real + lax.broadcasted_iota(
        jnp.int32, (TILE, real), 1
    )
    noise = jnp.zeros((TILE, real), jnp.float32)
    for k in range(own):
        noise = noise + jnp.where(spot == place * own + k, noise_ref[0:1, k : k + 1], 0.0)
    pay_ref[points : points + TILE] = noise
    coupling = coupling_ref[...]
    table_ref[0:1] = kappa_ref[...] + jnp.sum(coupling, axis=0, keepdims=True)
    table_ref[1:] = coupling
    marks = (classes_ref[...] + 1).astype(jnp.float32)
    marks_ref[...] = jnp.zeros_like(marks_ref)
    marks_ref[:, :cols] = marks
    edges = [
        (field_ref[:, cols - SWEEPS :, :], marks[:, cols - SWEEPS :]),
        (field_ref[:, :SWEEPS, :], marks[:, :SWEEPS]),
    ]

    def put(ref, start, chosen):
        for x in range(rows):
            ref[start + x * SWEEPS : start + (x + 1) * SWEEPS] = jnp.where(
                chosen, edges[0][0][x], edges[1][0][x]
            )
        start = start + rows * SWEEPS
        ref[start : start + rows] = jnp.zeros((rows, real), jnp.float32)
        ref[start : start + rows, :SWEEPS] = jnp.where(chosen, edges[0][1], edges[1][1])

    put(pay_ref, points + TILE, even)
    for ref in far_ref:
        put(ref, 0, jnp.logical_not(even))


def sides_of(one, two, axis):
    me = lax.axis_index(axis)
    even = me % 2 == 0
    before = jnp.where(me == 0, 0.0, jnp.where(even, two, one))
    after = jnp.where(me == lax.axis_size(axis) - 1, 0.0, jnp.where(even, one, two))
    return before, after


def add(mine_ref, got_ref, out_ref):
    size = out_ref.shape[0]
    out_ref[...] = mine_ref[:size] + got_ref[:size]


def add_and_join(mine_ref, got_ref, one_ref, two_ref, out_ref, joined_ref):
    out_ref[...] = mine_ref[...] + got_ref[...]
    half = one_ref.shape[0]
    joined_ref[:half] = one_ref[...]
    joined_ref[half:] = two_ref[...]


def lay(got_ref, field_ref, marks_ref, far_ref, side_ref, wide_ref, rows_ref, base):
    rows, cols, real = field_ref.shape
    one = got_ref[got_ref.shape[0] - rows * (SWEEPS + 1) :]
    before, after = sides_of(one, far_ref[0][...] if far_ref else one, "py")
    fields = rows * SWEEPS
    wide_ref[...] = (
        marks_ref[...]
        + pltpu.roll(after[fields:], cols, 1)
        + pltpu.roll(before[fields:], cols + SWEEPS, 1)
    )
    for x in range(rows):
        pick = slice(x * SWEEPS, (x + 1) * SWEEPS)
        side_ref[x] = jnp.concatenate([after[pick], before[pick]], axis=0)
    chosen = lax.axis_index("px") % 2 == 0
    if lax.axis_size("px") > 2:
        chosen = chosen == (lax.axis_index("freq") % 2 == 0)
    spot = lax.broadcasted_iota(jnp.int32, (2 * TILE, real), 0)
    blocks, tile = [], jnp.zeros((2 * TILE, real), jnp.float32)
    for k in range(SWEEPS):
        last = rows - SWEEPS + k
        blocks.append(jnp.where(chosen, field_ref[last], field_ref[k]))
        blocks.append(jnp.where(chosen, side_ref[last], side_ref[k]))
        marks = jnp.where(chosen, wide_ref[last : last + 1], wide_ref[k : k + 1])
        tile = jnp.where(spot == k, marks, tile)
    rows_ref[base:] = jnp.concatenate(blocks + [tile], axis=0).astype(jnp.bfloat16)


def edge(after_ref, got_ref, field_ref, marks_ref, *refs):
    *far_ref, side_ref, wide_ref, rows_ref = refs
    lay(got_ref, field_ref, marks_ref, far_ref, side_ref, wide_ref, rows_ref, 0)


def spread(mine_ref, got_ref, field_ref, marks_ref, *refs):
    *far_ref, out_ref, side_ref, wide_ref, mixed_ref = refs
    size, real = out_ref.shape
    total = mine_ref[:size] + got_ref[:size]
    out_ref[...] = total
    points = size - TILE
    high = total.astype(jnp.bfloat16).astype(jnp.float32)
    low = total - high
    mixed_ref[: 2 * size] = jnp.concatenate(
        [high[:points], low[:points], high[points:], low[points:]], axis=0
    ).astype(jnp.bfloat16)
    lay(got_ref, field_ref, marks_ref, far_ref, side_ref, wide_ref, mixed_ref, 2 * size)


def join(one_ref, two_ref, after_ref, out_ref):
    half = one_ref.shape[0]
    out_ref[:half] = one_ref[...]
    out_ref[half:] = two_ref[...]


def weigh(*refs):
    mine_ref, *got_refs, low_ref, weighted_ref = refs
    comps, sensors, real = weighted_ref.shape
    points = comps * sensors
    total = mine_ref[...]
    size = total.shape[0]
    for got_ref in got_refs:
        if got_ref.dtype == jnp.bfloat16:
            parts = got_ref[: 2 * size].astype(jnp.float32)
            sums = parts[:points] + parts[points : 2 * points]
            noises = parts[2 * points : 2 * points + TILE] + parts[2 * points + TILE :]
            total = total + jnp.concatenate([sums, noises], axis=0)
        else:
            total = total + got_ref[...]
    chunk = min(sensors, real)
    eye = lax.broadcasted_iota(jnp.int32, (chunk, real), 0) == lax.broadcasted_iota(
        jnp.int32, (chunk, real), 1
    )
    for k in range(sensors // chunk):
        row = total[points + k : points + k + 1]
        noise = jnp.sum(jnp.where(eye, row, 0.0), axis=1, keepdims=True)
        inverse = 1.0 / (noise * noise)
        misfit = [total[c * sensors + k * chunk : c * sensors + (k + 1) * chunk] for c in range(comps)]
        spread = sum(part * part for part in misfit) * inverse
        factor = (FREEDOM + 2.0) / (FREEDOM + spread) * inverse
        for c in range(comps):
            weighted = misfit[c] * factor
            weighted_ref[c, k * chunk : (k + 1) * chunk] = weighted
            low_ref[c * sensors + k * chunk : c * sensors + (k + 1) * chunk] = weighted.astype(
                jnp.bfloat16
            )


def prior(
    field_ref,
    side_ref,
    wide_ref,
    rows_ref,
    other_ref,
    table_ref,
    weighted_ref,
    prior_ref,
    own_out,
    state_ref,
    coef_ref,
    own_ref,
    sem,
):
    own, comps, real = own_ref.shape
    sensors = weighted_ref.shape[1]
    place = lax.axis_index("px") * lax.axis_size("py") + lax.axis_index("py")
    spot = lax.broadcasted_iota(jnp.int32, (sensors, real), 0)
    for c in range(comps):
        for k in range(own):
            own_ref[k, c : c + 1] = jnp.sum(
                jnp.where(spot == place * own + k, weighted_ref[c], 0.0), axis=0, keepdims=True
            )
    out = pltpu.make_async_copy(own_ref, own_out, sem)
    out.start()
    rows, cols, _ = field_ref.shape
    wide = cols + 2 * SWEEPS
    tile = SWEEPS * wide
    mine = rows_ref[rows_ref.shape[0] - other_ref.shape[0] :].astype(jnp.float32)
    other = other_ref[...].astype(jnp.float32)
    even = lax.axis_index("freq") % 2 == 0
    before, after = sides_of(
        jnp.where(even, mine, other), jnp.where(even, other, mine), "px"
    )
    for k in range(SWEEPS):
        state_ref[0, k] = before[k * wide : (k + 1) * wide]
        state_ref[0, SWEEPS + rows + k] = after[k * wide : (k + 1) * wide]
    for x in range(rows):
        state_ref[0, SWEEPS + x] = jnp.concatenate([field_ref[x], side_ref[x]], axis=0)
    marks = (
        [before[tile + k : tile + k + 1] for k in range(SWEEPS)]
        + [wide_ref[x : x + 1] for x in range(rows)]
        + [after[tile + k : tile + k + 1] for k in range(SWEEPS)]
    )
    count, levels = table_ref.shape
    spread = (
        lax.broadcasted_iota(jnp.int32, (count, count * real), 1) // real
        == lax.broadcasted_iota(jnp.int32, (count, count * real), 0)
    ).astype(jnp.float32)
    turn = (((0,), (0,)), ((), ()))
    table = lax.dot_general(
        table_ref[...],
        spread,
        turn,
        precision=lax.Precision.HIGHEST,
        preferred_element_type=jnp.float32,
    )
    high = table.astype(jnp.bfloat16)
    rest = table - high.astype(jnp.float32)
    middle = rest.astype(jnp.bfloat16)
    low = (rest - middle.astype(jnp.float32)).astype(jnp.bfloat16)
    table = jnp.concatenate([high, middle, low], axis=0)
    level = lax.broadcasted_iota(jnp.int32, (levels, real), 0).astype(jnp.float32) + 1.0
    for x in range(1, 2 * SWEEPS + rows - 1):
        onehot = (level == marks[x]).astype(jnp.float32).astype(jnp.bfloat16)
        onehot = jnp.concatenate([onehot] * 3, axis=0)[:, :wide]
        coef = lax.dot_general(onehot, table, turn, preferred_element_type=jnp.float32)
        for c in range(count):
            coef_ref[x, c] = coef[:, c * real : (c + 1) * real]
    for sweep in range(SWEEPS):
        now, later = sweep % 2, (sweep + 1) % 2
        for x in range(sweep + 1, 2 * SWEEPS + rows - sweep - 1):
            center = state_ref[now, x]
            beside = (
                coef_ref[x, 1] * state_ref[now, x - 1]
                + coef_ref[x, 2] * state_ref[now, x + 1]
                + coef_ref[x, 3] * pltpu.roll(center, 1, 0)
                + coef_ref[x, 4] * pltpu.roll(center, wide - 1, 0)
            )
            new = coef_ref[x, 0] * center - beside
            if sweep < SWEEPS - 1:
                state_ref[later, x] = new
            else:
                prior_ref[x - SWEEPS] = PRIOR_WEIGHT * new[:cols]
    out.wait()


def finish(pair_ref, far_ref, prior_ref, low0_ref, low3_ref, low2_ref, low1_ref, out, held_ref, sems):
    rows, cols, real = held_ref.shape
    beside = pair_ref.shape[0] // 2
    side = rows // beside
    low = jnp.concatenate([low0_ref[...], low1_ref[...], low2_ref[...], low3_ref[...]], axis=0)
    copies = []
    for x in range(beside):
        kernel = jnp.concatenate(
            [pair_ref[x], pair_ref[beside + x], far_ref[x], far_ref[beside + x]], axis=0
        )
        grad = lax.dot_general(
            kernel, low, (((0,), (0,)), ((), ())), preferred_element_type=jnp.float32
        )
        for k in range(side):
            row = k * beside + x
            held_ref[row] = grad[k * cols : (k + 1) * cols] + prior_ref[row]
            copies.append(pltpu.make_async_copy(held_ref.at[row], out.at[row], sems.at[row]))
            copies[-1].start()
    for copy in copies:
        copy.wait()


def local(observed, noise_scale, forward_kernel, model_field, classes, kappa_table, coupling_table):
    rows, cols, real = model_field.shape
    comps, sensors = forward_kernel.shape[3:]
    own = observed.shape[1]
    points = comps * sensors
    kernel_own = forward_kernel[0].transpose(0, 2, 3, 1).reshape(rows, points, cols)
    beside = rows // max(1, min(rows, LANES // cols))
    side = rows // beside
    assert sensors <= TILE * real and cols + 2 * SWEEPS <= LANES
    assert rows >= SWEEPS and cols % TILE == 0 and points % 16 == 0
    rim_rows = rows * (SWEEPS + 1)
    wide_py, wide_px = lax.axis_size("py") > 2, lax.axis_size("px") > 2
    payload, kernel_own, model_field, marks, table, *far_rim = call(
        prepare,
        ((points + TILE + rim_rows, real), jnp.float32),
        ((beside, points, side * cols), jnp.bfloat16),
        (model_field.shape, jnp.float32),
        ((rows, LANES), jnp.float32),
        ((1 + coupling_table.shape[0], coupling_table.shape[1]), jnp.float32),
        *[((rim_rows, real), jnp.float32)] * wide_py,
        fetch=True,
        keep=((3, 2),),
    )(
        noise_scale,
        observed[0],
        kernel_own,
        model_field,
        classes,
        kappa_table[None],
        coupling_table,
    )
    got = swap(payload, "py", near)
    kernel_next = swap(kernel_own, "freq", near)
    two = [swap(rim, "py", far("py")) for rim in far_rim]
    summed = ((points + TILE, real), jnp.float32)
    rim_size = SWEEPS * (cols + 2 * SWEEPS) + 2 * TILE
    peers, freqs = lax.axis_size("px"), lax.axis_size("freq")
    side_shapes = (
        ((rows, 2 * SWEEPS, real), jnp.float32),
        ((rows, LANES), jnp.float32),
    )
    pair_shape = ((2 * beside, points, side * cols), jnp.bfloat16)

    def by_parity(own, even_partner, odd_partner):
        return lax.ppermute(
            own,
            ("freq", "px"),
            [
                (f * peers + i, f * peers + (odd_partner if f % 2 else even_partner)(i))
                for f in range(freqs)
                for i in range(peers)
            ],
        )

    if peers == 4 and lax.axis_size("py") == 2:
        part = 2 * (points + TILE)
        total, side_rim, wide_marks, mixed = call(
            spread,
            summed,
            *side_shapes,
            ((part + rim_size, real), jnp.bfloat16),
        )(payload, got, model_field, marks)
        mixed = by_parity(mixed, near, far("px"))
        cross = by_parity(total, far("px"), near)
        skip = swap(total, "px", lambda i: i ^ 2)
        (kernel_pair,) = call(join, pair_shape, flops=JOIN_FLOPS)(kernel_own, kernel_next, total)
        sums = (total, cross, skip, mixed)
        rim_rows, sent_rows = mixed, mixed[part:]
    else:
        (total,) = call(add, summed)(payload, got)
        for bit in bits("py")[1:]:
            (total,) = call(add, summed)(total, swap(total, "py", lambda i: i ^ bit))
        side_rim, wide_marks, rim_rows = call(
            edge, *side_shapes, ((rim_size, real), jnp.bfloat16), flops=EDGE_FLOPS
        )(total, got, model_field, marks, *two)
        rim_rows = sent_rows = by_parity(rim_rows, near, far("px") if wide_px else near)
        *steps, last = bits("px")
        for bit in steps[:-1]:
            (total,) = call(add, summed)(total, swap(total, "px", lambda i: i ^ bit))
        total, kernel_pair = call(add_and_join, summed, pair_shape, flops=ORDER_FLOPS)(
            total, swap(total, "px", lambda i: i ^ steps[-1]), kernel_own, kernel_next
        )
        sums = (total, swap(total, "px", lambda i: i ^ last))
    kernel_far = swap(kernel_pair, "freq", lambda i: i ^ 2)
    assert freqs == 4
    weighted_low, weighted = call(
        weigh,
        ((points, real), jnp.bfloat16),
        ((comps, sensors, real), jnp.float32),
        flops=ORDER_FLOPS,
    )(*sums)
    other_rows = swap(sent_rows, "freq", near)
    low_one = swap(weighted_low, "freq", near)
    low_three = swap(weighted_low, "freq", lambda i: i ^ 3)
    low_two = swap(weighted_low, "freq", lambda i: i ^ 2)
    wide = cols + 2 * SWEEPS
    prior_term, weighted_own = call(
        prior,
        (model_field.shape, jnp.float32),
        ((own, comps, real), jnp.float32),
        stored=(1,),
        scratch=(
            pltpu.VMEM((2, rows + 2 * SWEEPS, wide, real), jnp.float32),
            pltpu.VMEM((rows + 2 * SWEEPS, table.shape[0], wide, real), jnp.float32),
            pltpu.VMEM((own, comps, real), jnp.float32),
            pltpu.SemaphoreType.DMA(()),
        ),
        flops=PRIOR_FLOPS,
    )(model_field, side_rim, wide_marks, rim_rows, other_rows, table, weighted)
    (gradient,) = call(
        finish,
        (model_field.shape, jnp.float32),
        stored=(0,),
        scratch=(
            pltpu.VMEM(model_field.shape, jnp.float32),
            pltpu.SemaphoreType.DMA((rows,)),
        ),
    )(kernel_pair, kernel_far, prior_term, weighted_low, low_three, low_two, low_one)
    return weighted_own[None], gradient


def solution(mesh):
    in_specs = (
        P("freq", ("px", "py"), None, None),
        P("freq", ("px", "py")),
        P("freq", "px", "py", None, None),
        P("px", "py", None),
        P("px", "py"),
        P(),
        P(),
    )
    out_specs = (P("freq", ("px", "py"), None, None), P("px", "py", None))
    return jax.shard_map(local, mesh=mesh, in_specs=in_specs, out_specs=out_specs, check_vma=False)
```

```python
import jax
import jax.numpy as jnp
from jax import lax
from jax.experimental import pallas as pl
from jax.experimental.pallas import tpu as pltpu
from jax.sharding import PartitionSpec as P

SWEEPS = 4
FREEDOM = 4.0
PRIOR_WEIGHT = 0.04
LANES = 128
TILE = 8
VMEM_BYTES = 40 << 20
PRIOR_FLOPS = 1 << 30
EDGE_FLOPS = 1 << 30
JOIN_FLOPS = 1 << 30
ORDER_FLOPS = 1 << 32


def swap(own, axis, partner):
    return lax.ppermute(own, axis, [(i, partner(i)) for i in range(lax.axis_size(axis))])


def bits(axis):
    size = lax.axis_size(axis)
    assert size & (size - 1) == 0
    return [1 << k for k in range(size.bit_length() - 1)]


def near(i):
    return i ^ 1


def far(axis):
    return lambda i: (((i + 1) ^ 1) - 1) % lax.axis_size(axis)


def call(body, *out_shapes, fetch=False, keep=(), scratch=(), stored=(), flops=0):
    def run(*operands):
        count, kept = len(operands), dict(keep)
        if fetch:
            operands = [pltpu.with_memory_space_constraint(x, pltpu.HBM) for x in operands]

        def fetched(*refs):
            outs = refs[count : count + len(out_shapes)]
            room, sems = iter(refs[count + len(out_shapes) : -1]), refs[-1]
            held = [outs[kept[k]] if k in kept else next(room) for k in range(count)]
            copies = [
                pltpu.make_async_copy(src, dst, sems.at[k])
                for k, (src, dst) in enumerate(zip(refs[:count], held))
            ]
            for k in sorted(range(count), key=lambda k: -operands[k].size):
                copies[k].start()
            for copy in copies:
                copy.wait()
            body(*held, *outs)

        return pl.pallas_call(
            fetched if fetch else body,
            out_shape=[jax.ShapeDtypeStruct(shape, dtype) for shape, dtype in out_shapes],
            in_specs=[pl.BlockSpec(memory_space=pltpu.HBM if fetch else pltpu.VMEM)] * count,
            out_specs=[
                pl.BlockSpec(memory_space=pltpu.HBM if k in stored else pltpu.VMEM)
                for k in range(len(out_shapes))
            ],
            scratch_shapes=list(scratch)
            + [pltpu.VMEM(x.shape, x.dtype) for k, x in enumerate(operands) if k not in kept] * fetch
            + [pltpu.SemaphoreType.DMA((count,))] * fetch,
            compiler_params=pltpu.CompilerParams(vmem_limit_bytes=VMEM_BYTES),
            cost_estimate=pl.CostEstimate(flops=flops, bytes_accessed=0, transcendentals=0),
        )(*operands)

    return run


def prepare(
    noise_ref,
    observed_ref,
    kernel_ref,
    field_ref,
    classes_ref,
    kappa_ref,
    coupling_ref,
    pay_ref,
    packed_ref,
    _,
    marks_ref,
    table_ref,
    *far_ref,
):
    beside, points, width = packed_ref.shape
    rows, cols, real = field_ref.shape
    own, comps = observed_ref.shape[:2]
    sensors = points // comps
    place = lax.axis_index("px") * lax.axis_size("py") + lax.axis_index("py")
    even = lax.axis_index("py") % 2 == 0
    packed, field = [], []
    for x in range(beside):
        picks = range(x, rows, beside)
        packed.append(jnp.concatenate([kernel_ref[k] for k in picks], axis=1))
        packed_ref[x] = packed[-1]
        field += [field_ref[k].astype(jnp.bfloat16) for k in picks]
    total = jnp.dot(
        jnp.concatenate(packed, axis=1),
        jnp.concatenate(field, axis=0),
        preferred_element_type=jnp.float32,
    )
    spot = lax.broadcasted_iota(jnp.int32, (points, real), 0)
    for c in range(comps):
        for k in range(own):
            row = c * sensors + place * own + k
            total = total - jnp.where(spot == row, observed_ref[k, c : c + 1, :], 0.0)
    pay_ref[:points] = total
    spot = lax.broadcasted_iota(jnp.int32, (TILE, real), 0) * real + lax.broadcasted_iota(
        jnp.int32, (TILE, real), 1
    )
    noise = jnp.zeros((TILE, real), jnp.float32)
    for k in range(own):
        noise = noise + jnp.where(spot == place * own + k, noise_ref[0:1, k : k + 1], 0.0)
    pay_ref[points : points + TILE] = noise
    coupling = coupling_ref[...]
    table_ref[0:1] = kappa_ref[...] + jnp.sum(coupling, axis=0, keepdims=True)
    table_ref[1:] = coupling
    marks = (classes_ref[...] + 1).astype(jnp.float32)
    marks_ref[...] = jnp.zeros_like(marks_ref)
    marks_ref[:, :cols] = marks
    edges = [
        (field_ref[:, cols - SWEEPS :, :], marks[:, cols - SWEEPS :]),
        (field_ref[:, :SWEEPS, :], marks[:, :SWEEPS]),
    ]

    def put(ref, start, chosen):
        for x in range(rows):
            ref[start + x * SWEEPS : start + (x + 1) * SWEEPS] = jnp.where(
                chosen, edges[0][0][x], edges[1][0][x]
            )
        start = start + rows * SWEEPS
        ref[start : start + rows] = jnp.zeros((rows, real), jnp.float32)
        ref[start : start + rows, :SWEEPS] = jnp.where(chosen, edges[0][1], edges[1][1])

    put(pay_ref, points + TILE, even)
    for ref in far_ref:
        put(ref, 0, jnp.logical_not(even))


def sides_of(one, two, axis):
    me = lax.axis_index(axis)
    even = me % 2 == 0
    before = jnp.where(me == 0, 0.0, jnp.where(even, two, one))
    after = jnp.where(me == lax.axis_size(axis) - 1, 0.0, jnp.where(even, one, two))
    return before, after


def add(mine_ref, got_ref, out_ref):
    size = out_ref.shape[0]
    out_ref[...] = mine_ref[:size] + got_ref[:size]


def add_and_join(mine_ref, got_ref, one_ref, two_ref, out_ref, joined_ref):
    out_ref[...] = mine_ref[...] + got_ref[...]
    half = one_ref.shape[0]
    joined_ref[:half] = one_ref[...]
    joined_ref[half:] = two_ref[...]


def lay(got_ref, field_ref, marks_ref, far_ref, side_ref, wide_ref, rows_ref, base):
    rows, cols, real = field_ref.shape
    one = got_ref[got_ref.shape[0] - rows * (SWEEPS + 1) :]
    before, after = sides_of(one, far_ref[0][...] if far_ref else one, "py")
    fields = rows * SWEEPS
    wide_ref[...] = (
        marks_ref[...]
        + pltpu.roll(after[fields:], cols, 1)
        + pltpu.roll(before[fields:], cols + SWEEPS, 1)
    )
    for x in range(rows):
        pick = slice(x * SWEEPS, (x + 1) * SWEEPS)
        side_ref[x] = jnp.concatenate([after[pick], before[pick]], axis=0)
    chosen = lax.axis_index("px") % 2 == 0
    if lax.axis_size("px") > 2:
        chosen = chosen == (lax.axis_index("freq") % 2 == 0)
    spot = lax.broadcasted_iota(jnp.int32, (2 * TILE, real), 0)
    blocks, tile = [], jnp.zeros((2 * TILE, real), jnp.float32)
    for k in range(SWEEPS):
        last = rows - SWEEPS + k
        blocks.append(jnp.where(chosen, field_ref[last], field_ref[k]))
        blocks.append(jnp.where(chosen, side_ref[last], side_ref[k]))
        marks = jnp.where(chosen, wide_ref[last : last + 1], wide_ref[k : k + 1])
        tile = jnp.where(spot == k, marks, tile)
    rows_ref[base:] = jnp.concatenate(blocks + [tile], axis=0).astype(jnp.bfloat16)


def edge(after_ref, got_ref, field_ref, marks_ref, *refs):
    *far_ref, side_ref, wide_ref, rows_ref = refs
    lay(got_ref, field_ref, marks_ref, far_ref, side_ref, wide_ref, rows_ref, 0)


def spread(mine_ref, got_ref, field_ref, marks_ref, *refs):
    *far_ref, out_ref, side_ref, wide_ref, mixed_ref = refs
    size, real = out_ref.shape
    total = mine_ref[:size] + got_ref[:size]
    out_ref[...] = total
    points = size - TILE
    high = total.astype(jnp.bfloat16).astype(jnp.float32)
    low = total - high
    mixed_ref[: 2 * size] = jnp.concatenate(
        [high[:points], low[:points], high[points:], low[points:]], axis=0
    ).astype(jnp.bfloat16)
    lay(got_ref, field_ref, marks_ref, far_ref, side_ref, wide_ref, mixed_ref, 2 * size)


def join(one_ref, two_ref, after_ref, out_ref):
    half = one_ref.shape[0]
    out_ref[:half] = one_ref[...]
    out_ref[half:] = two_ref[...]


def weigh(*refs):
    mine_ref, *got_refs, low_ref, weighted_ref = refs
    comps, sensors, real = weighted_ref.shape
    points = comps * sensors
    total = mine_ref[...]
    size = total.shape[0]
    for got_ref in got_refs:
        if got_ref.dtype == jnp.bfloat16:
            parts = got_ref[: 2 * size].astype(jnp.float32)
            sums = parts[:points] + parts[points : 2 * points]
            noises = parts[2 * points : 2 * points + TILE] + parts[2 * points + TILE :]
            total = total + jnp.concatenate([sums, noises], axis=0)
        else:
            total = total + got_ref[...]
    chunk = min(sensors, real)
    eye = lax.broadcasted_iota(jnp.int32, (chunk, real), 0) == lax.broadcasted_iota(
        jnp.int32, (chunk, real), 1
    )
    for k in range(sensors // chunk):
        row = total[points + k : points + k + 1]
        noise = jnp.sum(jnp.where(eye, row, 0.0), axis=1, keepdims=True)
        inverse = 1.0 / (noise * noise)
        misfit = [total[c * sensors + k * chunk : c * sensors + (k + 1) * chunk] for c in range(comps)]
        spread = sum(part * part for part in misfit) * inverse
        factor = (FREEDOM + 2.0) / (FREEDOM + spread) * inverse
        for c in range(comps):
            weighted = misfit[c] * factor
            weighted_ref[c, k * chunk : (k + 1) * chunk] = weighted
            low_ref[c * sensors + k * chunk : c * sensors + (k + 1) * chunk] = weighted.astype(
                jnp.bfloat16
            )


def prior(
    field_ref,
    side_ref,
    wide_ref,
    rows_ref,
    other_ref,
    table_ref,
    weighted_ref,
    prior_ref,
    own_out,
    state_ref,
    coef_ref,
    own_ref,
    sem,
):
    own, comps, real = own_ref.shape
    sensors = weighted_ref.shape[1]
    place = lax.axis_index("px") * lax.axis_size("py") + lax.axis_index("py")
    spot = lax.broadcasted_iota(jnp.int32, (sensors, real), 0)
    for c in range(comps):
        for k in range(own):
            own_ref[k, c : c + 1] = jnp.sum(
                jnp.where(spot == place * own + k, weighted_ref[c], 0.0), axis=0, keepdims=True
            )
    out = pltpu.make_async_copy(own_ref, own_out, sem)
    out.start()
    rows, cols, _ = field_ref.shape
    wide = cols + 2 * SWEEPS
    tile = SWEEPS * wide
    mine = rows_ref[rows_ref.shape[0] - other_ref.shape[0] :].astype(jnp.float32)
    other = other_ref[...].astype(jnp.float32)
    even = lax.axis_index("freq") % 2 == 0
    before, after = sides_of(
        jnp.where(even, mine, other), jnp.where(even, other, mine), "px"
    )
    for k in range(SWEEPS):
        state_ref[0, k] = before[k * wide : (k + 1) * wide]
        state_ref[0, SWEEPS + rows + k] = after[k * wide : (k + 1) * wide]
    for x in range(rows):
        state_ref[0, SWEEPS + x] = jnp.concatenate([field_ref[x], side_ref[x]], axis=0)
    marks = (
        [before[tile + k : tile + k + 1] for k in range(SWEEPS)]
        + [wide_ref[x : x + 1] for x in range(rows)]
        + [after[tile + k : tile + k + 1] for k in range(SWEEPS)]
    )
    count, levels = table_ref.shape
    spread = (
        lax.broadcasted_iota(jnp.int32, (count, count * real), 1) // real
        == lax.broadcasted_iota(jnp.int32, (count, count * real), 0)
    ).astype(jnp.float32)
    turn = (((0,), (0,)), ((), ()))
    table = lax.dot_general(
        table_ref[...],
        spread,
        turn,
        precision=lax.Precision.HIGHEST,
        preferred_element_type=jnp.float32,
    )
    high = table.astype(jnp.bfloat16)
    rest = table - high.astype(jnp.float32)
    middle = rest.astype(jnp.bfloat16)
    low = (rest - middle.astype(jnp.float32)).astype(jnp.bfloat16)
    table = jnp.concatenate([high, middle, low], axis=0)
    level = lax.broadcasted_iota(jnp.int32, (levels, real), 0).astype(jnp.float32) + 1.0
    for x in range(1, 2 * SWEEPS + rows - 1):
        onehot = (level == marks[x]).astype(jnp.float32).astype(jnp.bfloat16)
        onehot = jnp.concatenate([onehot] * 3, axis=0)[:, :wide]
        coef = lax.dot_general(onehot, table, turn, preferred_element_type=jnp.float32)
        for c in range(count):
            coef_ref[x, c] = coef[:, c * real : (c + 1) * real]
    for sweep in range(SWEEPS):
        now, later = sweep % 2, (sweep + 1) % 2
        for x in range(sweep + 1, 2 * SWEEPS + rows - sweep - 1):
            center = state_ref[now, x]
            beside = (
                coef_ref[x, 1] * state_ref[now, x - 1]
                + coef_ref[x, 2] * state_ref[now, x + 1]
                + coef_ref[x, 3] * pltpu.roll(center, 1, 0)
                + coef_ref[x, 4] * pltpu.roll(center, wide - 1, 0)
            )
            new = coef_ref[x, 0] * center - beside
            if sweep < SWEEPS - 1:
                state_ref[later, x] = new
            else:
                prior_ref[x - SWEEPS] = PRIOR_WEIGHT * new[:cols]
    out.wait()


def share(one, two, low):
    return lax.dot_general(
        jnp.concatenate([one, two], axis=0),
        low,
        (((0,), (0,)), ((), ())),
        preferred_element_type=jnp.float32,
    )


def begin(pair_ref, far_ref, prior_ref, low0_ref, low3_ref, base_ref):
    rows, cols, real = prior_ref.shape
    beside = pair_ref.shape[0] // 2
    low = jnp.concatenate([low0_ref[...], low3_ref[...]], axis=0)
    for x in range(beside):
        grad = share(pair_ref[x], far_ref[beside + x], low)
        for k in range(rows // beside):
            row = k * beside + x
            base_ref[row] = grad[k * cols : (k + 1) * cols] + prior_ref[row]


def finish(pair_ref, far_ref, base_ref, low2_ref, low1_ref, out, held_ref, sems):
    rows, cols, real = held_ref.shape
    beside = pair_ref.shape[0] // 2
    low = jnp.concatenate([low1_ref[...], low2_ref[...]], axis=0)
    copies = []
    for x in range(beside):
        grad = share(pair_ref[beside + x], far_ref[x], low)
        for k in range(rows // beside):
            row = k * beside + x
            held_ref[row] = grad[k * cols : (k + 1) * cols] + base_ref[row]
            copies.append(pltpu.make_async_copy(held_ref.at[row], out.at[row], sems.at[row]))
            copies[-1].start()
    for copy in copies:
        copy.wait()


def local(observed, noise_scale, forward_kernel, model_field, classes, kappa_table, coupling_table):
    rows, cols, real = model_field.shape
    comps, sensors = forward_kernel.shape[3:]
    own = observed.shape[1]
    points = comps * sensors
    kernel_own = forward_kernel[0].transpose(0, 2, 3, 1).reshape(rows, points, cols)
    beside = rows // max(1, min(rows, LANES // cols))
    side = rows // beside
    assert sensors <= TILE * real and cols + 2 * SWEEPS <= LANES
    assert rows >= SWEEPS and cols % TILE == 0 and points % 16 == 0
    rim_rows = rows * (SWEEPS + 1)
    wide_py, wide_px = lax.axis_size("py") > 2, lax.axis_size("px") > 2
    payload, kernel_own, model_field, marks, table, *far_rim = call(
        prepare,
        ((points + TILE + rim_rows, real), jnp.float32),
        ((beside, points, side * cols), jnp.bfloat16),
        (model_field.shape, jnp.float32),
        ((rows, LANES), jnp.float32),
        ((1 + coupling_table.shape[0], coupling_table.shape[1]), jnp.float32),
        *[((rim_rows, real), jnp.float32)] * wide_py,
        fetch=True,
        keep=((3, 2),),
    )(
        noise_scale,
        observed[0],
        kernel_own,
        model_field,
        classes,
        kappa_table[None],
        coupling_table,
    )
    got = swap(payload, "py", near)
    kernel_next = swap(kernel_own, "freq", near)
    two = [swap(rim, "py", far("py")) for rim in far_rim]
    summed = ((points + TILE, real), jnp.float32)
    rim_size = SWEEPS * (cols + 2 * SWEEPS) + 2 * TILE
    peers, freqs = lax.axis_size("px"), lax.axis_size("freq")
    side_shapes = (
        ((rows, 2 * SWEEPS, real), jnp.float32),
        ((rows, LANES), jnp.float32),
    )
    pair_shape = ((2 * beside, points, side * cols), jnp.bfloat16)

    def by_parity(own, even_partner, odd_partner):
        return lax.ppermute(
            own,
            ("freq", "px"),
            [
                (f * peers + i, f * peers + (odd_partner if f % 2 else even_partner)(i))
                for f in range(freqs)
                for i in range(peers)
            ],
        )

    if peers == 4 and lax.axis_size("py") == 2:
        part = 2 * (points + TILE)
        total, side_rim, wide_marks, mixed = call(
            spread,
            summed,
            *side_shapes,
            ((part + rim_size, real), jnp.bfloat16),
        )(payload, got, model_field, marks)
        mixed = by_parity(mixed, near, far("px"))
        cross = by_parity(total, far("px"), near)
        skip = swap(total, "px", lambda i: i ^ 2)
        (kernel_pair,) = call(join, pair_shape, flops=JOIN_FLOPS)(kernel_own, kernel_next, total)
        sums = (total, cross, skip, mixed)
        rim_rows, sent_rows = mixed, mixed[part:]
    else:
        (total,) = call(add, summed)(payload, got)
        for bit in bits("py")[1:]:
            (total,) = call(add, summed)(total, swap(total, "py", lambda i: i ^ bit))
        side_rim, wide_marks, rim_rows = call(
            edge, *side_shapes, ((rim_size, real), jnp.bfloat16), flops=EDGE_FLOPS
        )(total, got, model_field, marks, *two)
        rim_rows = sent_rows = by_parity(rim_rows, near, far("px") if wide_px else near)
        *steps, last = bits("px")
        for bit in steps[:-1]:
            (total,) = call(add, summed)(total, swap(total, "px", lambda i: i ^ bit))
        total, kernel_pair = call(add_and_join, summed, pair_shape, flops=ORDER_FLOPS)(
            total, swap(total, "px", lambda i: i ^ steps[-1]), kernel_own, kernel_next
        )
        sums = (total, swap(total, "px", lambda i: i ^ last))
    kernel_far = swap(kernel_pair, "freq", lambda i: i ^ 2)
    assert freqs == 4
    weighted_low, weighted = call(
        weigh,
        ((points, real), jnp.bfloat16),
        ((comps, sensors, real), jnp.float32),
        flops=ORDER_FLOPS,
    )(*sums)
    other_rows = swap(sent_rows, "freq", near)
    low_one = swap(weighted_low, "freq", near)
    low_three = swap(weighted_low, "freq", lambda i: i ^ 3)
    low_two = swap(weighted_low, "freq", lambda i: i ^ 2)
    wide = cols + 2 * SWEEPS
    prior_term, weighted_own = call(
        prior,
        (model_field.shape, jnp.float32),
        ((own, comps, real), jnp.float32),
        stored=(1,),
        scratch=(
            pltpu.VMEM((2, rows + 2 * SWEEPS, wide, real), jnp.float32),
            pltpu.VMEM((rows + 2 * SWEEPS, table.shape[0], wide, real), jnp.float32),
            pltpu.VMEM((own, comps, real), jnp.float32),
            pltpu.SemaphoreType.DMA(()),
        ),
        flops=PRIOR_FLOPS,
    )(model_field, side_rim, wide_marks, rim_rows, other_rows, table, weighted)
    (base,) = call(begin, (model_field.shape, jnp.float32), flops=EDGE_FLOPS)(
        kernel_pair, kernel_far, prior_term, weighted_low, low_three
    )
    (gradient,) = call(
        finish,
        (model_field.shape, jnp.float32),
        stored=(0,),
        scratch=(
            pltpu.VMEM(model_field.shape, jnp.float32),
            pltpu.SemaphoreType.DMA((rows,)),
        ),
    )(kernel_pair, kernel_far, base, low_two, low_one)
    return weighted_own[None], gradient


def solution(mesh):
    in_specs = (
        P("freq", ("px", "py"), None, None),
        P("freq", ("px", "py")),
        P("freq", "px", "py", None, None),
        P("px", "py", None),
        P("px", "py"),
        P(),
        P(),
    )
    out_specs = (P("freq", ("px", "py"), None, None), P("px", "py", None))
    return jax.shard_map(local, mesh=mesh, in_specs=in_specs, out_specs=out_specs, check_vma=False)
```

```python
import jax
import jax.numpy as jnp
from jax import lax
from jax.experimental import pallas as pl
from jax.experimental.pallas import tpu as pltpu
from jax.sharding import PartitionSpec as P

SWEEPS = 4
FREEDOM = 4.0
PRIOR_WEIGHT = 0.04
LANES = 128
TILE = 8
VMEM_BYTES = 40 << 20
PRIOR_FLOPS = 1 << 30
EDGE_FLOPS = 1 << 30
JOIN_FLOPS = 1 << 30
ORDER_FLOPS = 1 << 32


def swap(own, axis, partner):
    return lax.ppermute(own, axis, [(i, partner(i)) for i in range(lax.axis_size(axis))])


def bits(axis):
    size = lax.axis_size(axis)
    assert size & (size - 1) == 0
    return [1 << k for k in range(size.bit_length() - 1)]


def near(i):
    return i ^ 1


def far(axis):
    return lambda i: (((i + 1) ^ 1) - 1) % lax.axis_size(axis)


def call(body, *out_shapes, fetch=False, keep=(), scratch=(), stored=(), flops=0):
    def run(*operands):
        count, kept = len(operands), dict(keep)
        if fetch:
            operands = [pltpu.with_memory_space_constraint(x, pltpu.HBM) for x in operands]

        def fetched(*refs):
            outs = refs[count : count + len(out_shapes)]
            room, sems = iter(refs[count + len(out_shapes) : -1]), refs[-1]
            held = [outs[kept[k]] if k in kept else next(room) for k in range(count)]
            copies = [
                pltpu.make_async_copy(src, dst, sems.at[k])
                for k, (src, dst) in enumerate(zip(refs[:count], held))
            ]
            for k in sorted(range(count), key=lambda k: -operands[k].size):
                copies[k].start()
            for copy in copies:
                copy.wait()
            body(*held, *outs)

        return pl.pallas_call(
            fetched if fetch else body,
            out_shape=[jax.ShapeDtypeStruct(shape, dtype) for shape, dtype in out_shapes],
            in_specs=[pl.BlockSpec(memory_space=pltpu.HBM if fetch else pltpu.VMEM)] * count,
            out_specs=[
                pl.BlockSpec(memory_space=pltpu.HBM if k in stored else pltpu.VMEM)
                for k in range(len(out_shapes))
            ],
            scratch_shapes=list(scratch)
            + [pltpu.VMEM(x.shape, x.dtype) for k, x in enumerate(operands) if k not in kept] * fetch
            + [pltpu.SemaphoreType.DMA((count,))] * fetch,
            compiler_params=pltpu.CompilerParams(vmem_limit_bytes=VMEM_BYTES),
            cost_estimate=pl.CostEstimate(flops=flops, bytes_accessed=0, transcendentals=0),
        )(*operands)

    return run


def prepare(
    noise_ref,
    observed_ref,
    kernel_ref,
    field_ref,
    classes_ref,
    kappa_ref,
    coupling_ref,
    pay_ref,
    packed_ref,
    _,
    marks_ref,
    table_ref,
    *far_ref,
):
    beside, points, width = packed_ref.shape
    rows, cols, real = field_ref.shape
    own, comps = observed_ref.shape[:2]
    sensors = points // comps
    place = lax.axis_index("px") * lax.axis_size("py") + lax.axis_index("py")
    even = lax.axis_index("py") % 2 == 0
    packed, field = [], []
    for x in range(beside):
        picks = range(x, rows, beside)
        packed.append(jnp.concatenate([kernel_ref[k] for k in picks], axis=1))
        packed_ref[x] = packed[-1]
        field += [field_ref[k].astype(jnp.bfloat16) for k in picks]
    total = jnp.dot(
        jnp.concatenate(packed, axis=1),
        jnp.concatenate(field, axis=0),
        preferred_element_type=jnp.float32,
    )
    spot = lax.broadcasted_iota(jnp.int32, (points, real), 0)
    for c in range(comps):
        for k in range(own):
            row = c * sensors + place * own + k
            total = total - jnp.where(spot == row, observed_ref[k, c : c + 1, :], 0.0)
    pay_ref[:points] = total
    spot = lax.broadcasted_iota(jnp.int32, (TILE, real), 0) * real + lax.broadcasted_iota(
        jnp.int32, (TILE, real), 1
    )
    noise = jnp.zeros((TILE, real), jnp.float32)
    for k in range(own):
        noise = noise + jnp.where(spot == place * own + k, noise_ref[0:1, k : k + 1], 0.0)
    pay_ref[points : points + TILE] = noise
    coupling = coupling_ref[...]
    table_ref[0:1] = kappa_ref[...] + jnp.sum(coupling, axis=0, keepdims=True)
    table_ref[1:] = coupling
    marks = (classes_ref[...] + 1).astype(jnp.float32)
    marks_ref[...] = jnp.zeros_like(marks_ref)
    marks_ref[:, :cols] = marks
    edges = [
        (field_ref[:, cols - SWEEPS :, :], marks[:, cols - SWEEPS :]),
        (field_ref[:, :SWEEPS, :], marks[:, :SWEEPS]),
    ]

    def put(ref, start, chosen):
        for x in range(rows):
            ref[start + x * SWEEPS : start + (x + 1) * SWEEPS] = jnp.where(
                chosen, edges[0][0][x], edges[1][0][x]
            )
        start = start + rows * SWEEPS
        ref[start : start + rows] = jnp.zeros((rows, real), jnp.float32)
        ref[start : start + rows, :SWEEPS] = jnp.where(chosen, edges[0][1], edges[1][1])

    put(pay_ref, points + TILE, even)
    for ref in far_ref:
        put(ref, 0, jnp.logical_not(even))


def sides_of(one, two, axis):
    me = lax.axis_index(axis)
    even = me % 2 == 0
    before = jnp.where(me == 0, 0.0, jnp.where(even, two, one))
    after = jnp.where(me == lax.axis_size(axis) - 1, 0.0, jnp.where(even, one, two))
    return before, after


def add(mine_ref, got_ref, out_ref):
    size = out_ref.shape[0]
    out_ref[...] = mine_ref[:size] + got_ref[:size]


def add_and_join(mine_ref, got_ref, one_ref, two_ref, out_ref, joined_ref):
    out_ref[...] = mine_ref[...] + got_ref[...]
    half = one_ref.shape[0]
    joined_ref[:half] = one_ref[...]
    joined_ref[half:] = two_ref[...]


def lay(got_ref, field_ref, marks_ref, far_ref, side_ref, wide_ref, rows_ref, base):
    rows, cols, real = field_ref.shape
    one = got_ref[got_ref.shape[0] - rows * (SWEEPS + 1) :]
    before, after = sides_of(one, far_ref[0][...] if far_ref else one, "py")
    fields = rows * SWEEPS
    wide_ref[...] = (
        marks_ref[...]
        + pltpu.roll(after[fields:], cols, 1)
        + pltpu.roll(before[fields:], cols + SWEEPS, 1)
    )
    for x in range(rows):
        pick = slice(x * SWEEPS, (x + 1) * SWEEPS)
        side_ref[x] = jnp.concatenate([after[pick], before[pick]], axis=0)
    chosen = lax.axis_index("px") % 2 == 0
    if lax.axis_size("px") > 2:
        chosen = chosen == (lax.axis_index("freq") % 2 == 0)
    spot = lax.broadcasted_iota(jnp.int32, (2 * TILE, real), 0)
    blocks, tile = [], jnp.zeros((2 * TILE, real), jnp.float32)
    for k in range(SWEEPS):
        last = rows - SWEEPS + k
        blocks.append(jnp.where(chosen, field_ref[last], field_ref[k]))
        blocks.append(jnp.where(chosen, side_ref[last], side_ref[k]))
        marks = jnp.where(chosen, wide_ref[last : last + 1], wide_ref[k : k + 1])
        tile = jnp.where(spot == k, marks, tile)
    rows_ref[base:] = jnp.concatenate(blocks + [tile], axis=0).astype(jnp.bfloat16)


def edge(after_ref, got_ref, field_ref, marks_ref, *refs):
    *far_ref, side_ref, wide_ref, rows_ref = refs
    lay(got_ref, field_ref, marks_ref, far_ref, side_ref, wide_ref, rows_ref, 0)


def spread(mine_ref, got_ref, field_ref, marks_ref, *refs):
    *far_ref, out_ref, side_ref, wide_ref, mixed_ref = refs
    size, real = out_ref.shape
    total = mine_ref[:size] + got_ref[:size]
    out_ref[...] = total
    points = size - TILE
    high = total.astype(jnp.bfloat16).astype(jnp.float32)
    low = total - high
    mixed_ref[: 2 * size] = jnp.concatenate(
        [high[:points], low[:points], high[points:], low[points:]], axis=0
    ).astype(jnp.bfloat16)
    lay(got_ref, field_ref, marks_ref, far_ref, side_ref, wide_ref, mixed_ref, 2 * size)


def join(one_ref, two_ref, after_ref, out_ref):
    half = one_ref.shape[0]
    out_ref[:half] = one_ref[...]
    out_ref[half:] = two_ref[...]


def weigh(*refs):
    mine_ref, *got_refs, low_ref, weighted_ref = refs
    comps, sensors, real = weighted_ref.shape
    points = comps * sensors
    total = mine_ref[...]
    size = total.shape[0]
    for got_ref in got_refs:
        if got_ref.dtype == jnp.bfloat16:
            parts = got_ref[: 2 * size].astype(jnp.float32)
            sums = parts[:points] + parts[points : 2 * points]
            noises = parts[2 * points : 2 * points + TILE] + parts[2 * points + TILE :]
            total = total + jnp.concatenate([sums, noises], axis=0)
        else:
            total = total + got_ref[...]
    chunk = min(sensors, real)
    eye = lax.broadcasted_iota(jnp.int32, (chunk, real), 0) == lax.broadcasted_iota(
        jnp.int32, (chunk, real), 1
    )
    for k in range(sensors // chunk):
        row = total[points + k : points + k + 1]
        noise = jnp.sum(jnp.where(eye, row, 0.0), axis=1, keepdims=True)
        inverse = 1.0 / (noise * noise)
        misfit = [total[c * sensors + k * chunk : c * sensors + (k + 1) * chunk] for c in range(comps)]
        spread = sum(part * part for part in misfit) * inverse
        factor = (FREEDOM + 2.0) / (FREEDOM + spread) * inverse
        for c in range(comps):
            weighted = misfit[c] * factor
            weighted_ref[c, k * chunk : (k + 1) * chunk] = weighted
            low_ref[c * sensors + k * chunk : c * sensors + (k + 1) * chunk] = weighted.astype(
                jnp.bfloat16
            )


def coefficients(marks, table_ref, count, wide):
    levels, real = table_ref.shape[0] // 3, marks.shape[1]
    level = lax.broadcasted_iota(jnp.int32, (levels, real), 0).astype(jnp.float32) + 1.0
    onehot = (level == marks).astype(jnp.float32).astype(jnp.bfloat16)
    coef = lax.dot_general(
        jnp.concatenate([onehot] * 3, axis=0)[:, :wide],
        table_ref[...],
        (((0,), (0,)), ((), ())),
        preferred_element_type=jnp.float32,
    )
    return [coef[:, c * real : (c + 1) * real] for c in range(count)]


def ready(wide_ref, table_ref, weighted_ref, coef_ref, parts_ref, own_out, own_ref, sem):
    own, comps, real = own_ref.shape
    sensors = weighted_ref.shape[1]
    place = lax.axis_index("px") * lax.axis_size("py") + lax.axis_index("py")
    spot = lax.broadcasted_iota(jnp.int32, (sensors, real), 0)
    for c in range(comps):
        for k in range(own):
            own_ref[k, c : c + 1] = jnp.sum(
                jnp.where(spot == place * own + k, weighted_ref[c], 0.0), axis=0, keepdims=True
            )
    out = pltpu.make_async_copy(own_ref, own_out, sem)
    out.start()
    count, levels = table_ref.shape
    spread = (
        lax.broadcasted_iota(jnp.int32, (count, count * real), 1) // real
        == lax.broadcasted_iota(jnp.int32, (count, count * real), 0)
    ).astype(jnp.float32)
    turn = (((0,), (0,)), ((), ()))
    table = lax.dot_general(
        table_ref[...],
        spread,
        turn,
        precision=lax.Precision.HIGHEST,
        preferred_element_type=jnp.float32,
    )
    high = table.astype(jnp.bfloat16)
    rest = table - high.astype(jnp.float32)
    middle = rest.astype(jnp.bfloat16)
    low = (rest - middle.astype(jnp.float32)).astype(jnp.bfloat16)
    table = jnp.concatenate([high, middle, low], axis=0)
    parts_ref[...] = table
    for x in range(coef_ref.shape[0]):
        for c, coef in enumerate(
            coefficients(wide_ref[x : x + 1], parts_ref, count, coef_ref.shape[2])
        ):
            coef_ref[x, c] = coef
    out.wait()


def prior(
    field_ref,
    side_ref,
    rows_ref,
    other_ref,
    own_coef_ref,
    parts_ref,
    prior_ref,
    state_ref,
    coef_ref,
):
    rows, cols, _ = field_ref.shape
    wide = cols + 2 * SWEEPS
    tile = SWEEPS * wide
    mine = rows_ref[rows_ref.shape[0] - other_ref.shape[0] :].astype(jnp.float32)
    other = other_ref[...].astype(jnp.float32)
    even = lax.axis_index("freq") % 2 == 0
    before, after = sides_of(
        jnp.where(even, mine, other), jnp.where(even, other, mine), "px"
    )
    for k in range(SWEEPS):
        state_ref[0, k] = before[k * wide : (k + 1) * wide]
        state_ref[0, SWEEPS + rows + k] = after[k * wide : (k + 1) * wide]
    for x in range(rows):
        state_ref[0, SWEEPS + x] = jnp.concatenate([field_ref[x], side_ref[x]], axis=0)
    marks = {k: before[tile + k : tile + k + 1] for k in range(1, SWEEPS)}
    marks |= {SWEEPS + rows + k: after[tile + k : tile + k + 1] for k in range(SWEEPS - 1)}
    count = own_coef_ref.shape[1]
    for x in marks:
        for c, coef in enumerate(coefficients(marks[x], parts_ref, count, wide)):
            coef_ref[x, c] = coef

    def coef_of(x, c):
        own = SWEEPS <= x < SWEEPS + rows
        return own_coef_ref[x - SWEEPS, c] if own else coef_ref[x, c]

    for sweep in range(SWEEPS):
        now, later = sweep % 2, (sweep + 1) % 2
        for x in range(sweep + 1, 2 * SWEEPS + rows - sweep - 1):
            center = state_ref[now, x]
            beside = (
                coef_of(x, 1) * state_ref[now, x - 1]
                + coef_of(x, 2) * state_ref[now, x + 1]
                + coef_of(x, 3) * pltpu.roll(center, 1, 0)
                + coef_of(x, 4) * pltpu.roll(center, wide - 1, 0)
            )
            new = coef_of(x, 0) * center - beside
            if sweep < SWEEPS - 1:
                state_ref[later, x] = new
            else:
                prior_ref[x - SWEEPS] = PRIOR_WEIGHT * new[:cols]


def share(one, two, low):
    return lax.dot_general(
        jnp.concatenate([one, two], axis=0),
        low,
        (((0,), (0,)), ((), ())),
        preferred_element_type=jnp.float32,
    )


def begin(pair_ref, far_ref, prior_ref, low0_ref, low3_ref, base_ref):
    rows, cols, real = prior_ref.shape
    beside = pair_ref.shape[0] // 2
    low = jnp.concatenate([low0_ref[...], low3_ref[...]], axis=0)
    for x in range(beside):
        grad = share(pair_ref[x], far_ref[beside + x], low)
        for k in range(rows // beside):
            row = k * beside + x
            base_ref[row] = grad[k * cols : (k + 1) * cols] + prior_ref[row]


def finish(pair_ref, far_ref, base_ref, low2_ref, low1_ref, out, held_ref, sems):
    rows, cols, real = held_ref.shape
    beside = pair_ref.shape[0] // 2
    low = jnp.concatenate([low1_ref[...], low2_ref[...]], axis=0)
    copies = []
    for x in range(beside):
        grad = share(pair_ref[beside + x], far_ref[x], low)
        for k in range(rows // beside):
            row = k * beside + x
            held_ref[row] = grad[k * cols : (k + 1) * cols] + base_ref[row]
            copies.append(pltpu.make_async_copy(held_ref.at[row], out.at[row], sems.at[row]))
            copies[-1].start()
    for copy in copies:
        copy.wait()


def local(observed, noise_scale, forward_kernel, model_field, classes, kappa_table, coupling_table):
    rows, cols, real = model_field.shape
    comps, sensors = forward_kernel.shape[3:]
    own = observed.shape[1]
    points = comps * sensors
    kernel_own = forward_kernel[0].transpose(0, 2, 3, 1).reshape(rows, points, cols)
    beside = rows // max(1, min(rows, LANES // cols))
    side = rows // beside
    assert sensors <= TILE * real and cols + 2 * SWEEPS <= LANES
    assert rows >= SWEEPS and cols % TILE == 0 and points % 16 == 0
    rim_rows = rows * (SWEEPS + 1)
    wide_py, wide_px = lax.axis_size("py") > 2, lax.axis_size("px") > 2
    payload, kernel_own, model_field, marks, table, *far_rim = call(
        prepare,
        ((points + TILE + rim_rows, real), jnp.float32),
        ((beside, points, side * cols), jnp.bfloat16),
        (model_field.shape, jnp.float32),
        ((rows, LANES), jnp.float32),
        ((1 + coupling_table.shape[0], coupling_table.shape[1]), jnp.float32),
        *[((rim_rows, real), jnp.float32)] * wide_py,
        fetch=True,
        keep=((3, 2),),
    )(
        noise_scale,
        observed[0],
        kernel_own,
        model_field,
        classes,
        kappa_table[None],
        coupling_table,
    )
    got = swap(payload, "py", near)
    kernel_next = swap(kernel_own, "freq", near)
    two = [swap(rim, "py", far("py")) for rim in far_rim]
    summed = ((points + TILE, real), jnp.float32)
    rim_size = SWEEPS * (cols + 2 * SWEEPS) + 2 * TILE
    peers, freqs = lax.axis_size("px"), lax.axis_size("freq")
    side_shapes = (
        ((rows, 2 * SWEEPS, real), jnp.float32),
        ((rows, LANES), jnp.float32),
    )
    pair_shape = ((2 * beside, points, side * cols), jnp.bfloat16)

    def by_parity(own, even_partner, odd_partner):
        return lax.ppermute(
            own,
            ("freq", "px"),
            [
                (f * peers + i, f * peers + (odd_partner if f % 2 else even_partner)(i))
                for f in range(freqs)
                for i in range(peers)
            ],
        )

    if peers == 4 and lax.axis_size("py") == 2:
        part = 2 * (points + TILE)
        total, side_rim, wide_marks, mixed = call(
            spread,
            summed,
            *side_shapes,
            ((part + rim_size, real), jnp.bfloat16),
        )(payload, got, model_field, marks)
        mixed = by_parity(mixed, near, far("px"))
        cross = by_parity(total, far("px"), near)
        skip = swap(total, "px", lambda i: i ^ 2)
        (kernel_pair,) = call(join, pair_shape, flops=JOIN_FLOPS)(kernel_own, kernel_next, total)
        sums = (total, cross, skip, mixed)
        rim_rows, sent_rows = mixed, mixed[part:]
    else:
        (total,) = call(add, summed)(payload, got)
        for bit in bits("py")[1:]:
            (total,) = call(add, summed)(total, swap(total, "py", lambda i: i ^ bit))
        side_rim, wide_marks, rim_rows = call(
            edge, *side_shapes, ((rim_size, real), jnp.bfloat16), flops=EDGE_FLOPS
        )(total, got, model_field, marks, *two)
        rim_rows = sent_rows = by_parity(rim_rows, near, far("px") if wide_px else near)
        *steps, last = bits("px")
        for bit in steps[:-1]:
            (total,) = call(add, summed)(total, swap(total, "px", lambda i: i ^ bit))
        total, kernel_pair = call(add_and_join, summed, pair_shape, flops=ORDER_FLOPS)(
            total, swap(total, "px", lambda i: i ^ steps[-1]), kernel_own, kernel_next
        )
        sums = (total, swap(total, "px", lambda i: i ^ last))
    kernel_far = swap(kernel_pair, "freq", lambda i: i ^ 2)
    assert freqs == 4
    weighted_low, weighted = call(
        weigh,
        ((points, real), jnp.bfloat16),
        ((comps, sensors, real), jnp.float32),
        flops=ORDER_FLOPS,
    )(*sums)
    other_rows = swap(sent_rows, "freq", near)
    low_one = swap(weighted_low, "freq", near)
    low_three = swap(weighted_low, "freq", lambda i: i ^ 3)
    low_two = swap(weighted_low, "freq", lambda i: i ^ 2)
    wide = cols + 2 * SWEEPS
    count, levels = table.shape
    own_coef, table_parts, weighted_own = call(
        ready,
        ((rows, count, wide, real), jnp.float32),
        ((3 * levels, count * real), jnp.bfloat16),
        ((own, comps, real), jnp.float32),
        stored=(2,),
        scratch=(pltpu.VMEM((own, comps, real), jnp.float32), pltpu.SemaphoreType.DMA(())),
    )(wide_marks, table, weighted)
    (prior_term,) = call(
        prior,
        (model_field.shape, jnp.float32),
        scratch=(
            pltpu.VMEM((2, rows + 2 * SWEEPS, wide, real), jnp.float32),
            pltpu.VMEM((rows + 2 * SWEEPS, count, wide, real), jnp.float32),
        ),
        flops=PRIOR_FLOPS,
    )(model_field, side_rim, rim_rows, other_rows, own_coef, table_parts)
    (base,) = call(begin, (model_field.shape, jnp.float32), flops=EDGE_FLOPS)(
        kernel_pair, kernel_far, prior_term, weighted_low, low_three
    )
    (gradient,) = call(
        finish,
        (model_field.shape, jnp.float32),
        stored=(0,),
        scratch=(
            pltpu.VMEM(model_field.shape, jnp.float32),
            pltpu.SemaphoreType.DMA((rows,)),
        ),
    )(kernel_pair, kernel_far, base, low_two, low_one)
    return weighted_own[None], gradient


def solution(mesh):
    in_specs = (
        P("freq", ("px", "py"), None, None),
        P("freq", ("px", "py")),
        P("freq", "px", "py", None, None),
        P("px", "py", None),
        P("px", "py"),
        P(),
        P(),
    )
    out_specs = (P("freq", ("px", "py"), None, None), P("px", "py", None))
    return jax.shard_map(local, mesh=mesh, in_specs=in_specs, out_specs=out_specs, check_vma=False)
```

```python
import jax
import jax.numpy as jnp
from jax import lax
from jax.experimental import pallas as pl
from jax.experimental.pallas import tpu as pltpu
from jax.sharding import PartitionSpec as P

SWEEPS = 4
FREEDOM = 4.0
PRIOR_WEIGHT = 0.04
LANES = 128
TILE = 8
VMEM_BYTES = 40 << 20
PRIOR_FLOPS = 1 << 30
EDGE_FLOPS = 1 << 30
JOIN_FLOPS = 1 << 30
ORDER_FLOPS = 1 << 32


def swap(own, axis, partner):
    return lax.ppermute(own, axis, [(i, partner(i)) for i in range(lax.axis_size(axis))])


def bits(axis):
    size = lax.axis_size(axis)
    assert size & (size - 1) == 0
    return [1 << k for k in range(size.bit_length() - 1)]


def near(i):
    return i ^ 1


def far(axis):
    return lambda i: (((i + 1) ^ 1) - 1) % lax.axis_size(axis)


def call(body, *out_shapes, fetch=False, keep=(), scratch=(), stored=(), flops=0):
    def run(*operands):
        count, kept = len(operands), dict(keep)
        if fetch:
            operands = [pltpu.with_memory_space_constraint(x, pltpu.HBM) for x in operands]

        def fetched(*refs):
            outs = refs[count : count + len(out_shapes)]
            room, sems = iter(refs[count + len(out_shapes) : -1]), refs[-1]
            held = [outs[kept[k]] if k in kept else next(room) for k in range(count)]
            copies = [
                pltpu.make_async_copy(src, dst, sems.at[k])
                for k, (src, dst) in enumerate(zip(refs[:count], held))
            ]
            for k in sorted(range(count), key=lambda k: -operands[k].size):
                copies[k].start()
            for copy in copies:
                copy.wait()
            body(*held, *outs)

        return pl.pallas_call(
            fetched if fetch else body,
            out_shape=[jax.ShapeDtypeStruct(shape, dtype) for shape, dtype in out_shapes],
            in_specs=[pl.BlockSpec(memory_space=pltpu.HBM if fetch else pltpu.VMEM)] * count,
            out_specs=[
                pl.BlockSpec(memory_space=pltpu.HBM if k in stored else pltpu.VMEM)
                for k in range(len(out_shapes))
            ],
            scratch_shapes=list(scratch)
            + [pltpu.VMEM(x.shape, x.dtype) for k, x in enumerate(operands) if k not in kept] * fetch
            + [pltpu.SemaphoreType.DMA((count,))] * fetch,
            compiler_params=pltpu.CompilerParams(vmem_limit_bytes=VMEM_BYTES),
            cost_estimate=pl.CostEstimate(flops=flops, bytes_accessed=0, transcendentals=0),
        )(*operands)

    return run


def prepare(
    noise_ref,
    observed_ref,
    kernel_ref,
    field_ref,
    classes_ref,
    kappa_ref,
    coupling_ref,
    pay_ref,
    packed_ref,
    _,
    marks_ref,
    table_ref,
    *far_ref,
):
    beside, points, width = packed_ref.shape
    rows, cols, real = field_ref.shape
    own, comps = observed_ref.shape[:2]
    sensors = points // comps
    place = lax.axis_index("px") * lax.axis_size("py") + lax.axis_index("py")
    even = lax.axis_index("py") % 2 == 0
    packed, field = [], []
    for x in range(beside):
        picks = range(x, rows, beside)
        packed.append(jnp.concatenate([kernel_ref[k] for k in picks], axis=1))
        packed_ref[x] = packed[-1]
        field += [field_ref[k].astype(jnp.bfloat16) for k in picks]
    total = jnp.dot(
        jnp.concatenate(packed, axis=1),
        jnp.concatenate(field, axis=0),
        preferred_element_type=jnp.float32,
    )
    spot = lax.broadcasted_iota(jnp.int32, (points, real), 0)
    for c in range(comps):
        for k in range(own):
            row = c * sensors + place * own + k
            total = total - jnp.where(spot == row, observed_ref[k, c : c + 1, :], 0.0)
    pay_ref[:points] = total
    spot = lax.broadcasted_iota(jnp.int32, (TILE, real), 0) * real + lax.broadcasted_iota(
        jnp.int32, (TILE, real), 1
    )
    noise = jnp.zeros((TILE, real), jnp.float32)
    for k in range(own):
        noise = noise + jnp.where(spot == place * own + k, noise_ref[0:1, k : k + 1], 0.0)
    pay_ref[points : points + TILE] = noise
    coupling = coupling_ref[...]
    table_ref[0:1] = kappa_ref[...] + jnp.sum(coupling, axis=0, keepdims=True)
    table_ref[1:] = coupling
    marks = (classes_ref[...] + 1).astype(jnp.float32)
    marks_ref[...] = jnp.zeros_like(marks_ref)
    marks_ref[:, :cols] = marks
    edges = [
        (field_ref[:, cols - SWEEPS :, :], marks[:, cols - SWEEPS :]),
        (field_ref[:, :SWEEPS, :], marks[:, :SWEEPS]),
    ]

    def put(ref, start, chosen):
        for x in range(rows):
            ref[start + x * SWEEPS : start + (x + 1) * SWEEPS] = jnp.where(
                chosen, edges[0][0][x], edges[1][0][x]
            )
        start = start + rows * SWEEPS
        ref[start : start + rows] = jnp.zeros((rows, real), jnp.float32)
        ref[start : start + rows, :SWEEPS] = jnp.where(chosen, edges[0][1], edges[1][1])

    put(pay_ref, points + TILE, even)
    for ref in far_ref:
        put(ref, 0, jnp.logical_not(even))


def sides_of(one, two, axis):
    me = lax.axis_index(axis)
    even = me % 2 == 0
    before = jnp.where(me == 0, 0.0, jnp.where(even, two, one))
    after = jnp.where(me == lax.axis_size(axis) - 1, 0.0, jnp.where(even, one, two))
    return before, after


def add(mine_ref, got_ref, out_ref):
    size = out_ref.shape[0]
    out_ref[...] = mine_ref[:size] + got_ref[:size]


def add_and_join(mine_ref, got_ref, one_ref, two_ref, out_ref, joined_ref):
    out_ref[...] = mine_ref[...] + got_ref[...]
    half = one_ref.shape[0]
    joined_ref[:half] = one_ref[...]
    joined_ref[half:] = two_ref[...]


def lay(got_ref, field_ref, marks_ref, far_ref, side_ref, wide_ref, rows_ref, base):
    rows, cols, real = field_ref.shape
    one = got_ref[got_ref.shape[0] - rows * (SWEEPS + 1) :]
    before, after = sides_of(one, far_ref[0][...] if far_ref else one, "py")
    fields = rows * SWEEPS
    wide_ref[...] = (
        marks_ref[...]
        + pltpu.roll(after[fields:], cols, 1)
        + pltpu.roll(before[fields:], cols + SWEEPS, 1)
    )
    for x in range(rows):
        pick = slice(x * SWEEPS, (x + 1) * SWEEPS)
        side_ref[x] = jnp.concatenate([after[pick], before[pick]], axis=0)
    chosen = lax.axis_index("px") % 2 == 0
    if lax.axis_size("px") > 2:
        chosen = chosen == (lax.axis_index("freq") % 2 == 0)
    spot = lax.broadcasted_iota(jnp.int32, (2 * TILE, real), 0)
    blocks, tile = [], jnp.zeros((2 * TILE, real), jnp.float32)
    for k in range(SWEEPS):
        last = rows - SWEEPS + k
        blocks.append(jnp.where(chosen, field_ref[last], field_ref[k]))
        blocks.append(jnp.where(chosen, side_ref[last], side_ref[k]))
        marks = jnp.where(chosen, wide_ref[last : last + 1], wide_ref[k : k + 1])
        tile = jnp.where(spot == k, marks, tile)
    rows_ref[base:] = jnp.concatenate(blocks + [tile], axis=0).astype(jnp.bfloat16)


def edge(after_ref, got_ref, field_ref, marks_ref, *refs):
    *far_ref, side_ref, wide_ref, rows_ref = refs
    lay(got_ref, field_ref, marks_ref, far_ref, side_ref, wide_ref, rows_ref, 0)


def spread(mine_ref, got_ref, field_ref, marks_ref, *refs):
    *far_ref, out_ref, side_ref, wide_ref, mixed_ref = refs
    size, real = out_ref.shape
    total = mine_ref[:size] + got_ref[:size]
    out_ref[...] = total
    points = size - TILE
    high = total.astype(jnp.bfloat16).astype(jnp.float32)
    low = total - high
    mixed_ref[: 2 * size] = jnp.concatenate(
        [high[:points], low[:points], high[points:], low[points:]], axis=0
    ).astype(jnp.bfloat16)
    lay(got_ref, field_ref, marks_ref, far_ref, side_ref, wide_ref, mixed_ref, 2 * size)


def join(one_ref, two_ref, after_ref, out_ref):
    half = one_ref.shape[0]
    out_ref[:half] = one_ref[...]
    out_ref[half:] = two_ref[...]


def weigh(*refs):
    mine_ref, *got_refs, low_ref, weighted_ref = refs
    comps, sensors, real = weighted_ref.shape
    points = comps * sensors
    total = mine_ref[...]
    size = total.shape[0]
    for got_ref in got_refs:
        if got_ref.dtype == jnp.bfloat16:
            parts = got_ref[: 2 * size].astype(jnp.float32)
            sums = parts[:points] + parts[points : 2 * points]
            noises = parts[2 * points : 2 * points + TILE] + parts[2 * points + TILE :]
            total = total + jnp.concatenate([sums, noises], axis=0)
        else:
            total = total + got_ref[...]
    chunk = min(sensors, real)
    eye = lax.broadcasted_iota(jnp.int32, (chunk, real), 0) == lax.broadcasted_iota(
        jnp.int32, (chunk, real), 1
    )
    for k in range(sensors // chunk):
        row = total[points + k : points + k + 1]
        noise = jnp.sum(jnp.where(eye, row, 0.0), axis=1, keepdims=True)
        inverse = 1.0 / (noise * noise)
        misfit = [total[c * sensors + k * chunk : c * sensors + (k + 1) * chunk] for c in range(comps)]
        spread = sum(part * part for part in misfit) * inverse
        factor = (FREEDOM + 2.0) / (FREEDOM + spread) * inverse
        for c in range(comps):
            weighted = misfit[c] * factor
            weighted_ref[c, k * chunk : (k + 1) * chunk] = weighted
            low_ref[c * sensors + k * chunk : c * sensors + (k + 1) * chunk] = weighted.astype(
                jnp.bfloat16
            )


def coefficients(marks, table_ref, count, wide):
    levels, real = table_ref.shape[0] // 3, marks.shape[1]
    level = lax.broadcasted_iota(jnp.int32, (levels, real), 0).astype(jnp.float32) + 1.0
    onehot = (level == marks).astype(jnp.float32).astype(jnp.bfloat16)
    coef = lax.dot_general(
        jnp.concatenate([onehot] * 3, axis=0)[:, :wide],
        table_ref[...],
        (((0,), (0,)), ((), ())),
        preferred_element_type=jnp.float32,
    )
    return [coef[:, c * real : (c + 1) * real] for c in range(count)]


def ready(wide_ref, table_ref, weighted_ref, coef_ref, parts_ref, own_out, own_ref, sem):
    own, comps, real = own_ref.shape
    sensors = weighted_ref.shape[1]
    place = lax.axis_index("px") * lax.axis_size("py") + lax.axis_index("py")
    spot = lax.broadcasted_iota(jnp.int32, (sensors, real), 0)
    for c in range(comps):
        for k in range(own):
            own_ref[k, c : c + 1] = jnp.sum(
                jnp.where(spot == place * own + k, weighted_ref[c], 0.0), axis=0, keepdims=True
            )
    out = pltpu.make_async_copy(own_ref, own_out, sem)
    out.start()
    count, levels = table_ref.shape
    spread = (
        lax.broadcasted_iota(jnp.int32, (count, count * real), 1) // real
        == lax.broadcasted_iota(jnp.int32, (count, count * real), 0)
    ).astype(jnp.float32)
    turn = (((0,), (0,)), ((), ()))
    table = lax.dot_general(
        table_ref[...],
        spread,
        turn,
        precision=lax.Precision.HIGHEST,
        preferred_element_type=jnp.float32,
    )
    high = table.astype(jnp.bfloat16)
    rest = table - high.astype(jnp.float32)
    middle = rest.astype(jnp.bfloat16)
    low = (rest - middle.astype(jnp.float32)).astype(jnp.bfloat16)
    table = jnp.concatenate([high, middle, low], axis=0)
    parts_ref[...] = table
    for x in range(coef_ref.shape[0]):
        for c, coef in enumerate(
            coefficients(wide_ref[x : x + 1], parts_ref, count, coef_ref.shape[2])
        ):
            coef_ref[x, c] = coef
    out.wait()


def prior(
    field_ref,
    side_ref,
    rows_ref,
    other_ref,
    own_coef_ref,
    parts_ref,
    prior_ref,
    state_ref,
    coef_ref,
):
    rows, cols, _ = field_ref.shape
    wide = cols + 2 * SWEEPS
    tile = SWEEPS * wide
    mine = rows_ref[rows_ref.shape[0] - other_ref.shape[0] :].astype(jnp.float32)
    other = other_ref[...].astype(jnp.float32)
    even = lax.axis_index("freq") % 2 == 0
    before, after = sides_of(
        jnp.where(even, mine, other), jnp.where(even, other, mine), "px"
    )
    for k in range(SWEEPS):
        state_ref[0, k] = before[k * wide : (k + 1) * wide]
        state_ref[0, SWEEPS + rows + k] = after[k * wide : (k + 1) * wide]
    for x in range(rows):
        state_ref[0, SWEEPS + x] = jnp.concatenate([field_ref[x], side_ref[x]], axis=0)
    marks = {k: before[tile + k : tile + k + 1] for k in range(1, SWEEPS)}
    marks |= {SWEEPS + rows + k: after[tile + k : tile + k + 1] for k in range(SWEEPS - 1)}
    count = own_coef_ref.shape[1]
    for x in marks:
        for c, coef in enumerate(coefficients(marks[x], parts_ref, count, wide)):
            coef_ref[x, c] = coef

    def coef_of(x, c):
        own = SWEEPS <= x < SWEEPS + rows
        return own_coef_ref[x - SWEEPS, c] if own else coef_ref[x, c]

    for sweep in range(SWEEPS):
        now, later = sweep % 2, (sweep + 1) % 2
        for x in range(sweep + 1, 2 * SWEEPS + rows - sweep - 1):
            center = state_ref[now, x]
            beside = (
                coef_of(x, 1) * state_ref[now, x - 1]
                + coef_of(x, 2) * state_ref[now, x + 1]
                + coef_of(x, 3) * pltpu.roll(center, 1, 0)
                + coef_of(x, 4) * pltpu.roll(center, wide - 1, 0)
            )
            new = coef_of(x, 0) * center - beside
            if sweep < SWEEPS - 1:
                state_ref[later, x] = new
            else:
                prior_ref[x - SWEEPS] = PRIOR_WEIGHT * new[:cols]


def share(one, two, low):
    return lax.dot_general(
        jnp.concatenate([one, two], axis=0),
        low,
        (((0,), (0,)), ((), ())),
        preferred_element_type=jnp.float32,
    )


def begin(pair_ref, far_ref, prior_ref, low0_ref, low3_ref, base_ref):
    rows, cols, real = prior_ref.shape
    beside = pair_ref.shape[0] // 2
    low = jnp.concatenate([low0_ref[...], low3_ref[...]], axis=0)
    for x in range(beside):
        grad = share(pair_ref[x], far_ref[beside + x], low)
        for k in range(rows // beside):
            row = k * beside + x
            base_ref[row] = grad[k * cols : (k + 1) * cols] + prior_ref[row]


def finish(pair_ref, far_ref, low2_ref, low1_ref, rest_ref):
    rows, cols, real = rest_ref.shape
    beside = pair_ref.shape[0] // 2
    low = jnp.concatenate([low1_ref[...], low2_ref[...]], axis=0)
    for x in range(beside):
        grad = share(pair_ref[beside + x], far_ref[x], low)
        for k in range(rows // beside):
            rest_ref[k * beside + x] = grad[k * cols : (k + 1) * cols]


def local(observed, noise_scale, forward_kernel, model_field, classes, kappa_table, coupling_table):
    rows, cols, real = model_field.shape
    comps, sensors = forward_kernel.shape[3:]
    own = observed.shape[1]
    points = comps * sensors
    kernel_own = forward_kernel[0].transpose(0, 2, 3, 1).reshape(rows, points, cols)
    beside = rows // max(1, min(rows, LANES // cols))
    side = rows // beside
    assert sensors <= TILE * real and cols + 2 * SWEEPS <= LANES
    assert rows >= SWEEPS and cols % TILE == 0 and points % 16 == 0
    rim_rows = rows * (SWEEPS + 1)
    wide_py, wide_px = lax.axis_size("py") > 2, lax.axis_size("px") > 2
    payload, kernel_own, model_field, marks, table, *far_rim = call(
        prepare,
        ((points + TILE + rim_rows, real), jnp.float32),
        ((beside, points, side * cols), jnp.bfloat16),
        (model_field.shape, jnp.float32),
        ((rows, LANES), jnp.float32),
        ((1 + coupling_table.shape[0], coupling_table.shape[1]), jnp.float32),
        *[((rim_rows, real), jnp.float32)] * wide_py,
        fetch=True,
        keep=((3, 2),),
    )(
        noise_scale,
        observed[0],
        kernel_own,
        model_field,
        classes,
        kappa_table[None],
        coupling_table,
    )
    got = swap(payload, "py", near)
    kernel_next = swap(kernel_own, "freq", near)
    two = [swap(rim, "py", far("py")) for rim in far_rim]
    summed = ((points + TILE, real), jnp.float32)
    rim_size = SWEEPS * (cols + 2 * SWEEPS) + 2 * TILE
    peers, freqs = lax.axis_size("px"), lax.axis_size("freq")
    side_shapes = (
        ((rows, 2 * SWEEPS, real), jnp.float32),
        ((rows, LANES), jnp.float32),
    )
    pair_shape = ((2 * beside, points, side * cols), jnp.bfloat16)

    def by_parity(own, even_partner, odd_partner):
        return lax.ppermute(
            own,
            ("freq", "px"),
            [
                (f * peers + i, f * peers + (odd_partner if f % 2 else even_partner)(i))
                for f in range(freqs)
                for i in range(peers)
            ],
        )

    if peers == 4 and lax.axis_size("py") == 2:
        part = 2 * (points + TILE)
        total, side_rim, wide_marks, mixed = call(
            spread,
            summed,
            *side_shapes,
            ((part + rim_size, real), jnp.bfloat16),
        )(payload, got, model_field, marks)
        mixed = by_parity(mixed, near, far("px"))
        cross = by_parity(total, far("px"), near)
        skip = swap(total, "px", lambda i: i ^ 2)
        (kernel_pair,) = call(join, pair_shape, flops=JOIN_FLOPS)(kernel_own, kernel_next, total)
        sums = (total, cross, skip, mixed)
        rim_rows, sent_rows = mixed, mixed[part:]
    else:
        (total,) = call(add, summed)(payload, got)
        for bit in bits("py")[1:]:
            (total,) = call(add, summed)(total, swap(total, "py", lambda i: i ^ bit))
        side_rim, wide_marks, rim_rows = call(
            edge, *side_shapes, ((rim_size, real), jnp.bfloat16), flops=EDGE_FLOPS
        )(total, got, model_field, marks, *two)
        rim_rows = sent_rows = by_parity(rim_rows, near, far("px") if wide_px else near)
        *steps, last = bits("px")
        for bit in steps[:-1]:
            (total,) = call(add, summed)(total, swap(total, "px", lambda i: i ^ bit))
        total, kernel_pair = call(add_and_join, summed, pair_shape, flops=ORDER_FLOPS)(
            total, swap(total, "px", lambda i: i ^ steps[-1]), kernel_own, kernel_next
        )
        sums = (total, swap(total, "px", lambda i: i ^ last))
    kernel_far = swap(kernel_pair, "freq", lambda i: i ^ 2)
    assert freqs == 4
    weighted_low, weighted = call(
        weigh,
        ((points, real), jnp.bfloat16),
        ((comps, sensors, real), jnp.float32),
        flops=ORDER_FLOPS,
    )(*sums)
    other_rows = swap(sent_rows, "freq", near)
    low_one = swap(weighted_low, "freq", near)
    low_three = swap(weighted_low, "freq", lambda i: i ^ 3)
    low_two = swap(weighted_low, "freq", lambda i: i ^ 2)
    wide = cols + 2 * SWEEPS
    count, levels = table.shape
    own_coef, table_parts, weighted_own = call(
        ready,
        ((rows, count, wide, real), jnp.float32),
        ((3 * levels, count * real), jnp.bfloat16),
        ((own, comps, real), jnp.float32),
        stored=(2,),
        scratch=(pltpu.VMEM((own, comps, real), jnp.float32), pltpu.SemaphoreType.DMA(())),
    )(wide_marks, table, weighted)
    (prior_term,) = call(
        prior,
        (model_field.shape, jnp.float32),
        scratch=(
            pltpu.VMEM((2, rows + 2 * SWEEPS, wide, real), jnp.float32),
            pltpu.VMEM((rows + 2 * SWEEPS, count, wide, real), jnp.float32),
        ),
        flops=PRIOR_FLOPS,
    )(model_field, side_rim, rim_rows, other_rows, own_coef, table_parts)
    (base,) = call(begin, (model_field.shape, jnp.float32), flops=EDGE_FLOPS)(
        kernel_pair, kernel_far, prior_term, weighted_low, low_three
    )
    (rest,) = call(finish, (model_field.shape, jnp.float32))(
        kernel_pair, kernel_far, low_two, low_one
    )
    return weighted_own[None], base + rest


def solution(mesh):
    in_specs = (
        P("freq", ("px", "py"), None, None),
        P("freq", ("px", "py")),
        P("freq", "px", "py", None, None),
        P("px", "py", None),
        P("px", "py"),
        P(),
        P(),
    )
    out_specs = (P("freq", ("px", "py"), None, None), P("px", "py", None))
    return jax.shard_map(local, mesh=mesh, in_specs=in_specs, out_specs=out_specs, check_vma=False)
```
